32 devices in a mesh: shot: 2 (over core), gx: 8 (over z, y), gy: 2 (over x).
Axes of the slice: x: 2, y: 2, z: 4, core: 2. Of those that a mesh axis runs over, the one named last changes fastest.
Arguments:
- source_now: float32 [2, 256, 256, 128], P('shot', 'gx', 'gy'), may hold values from -6 to 6
- source_before: float32 [2, 256, 256, 128], P('shot', 'gx', 'gy'), may hold values from -6 to 6
- receiver_now: float32 [2, 256, 256, 128], P('shot', 'gx', 'gy'), may hold values from -6 to 6
- receiver_before: float32 [2, 256, 256, 128], P('shot', 'gx', 'gy'), may hold values from -6 to 6
- courant: float32 [256, 256, 128], P('gx', 'gy'), may hold values from 0.02 to 0.18
Outputs:
- offset_gathers: float32 [65, 64, 64, 128], P(None, 'gx', 'gy', 'shot')
The draws below stay inside these ranges and needn't reach their ends.
All inputs are finite; a program needn't handle non-finite values.
Results may differ from the reference program's by a relative error of at most 0.000096.
Values sent between devices are 32-bit elements; how exact they have to be, the bound alone decides.
No kernel may reach another device: no remote copies, remote signals or barrier semaphores. Data moves between devices by JAX's collectives and lax.ppermute only.
A program may use at most 192 MiB of HBM per device.

```python
import math
import jax
import jax.numpy as jnp
from jax import lax

HALF = 32
SUB = 2
SHOTS = 2
NX = 256
NY = 256
NZ = 128


def block_scale(own_key, dims, cuts, low, largest):
    def one(axis_at, parts):
        draws = jax.random.uniform(jax.random.fold_in(jax.random.fold_in(own_key, 6), axis_at), (parts,), jnp.float32, low / len(cuts), largest / len(cuts))
        return jnp.repeat(jnp.exp(draws), dims[axis_at] // parts).reshape((-1,) + (1,) * (len(dims) - axis_at - 1))

    factor_of = one(*cuts[0])
    for cut in cuts[1:]:
        factor_of = factor_of * one(*cut)
    return factor_of


def gaussian(key, extent, width, limit, cuts=(), held_as=jnp.bfloat16):
    values = width * jax.random.normal(key, extent, jnp.float32)
    if cuts:
        values = values * block_scale(key, extent, cuts, -0.22, 0.18)
    return jnp.clip(values, -limit, limit).astype(held_as)


def setup_inputs(seed: int = 0) -> dict:
    arg_keys = jax.random.split(jax.random.key(seed), 6)
    return {
        "source_now": gaussian(arg_keys[0], (SHOTS, NX, NY, NZ), 1.0, 6.0, ((0, 2), (1, 8), (2, 2)), jnp.float32),
        "source_before": gaussian(arg_keys[1], (SHOTS, NX, NY, NZ), 1.0, 6.0, ((0, 2), (1, 8), (2, 2)), jnp.float32),
        "receiver_now": gaussian(arg_keys[2], (SHOTS, NX, NY, NZ), 1.0, 6.0, ((0, 2), (1, 8), (2, 2)), jnp.float32),
        "receiver_before": gaussian(arg_keys[3], (SHOTS, NX, NY, NZ), 1.0, 6.0, ((0, 2), (1, 8), (2, 2)), jnp.float32),
        "courant": jnp.clip(jnp.exp(math.log(0.18) - 2.1972246 * jax.random.uniform(arg_keys[4], (NX, NY, NZ), jnp.float32) ** block_scale(arg_keys[4], (NX, NY, NZ), ((0, 8), (1, 2)), -0.2, 0.2)), 0.02, 0.18),
    }


STENCIL_WEIGHTS = (-205.0 / 72.0, 8.0 / 5.0, -1.0 / 5.0, 8.0 / 315.0, -1.0 / 560.0)


def laplace(field):
    size_x, size_y, size_z = field.shape[1], field.shape[2], field.shape[3]
    padded = jnp.pad(field, ((0, 0), (4, 4), (4, 4), (4, 4)))
    result = 3.0 * STENCIL_WEIGHTS[0] * field
    for distance in range(1, 5):
        weight = STENCIL_WEIGHTS[distance]
        along_x = padded[:, 4 + distance:4 + distance + size_x, 4:4 + size_y, 4:4 + size_z] + padded[:, 4 - distance:4 - distance + size_x, 4:4 + size_y, 4:4 + size_z]
        along_y = padded[:, 4:4 + size_x, 4 + distance:4 + distance + size_y, 4:4 + size_z] + padded[:, 4:4 + size_x, 4 - distance:4 - distance + size_y, 4:4 + size_z]
        along_z = padded[:, 4:4 + size_x, 4:4 + size_y, 4 + distance:4 + distance + size_z] + padded[:, 4:4 + size_x, 4:4 + size_y, 4 - distance:4 - distance + size_z]
        result = result + weight * (along_x + along_y + along_z)
    return result


def image_once(fields, shot_count):
    decimated = fields[:, :, ::4, :]
    padded = jnp.pad(decimated, ((0, 0), (HALF, HALF), (0, 0), (0, 0)))
    row_count = decimated.shape[1]
    sample_rows = jnp.arange(row_count // 4, dtype=jnp.int32) * 4

    def per_offset(offset):
        source_rows = jnp.take(padded[:shot_count], sample_rows + 2 * HALF - offset, axis=1)
        receiver_rows = jnp.take(padded[shot_count:], sample_rows + offset, axis=1)
        return jnp.sum(source_rows * receiver_rows, axis=0)

    return lax.map(per_offset, jnp.arange(2 * HALF + 1, dtype=jnp.int32))


def reference(source_now, source_before, receiver_now, receiver_before, courant):
    shot_count = source_now.shape[0]
    fields = jnp.concatenate([source_now, receiver_now], axis=0)
    before = jnp.concatenate([source_before, receiver_before], axis=0)
    image_sum = image_once(fields, shot_count)
    for repeat in range(SUB):
        advanced = 2.0 * fields - before + courant[None] * laplace(fields)
        before = fields
        fields = advanced
    return image_sum + image_once(fields, shot_count)
```

```python
import functools

import jax
import jax.numpy as jnp
from jax import lax
from jax.experimental import pallas as pl
from jax.experimental.pallas import tpu as pltpu
from jax.sharding import PartitionSpec as P

HALF = 32
REACH = 4
KEEP_EVERY = 4
OFFSETS = 2 * HALF + 1
OFFSETS_PER_STEP = 5
WEIGHTS = (-205.0 / 72.0, 8.0 / 5.0, -1.0 / 5.0, 8.0 / 315.0, -1.0 / 560.0)
PAD = 8
F32 = jnp.float32
HBM = pl.BlockSpec(memory_space=pl.ANY)
VMEM = pl.BlockSpec(memory_space=pltpu.VMEM)
SMEM = pl.BlockSpec(memory_space=pltpu.SMEM)


def params(mib):
    return pltpu.CompilerParams(vmem_limit_bytes=mib * 2**20)


def cost(flops, nbytes):
    return pl.CostEstimate(flops=flops, bytes_accessed=nbytes, transcendentals=0)


def run_copies(copies):
    for copy in copies:
        copy.start()
    for copy in copies:
        copy.wait()


def edge_kernel(source, receiver, up, down, sems):
    rows = source.shape[1]
    copies = []
    for field, ref in enumerate((source, receiver)):
        for out, start in ((up, rows - REACH), (down, 0)):
            copies.append(
                pltpu.make_async_copy(
                    ref.at[0, pl.ds(start, REACH)], out.at[field], sems.at[len(copies)]
                )
            )
    run_copies(copies)


def edges(source, receiver):
    _, _, size_y, size_z = source.shape
    shape = jax.ShapeDtypeStruct((2, REACH, size_y, size_z), F32)
    return pl.pallas_call(
        edge_kernel,
        out_shape=(shape, shape),
        in_specs=[HBM, HBM],
        out_specs=(HBM, HBM),
        scratch_shapes=[pltpu.SemaphoreType.DMA((4,))],
        cost_estimate=cost(0, 2 * 2**20),
        name="edges",
    )(source, receiver)


def z_halves(lines):
    count, size_z = lines.shape
    top, bottom = lines[: count // 2], lines[count // 2 :]
    low = lax.broadcasted_iota(jnp.int32, top.shape, 1) < size_z // 2
    first = jnp.where(low, top, pltpu.roll(bottom, size_z // 2, 1))
    second = jnp.where(low, pltpu.roll(top, size_z // 2, 1), bottom)
    return first, second


def pack_kernel(place, source, receiver, keep, give, side):
    shot, gy = place[0], place[1]
    rows, size_y, size_z = source.shape[1:]
    lines = size_y // KEEP_EVERY
    for row in range(rows):
        parts = []
        for field, ref in enumerate((source, receiver)):
            first, second = z_halves(ref[0, row, pl.ds(0, lines, stride=KEEP_EVERY), :])
            keep[field, row] = jnp.where(shot == 0, first, second)
            give[field, row] = jnp.where(shot == 0, second, first)
            low = ref[0, row, 0:REACH, :]
            high = ref[0, row, size_y - REACH : size_y, :]
            parts.append(jnp.where(gy == 0, high, low))
        side[row] = jnp.concatenate(parts, axis=0)


def pack(place, source, receiver):
    _, rows, size_y, size_z = source.shape
    lines = size_y // KEEP_EVERY // 2
    step = 4
    half = jax.ShapeDtypeStruct((2, rows, lines, size_z), F32)
    half_spec = pl.BlockSpec((2, step, lines, size_z), lambda i: (0, i, 0, 0))
    field_spec = pl.BlockSpec((1, step, size_y, size_z), lambda i: (0, i, 0, 0))
    return pl.pallas_call(
        pack_kernel,
        grid=(rows // step,),
        out_shape=(half, half, jax.ShapeDtypeStruct((rows, 2 * REACH, size_z), F32)),
        in_specs=[SMEM, field_spec, field_spec],
        out_specs=(
            half_spec,
            half_spec,
            pl.BlockSpec((step, 2 * REACH, size_z), lambda i: (i, 0, 0)),
        ),
        cost_estimate=cost(2**20, 7 * 2**20),
        name="pack",
    )(place, source, receiver)


def z_weights(size_z):
    z = lax.broadcasted_iota(jnp.int32, (8, size_z), 1)
    return [
        (jnp.where(z >= d, WEIGHTS[d], 0.0), jnp.where(z < size_z - d, WEIGHTS[d], 0.0))
        for d in range(1, REACH + 1)
    ]


def z_terms(center, masks):
    size_z = center.shape[1]
    total = None
    for d, (below, above) in enumerate(masks, start=1):
        term = below * pltpu.roll(center, d, 1) + above * pltpu.roll(center, size_z - d, 1)
        total = term if total is None else total + term
    return total


def step_kernel(
    place, source, receiver, source_before, receiver_before, courant, left, right, side,
    partial, kept_courant, up, down, side_out, now, before, scale, after, sems,
):
    gy = place[1]
    rows, size_y, size_z = courant.shape
    lines = size_y // KEEP_EVERY
    copies = []

    def copy(src, dst):
        copies.append(pltpu.make_async_copy(src, dst, sems.at[len(copies)]))

    middle = pl.ds(PAD, size_y)
    for field, ref in enumerate((source, receiver)):
        copy(ref.at[0], now.at[field, pl.ds(REACH, rows), middle])
    for field, ref in enumerate((source_before, receiver_before)):
        copy(ref.at[0], before.at[field])
    for field in range(2):
        copy(left.at[field], now.at[field, pl.ds(0, REACH), middle])
        copy(right.at[field], now.at[field, pl.ds(rows + REACH, REACH), middle])
    copy(courant, scale)
    for one in copies:
        one.start()

    blank = jnp.zeros((REACH, size_z), F32)
    for field in range(2):
        for row in list(range(REACH)) + list(range(rows + REACH, rows + 2 * REACH)):
            after[field, row] = jnp.zeros((size_y + 2 * PAD, size_z), F32)

    def fill(row, carry):
        for field in range(2):
            got = side[row, field * REACH : (field + 1) * REACH, :]
            now[field, row + REACH, PAD - REACH : PAD, :] = jnp.where(gy == 0, blank, got)
            now[field, row + REACH, size_y + PAD : size_y + PAD + REACH, :] = jnp.where(gy == 0, got, blank)
            after[field, row + REACH, PAD - REACH : PAD, :] = blank
            after[field, row + REACH, size_y + PAD : size_y + PAD + REACH, :] = blank
        return carry

    lax.fori_loop(0, rows, fill, 0)
    for one in copies:
        one.wait()

    masks = z_weights(size_z)

    def first(row, carry):
        for field in range(2):
            for chunk in range(size_y // 8):
                at = PAD + 8 * chunk
                center = now[field, row + REACH, at : at + 8, :]
                total = (3.0 * WEIGHTS[0]) * center + z_terms(center, masks)
                for d in range(1, REACH + 1):
                    around = (
                        now[field, row + REACH + d, at : at + 8, :]
                        + now[field, row + REACH - d, at : at + 8, :]
                        + now[field, row + REACH, at + d : at + d + 8, :]
                        + now[field, row + REACH, at - d : at - d + 8, :]
                    )
                    total = total + WEIGHTS[d] * around
                here = pl.ds(8 * chunk, 8)
                after[field, row + REACH, at : at + 8, :] = (
                    2.0 * center - before[field, row, here, :] + scale[row, here, :] * total
                )
        return carry

    lax.fori_loop(0, rows, first, 0)

    def second(row, carry):
        for chunk in range(lines // 8):
            at = PAD + 8 * KEEP_EVERY * chunk
            kept = lambda start: pl.ds(start, 8, stride=KEEP_EVERY)
            line = pl.ds(8 * chunk, 8)
            scaled = scale[row, kept(at - PAD), :]
            kept_courant[row, line, :] = scaled
            for field in range(2):
                center = after[field, row + REACH, kept(at), :]
                total = (3.0 * WEIGHTS[0]) * center + z_terms(center, masks)
                for d in range(1, REACH + 1):
                    around = (
                        after[field, row + REACH + d, kept(at), :]
                        + after[field, row + REACH - d, kept(at), :]
                        + after[field, row + REACH, kept(at + d), :]
                        + after[field, row + REACH, kept(at - d), :]
                    )
                    total = total + WEIGHTS[d] * around
                partial[field, row, line, :] = (
                    2.0 * center - now[field, row + REACH, kept(at), :] + scaled * total
                )
        for field in range(2):
            lowest = WEIGHTS[REACH] * after[field, row + REACH, PAD : PAD + 1, :]
            highest = sum(
                WEIGHTS[d] * after[field, row + REACH, PAD + size_y - d : PAD + size_y - d + 1, :]
                for d in range(1, REACH + 1)
            )
            side_out[field, pl.ds(row, 1), :] = jnp.where(gy == 0, highest, lowest)
        return carry

    lax.fori_loop(0, rows, second, 0)
    kept_lines = pl.ds(PAD, lines, stride=KEEP_EVERY)
    for field in range(2):
        for row in range(REACH):
            down[field, row] = after[field, REACH + row, kept_lines, :]
            up[field, row] = after[field, rows + row, kept_lines, :]


def steps(place, source, receiver, source_before, receiver_before, courant, left, right, side):
    rows, size_y, size_z = courant.shape
    lines = size_y // KEEP_EVERY
    halo = jax.ShapeDtypeStruct((2, REACH, lines, size_z), F32)
    return pl.pallas_call(
        step_kernel,
        out_shape=(
            jax.ShapeDtypeStruct((2, rows, lines, size_z), F32),
            jax.ShapeDtypeStruct((rows, lines, size_z), F32),
            halo,
            halo,
            jax.ShapeDtypeStruct((2, rows, size_z), F32),
        ),
        in_specs=[SMEM] + [HBM] * 7 + [VMEM],
        out_specs=(VMEM,) * 5,
        scratch_shapes=[
            pltpu.VMEM((2, rows + 2 * REACH, size_y + 2 * PAD, size_z), F32),
            pltpu.VMEM((2, rows, size_y, size_z), F32),
            pltpu.VMEM((rows, size_y, size_z), F32),
            pltpu.VMEM((2, rows + 2 * REACH, size_y + 2 * PAD, size_z), F32),
            pltpu.SemaphoreType.DMA((9,)),
        ],
        compiler_params=params(40),
        cost_estimate=cost(60 * 2**20, 14 * 2**20),
        name="steps",
    )(place, source, receiver, source_before, receiver_before, courant, left, right, side)


def finish_kernel(place, partial, kept_courant, left, right, side, keep, give):
    shot, gy = place[0], place[1]
    _, rows, lines, size_z = partial.shape
    line = lax.broadcasted_iota(jnp.int32, (lines, size_z), 0)
    meets = line == jnp.where(gy == 0, lines - 1, 0)

    def one_row(row, extra):
        scaled = kept_courant[row]
        for field in range(2):
            total = jnp.where(meets, side[field, pl.ds(row, 1), :], 0.0)
            for weight, values in extra[field]:
                total = total + weight * values
            first, second = z_halves(partial[field, row] + scaled * total)
            keep[field, row] = jnp.where(shot == 0, first, second)
            give[field, row] = jnp.where(shot == 0, second, first)

    def middle(row, carry):
        one_row(row, ((), ()))
        return carry

    lax.fori_loop(REACH, rows - REACH, middle, 0)
    for row in range(REACH):
        one_row(
            row,
            [[(WEIGHTS[d], left[f, REACH + row - d]) for d in range(row + 1, REACH + 1)] for f in range(2)],
        )
        one_row(
            rows - 1 - row,
            [[(WEIGHTS[d], right[f, d - 1 - row]) for d in range(row + 1, REACH + 1)] for f in range(2)],
        )


def finish(place, partial, kept_courant, left, right, side):
    _, rows, lines, size_z = partial.shape
    half = jax.ShapeDtypeStruct((2, rows, lines // 2, size_z), F32)
    return pl.pallas_call(
        finish_kernel,
        out_shape=(half, half),
        in_specs=[SMEM] + [VMEM] * 5,
        out_specs=(VMEM,) * 2,
        compiler_params=params(24),
        cost_estimate=cost(2**20, 3 * 2**20),
        name="finish",
    )(place, partial, kept_courant, left, right, side)


def image_kernel(count, place, *refs):
    blocks, (out, rows_of, sems) = refs[:count], refs[count:]
    parity = place[2]
    rows = blocks[0].shape[1]
    step = pl.program_id(0)

    @pl.when(step == 0)
    def _():
        copies = []
        for index, ref in enumerate(blocks):
            group, kind = index // 3, index % 3
            if kind == 0:
                start = HALF
            elif kind == 1:
                start = jnp.where(parity == 0, HALF + rows, 0)
            else:
                start = jnp.where(parity == 0, 0, HALF + rows)
            copies.append(
                pltpu.make_async_copy(ref, rows_of.at[group, :, pl.ds(start, rows)], sems.at[index])
            )
        run_copies(copies)

    groups = count // 3
    lines, size_z = rows_of.shape[3], rows_of.shape[4]
    for offset in range(OFFSETS_PER_STEP):
        shift = step * OFFSETS_PER_STEP + offset
        for sample in range(rows // 4):
            for chunk in range(lines // 8):
                here = pl.ds(8 * chunk, 8)
                total = None
                for group in range(groups):
                    term = (
                        rows_of[group, 0, 2 * HALF + 4 * sample - shift, here, :]
                        * rows_of[group, 1, 4 * sample + shift, here, :]
                    )
                    total = term if total is None else total + term
                other = pltpu.roll(total, size_z // 2, 1)
                out[offset, sample, 8 * chunk : 8 * chunk + 8, :] = total[:, : size_z // 2]
                out[offset, sample, lines + 8 * chunk : lines + 8 * chunk + 8, :] = other[:, : size_z // 2]


def image(place, blocks):
    _, rows, lines, size_z = blocks[0].shape
    samples = rows // 4
    return pl.pallas_call(
        functools.partial(image_kernel, len(blocks)),
        grid=(OFFSETS // OFFSETS_PER_STEP,),
        out_shape=jax.ShapeDtypeStruct((OFFSETS, samples, 2 * lines, size_z // 2), F32),
        in_specs=[SMEM] + [HBM] * len(blocks),
        out_specs=pl.BlockSpec((OFFSETS_PER_STEP, samples, 2 * lines, size_z // 2), lambda i: (i, 0, 0, 0)),
        scratch_shapes=[
            pltpu.VMEM((len(blocks) // 3, 2, rows + 2 * HALF, lines, size_z), F32),
            pltpu.SemaphoreType.DMA((len(blocks),)),
        ],
        compiler_params=params(24),
        cost_estimate=cost(16 * 2**20, 16 * 2**20),
        name="image",
    )(place, *blocks)


def on_device(source_now, source_before, receiver_now, receiver_before, courant):
    size = lax.axis_size("gx")
    place = jnp.stack(
        [lax.axis_index("shot"), lax.axis_index("gy"), lax.axis_index("gx") % 2]
    ).astype(jnp.int32)
    up_pairs = [(i, i + 1) for i in range(size - 1)]
    down_pairs = [(j, i) for i, j in up_pairs]
    partner = [(i, i ^ 1) for i in range(size)]
    onward = [(i, i + 2) for i in range(0, size - 2, 2)] + [(i, i - 2) for i in range(3, size, 2)]
    both = [(0, 1), (1, 0)]

    def spread(keep, give):
        other = lax.ppermute(give, "shot", both)
        near = [lax.ppermute(part, "gx", partner) for part in (keep, other)]
        far = [lax.ppermute(part, "gx", onward) for part in near]
        return [keep, near[0], far[0], other, near[1], far[1]]

    up, down = edges(source_now, receiver_now)
    keep, give, side = pack(place, source_now, receiver_now)
    left = lax.ppermute(up, "gx", up_pairs)
    right = lax.ppermute(down, "gx", down_pairs)
    side = lax.ppermute(side, "gy", both)
    left, right, keep, give = lax.optimization_barrier((left, right, keep, give))
    blocks = spread(keep, give)
    partial, kept_courant, up, down, side = steps(
        place, source_now, receiver_now, source_before, receiver_before, courant, left, right, side
    )
    left = lax.ppermute(up, "gx", up_pairs)
    right = lax.ppermute(down, "gx", down_pairs)
    side = lax.ppermute(side, "gy", both)
    keep, give = finish(place, partial, kept_courant, left, right, side)
    blocks += spread(keep, give)
    return image(place, blocks)


def solution(mesh):
    in_specs = (
        P("shot", "gx", "gy", None),
        P("shot", "gx", "gy", None),
        P("shot", "gx", "gy", None),
        P("shot", "gx", "gy", None),
        P("gx", "gy", None),
    )
    out_specs = P(None, "gx", "gy", "shot")
    return jax.shard_map(
        on_device, mesh=mesh, in_specs=in_specs, out_specs=out_specs, check_vma=False
    )
```

```python
import functools

import jax
import jax.numpy as jnp
from jax import lax
from jax.experimental import pallas as pl
from jax.experimental.pallas import tpu as pltpu
from jax.sharding import PartitionSpec as P

HALF = 32
REACH = 4
KEEP_EVERY = 4
OFFSETS = 2 * HALF + 1
OFFSET_ROWS = 72
WEIGHTS = (-205.0 / 72.0, 8.0 / 5.0, -1.0 / 5.0, 8.0 / 315.0, -1.0 / 560.0)
PAD = 8
F32 = jnp.float32
HBM = pl.BlockSpec(memory_space=pltpu.HBM)
VMEM = pl.BlockSpec(memory_space=pltpu.VMEM)
SMEM = pl.BlockSpec(memory_space=pltpu.SMEM)


def params(mib):
    return pltpu.CompilerParams(vmem_limit_bytes=mib * 2**20)


def cost(flops, nbytes):
    return pl.CostEstimate(flops=flops, bytes_accessed=nbytes, transcendentals=0)


def run_copies(copies):
    for copy in copies:
        copy.start()
    for copy in copies:
        copy.wait()


def edge_kernel(source_low, receiver_low, source_high, receiver_high, up, down):
    down[0] = source_low[0]
    down[1] = receiver_low[0]
    up[0] = source_high[0]
    up[1] = receiver_high[0]


def edges(source, receiver):
    _, rows, size_y, size_z = source.shape
    shape = jax.ShapeDtypeStruct((2, REACH, size_y, size_z), F32)
    block = (1, REACH, size_y, size_z)
    low = pl.BlockSpec(block, lambda i: (0, 0, 0, 0))
    high = pl.BlockSpec(block, lambda i: (0, rows // REACH - 1, 0, 0))
    return pl.pallas_call(
        edge_kernel,
        grid=(1,),
        out_shape=(shape, shape),
        in_specs=[low, low, high, high],
        out_specs=(VMEM, VMEM),
        cost_estimate=cost(0, 2 * 2**20),
        name="edges",
    )(source, receiver, source, receiver)


def z_halves(lines):
    count, size_z = lines.shape
    top, bottom = lines[: count // 2], lines[count // 2 :]
    low = lax.broadcasted_iota(jnp.int32, top.shape, 1) < size_z // 2
    first = jnp.where(low, top, pltpu.roll(bottom, size_z // 2, 1))
    second = jnp.where(low, pltpu.roll(top, size_z // 2, 1), bottom)
    return first, second


def pack_kernel(place, source, receiver, keep, give, side):
    shot, gy = place[0], place[1]
    rows, size_y, size_z = source.shape[1:]
    lines = size_y // KEEP_EVERY
    for row in range(rows):
        parts = []
        for field, ref in enumerate((source, receiver)):
            first, second = z_halves(ref[0, row, pl.ds(0, lines, stride=KEEP_EVERY), :])
            keep[field, row] = jnp.where(shot == 0, first, second)
            give[field, row] = jnp.where(shot == 0, second, first)
            low = ref[0, row, 0:REACH, :]
            high = ref[0, row, size_y - REACH : size_y, :]
            parts.append(jnp.where(gy == 0, high, low))
        side[row] = jnp.concatenate(parts, axis=0)


def pack(place, source, receiver):
    _, rows, size_y, size_z = source.shape
    lines = size_y // KEEP_EVERY // 2
    step = 4
    half = jax.ShapeDtypeStruct((2, rows, lines, size_z), F32)
    half_spec = pl.BlockSpec((2, step, lines, size_z), lambda i: (0, i, 0, 0))
    field_spec = pl.BlockSpec((1, step, size_y, size_z), lambda i: (0, i, 0, 0))
    return pl.pallas_call(
        pack_kernel,
        grid=(rows // step,),
        out_shape=(half, half, jax.ShapeDtypeStruct((rows, 2 * REACH, size_z), F32)),
        in_specs=[SMEM, field_spec, field_spec],
        out_specs=(
            half_spec,
            half_spec,
            pl.BlockSpec((step, 2 * REACH, size_z), lambda i: (i, 0, 0)),
        ),
        cost_estimate=cost(2**20, 7 * 2**20),
        name="pack",
    )(place, source, receiver)


def z_weights(size_z):
    z = lax.broadcasted_iota(jnp.int32, (8, size_z), 1)
    return [
        (jnp.where(z >= d, WEIGHTS[d], 0.0), jnp.where(z < size_z - d, WEIGHTS[d], 0.0))
        for d in range(1, REACH + 1)
    ]


def z_terms(center, masks):
    size_z = center.shape[1]
    total = None
    for d, (below, above) in enumerate(masks, start=1):
        term = below * pltpu.roll(center, d, 1) + above * pltpu.roll(center, size_z - d, 1)
        total = term if total is None else total + term
    return total


def step_kernel(
    place, source, receiver, source_before, receiver_before, courant, left, right, side,
    partial, kept_courant, up, down, side_out, now, before, scale, after, sems,
):
    gy = place[1]
    rows, size_y, size_z = courant.shape
    lines = size_y // KEEP_EVERY
    copies = []

    def copy(src, dst):
        copies.append(pltpu.make_async_copy(src, dst, sems.at[len(copies)]))

    middle = pl.ds(PAD, size_y)
    for field, ref in enumerate((source, receiver)):
        copy(ref.at[0], now.at[field, pl.ds(REACH, rows), middle])
    for field, ref in enumerate((source_before, receiver_before)):
        copy(ref.at[0], before.at[field])
    for field in range(2):
        copy(left.at[field], now.at[field, pl.ds(0, REACH), middle])
        copy(right.at[field], now.at[field, pl.ds(rows + REACH, REACH), middle])
    copy(courant, scale)
    for one in copies:
        one.start()

    blank = jnp.zeros((REACH, size_z), F32)
    for field in range(2):
        for row in list(range(REACH)) + list(range(rows + REACH, rows + 2 * REACH)):
            after[field, row] = jnp.zeros((size_y + 2 * PAD, size_z), F32)

    def fill(row, carry):
        for field in range(2):
            got = side[row, field * REACH : (field + 1) * REACH, :]
            now[field, row + REACH, PAD - REACH : PAD, :] = jnp.where(gy == 0, blank, got)
            now[field, row + REACH, size_y + PAD : size_y + PAD + REACH, :] = jnp.where(gy == 0, got, blank)
            after[field, row + REACH, PAD - REACH : PAD, :] = blank
            after[field, row + REACH, size_y + PAD : size_y + PAD + REACH, :] = blank
        return carry

    lax.fori_loop(0, rows, fill, 0)
    for one in copies:
        one.wait()

    masks = z_weights(size_z)

    def first(row, carry):
        for field in range(2):
            for chunk in range(size_y // 8):
                at = PAD + 8 * chunk
                center = now[field, row + REACH, at : at + 8, :]
                total = (3.0 * WEIGHTS[0]) * center + z_terms(center, masks)
                for d in range(1, REACH + 1):
                    around = (
                        now[field, row + REACH + d, at : at + 8, :]
                        + now[field, row + REACH - d, at : at + 8, :]
                        + now[field, row + REACH, at + d : at + d + 8, :]
                        + now[field, row + REACH, at - d : at - d + 8, :]
                    )
                    total = total + WEIGHTS[d] * around
                here = pl.ds(8 * chunk, 8)
                after[field, row + REACH, at : at + 8, :] = (
                    2.0 * center - before[field, row, here, :] + scale[row, here, :] * total
                )
        return carry

    lax.fori_loop(0, rows, first, 0)

    def second(row, carry):
        for chunk in range(lines // 8):
            at = PAD + 8 * KEEP_EVERY * chunk
            kept = lambda start: pl.ds(start, 8, stride=KEEP_EVERY)
            line = pl.ds(8 * chunk, 8)
            scaled = scale[row, kept(at - PAD), :]
            kept_courant[row, line, :] = scaled
            for field in range(2):
                center = after[field, row + REACH, kept(at), :]
                total = (3.0 * WEIGHTS[0]) * center + z_terms(center, masks)
                for d in range(1, REACH + 1):
                    around = (
                        after[field, row + REACH + d, kept(at), :]
                        + after[field, row + REACH - d, kept(at), :]
                        + after[field, row + REACH, kept(at + d), :]
                        + after[field, row + REACH, kept(at - d), :]
                    )
                    total = total + WEIGHTS[d] * around
                partial[field, row, line, :] = (
                    2.0 * center - now[field, row + REACH, kept(at), :] + scaled * total
                )
        for field in range(2):
            lowest = WEIGHTS[REACH] * after[field, row + REACH, PAD : PAD + 1, :]
            highest = sum(
                WEIGHTS[d] * after[field, row + REACH, PAD + size_y - d : PAD + size_y - d + 1, :]
                for d in range(1, REACH + 1)
            )
            side_out[field, pl.ds(row, 1), :] = jnp.where(gy == 0, highest, lowest)
        return carry

    lax.fori_loop(0, rows, second, 0)
    kept_lines = pl.ds(PAD, lines, stride=KEEP_EVERY)
    for field in range(2):
        for row in range(REACH):
            down[field, row] = after[field, REACH + row, kept_lines, :]
            up[field, row] = after[field, rows + row, kept_lines, :]


def steps(place, source, receiver, source_before, receiver_before, courant, left, right, side):
    rows, size_y, size_z = courant.shape
    lines = size_y // KEEP_EVERY
    halo = jax.ShapeDtypeStruct((2, REACH, lines, size_z), F32)
    return pl.pallas_call(
        step_kernel,
        out_shape=(
            jax.ShapeDtypeStruct((2, rows, lines, size_z), F32),
            jax.ShapeDtypeStruct((rows, lines, size_z), F32),
            halo,
            halo,
            jax.ShapeDtypeStruct((2, rows, size_z), F32),
        ),
        in_specs=[SMEM] + [HBM] * 7 + [VMEM],
        out_specs=(VMEM,) * 5,
        scratch_shapes=[
            pltpu.VMEM((2, rows + 2 * REACH, size_y + 2 * PAD, size_z), F32),
            pltpu.VMEM((2, rows, size_y, size_z), F32),
            pltpu.VMEM((rows, size_y, size_z), F32),
            pltpu.VMEM((2, rows + 2 * REACH, size_y + 2 * PAD, size_z), F32),
            pltpu.SemaphoreType.DMA((9,)),
        ],
        compiler_params=params(60),
        cost_estimate=cost(2 * 10**10, 40 * 2**20),
        name="steps",
    )(place, source, receiver, source_before, receiver_before, courant, left, right, side)


def finish_kernel(place, partial, kept_courant, left, right, side, keep, give):
    shot, gy = place[0], place[1]
    _, rows, lines, size_z = partial.shape
    line = lax.broadcasted_iota(jnp.int32, (lines, size_z), 0)
    meets = line == jnp.where(gy == 0, lines - 1, 0)

    def one_row(row, extra):
        scaled = kept_courant[row]
        for field in range(2):
            total = jnp.where(meets, side[field, pl.ds(row, 1), :], 0.0)
            for weight, values in extra[field]:
                total = total + weight * values
            first, second = z_halves(partial[field, row] + scaled * total)
            keep[field, row] = jnp.where(shot == 0, first, second)
            give[field, row] = jnp.where(shot == 0, second, first)

    def middle(row, carry):
        one_row(row, ((), ()))
        return carry

    lax.fori_loop(REACH, rows - REACH, middle, 0)
    for row in range(REACH):
        one_row(
            row,
            [[(WEIGHTS[d], left[f, REACH + row - d]) for d in range(row + 1, REACH + 1)] for f in range(2)],
        )
        one_row(
            rows - 1 - row,
            [[(WEIGHTS[d], right[f, d - 1 - row]) for d in range(row + 1, REACH + 1)] for f in range(2)],
        )


def finish(place, partial, kept_courant, left, right, side):
    _, rows, lines, size_z = partial.shape
    half = jax.ShapeDtypeStruct((2, rows, lines // 2, size_z), F32)
    return pl.pallas_call(
        finish_kernel,
        out_shape=(half, half),
        in_specs=[SMEM] + [VMEM] * 5,
        out_specs=(VMEM,) * 2,
        compiler_params=params(24),
        cost_estimate=cost(2**20, 3 * 2**20),
        name="finish",
    )(place, partial, kept_courant, left, right, side)


def image_kernel(count, place, *refs):
    blocks, (out, rows_of, turned, sems) = refs[:count], refs[count:]
    parity = place[2]
    rows = blocks[0].shape[1]
    step = pl.program_id(0)

    @pl.when(step == 0)
    def _():
        copies = []
        for index, ref in enumerate(blocks):
            group, kind = index // 3, index % 3
            if kind == 0:
                start = HALF
            elif kind == 1:
                start = jnp.where(parity == 0, HALF + rows, 0)
            else:
                start = jnp.where(parity == 0, 0, HALF + rows)
            copies.append(
                pltpu.make_async_copy(ref, rows_of.at[group, :, pl.ds(start, rows)], sems.at[index])
            )
        run_copies(copies)

    groups = count // 3
    lines, size_z = rows_of.shape[3], rows_of.shape[4]
    sample = 4 * pl.program_id(0)
    for chunk in range(lines // 8):
        here = pl.ds(8 * chunk, 8)
        for shift in range(OFFSETS):
            total = None
            for group in range(groups):
                term = (
                    rows_of[group, 0, 2 * HALF + sample - shift, here, :]
                    * rows_of[group, 1, sample + shift, here, :]
                )
                total = term if total is None else total + term
            turned[pl.ds(shift, 8, stride=OFFSET_ROWS), :] = total
        for line in range(8):
            values = turned[line * OFFSET_ROWS : (line + 1) * OFFSET_ROWS, :].T
            at = 8 * chunk + line
            out[0, at] = values[: size_z // 2, :OFFSETS]
            out[0, lines + at] = values[size_z // 2 :, :OFFSETS]


def image(place, blocks):
    _, rows, lines, size_z = blocks[0].shape
    samples = rows // 4
    return pl.pallas_call(
        functools.partial(image_kernel, len(blocks)),
        grid=(samples,),
        out_shape=jax.ShapeDtypeStruct((samples, 2 * lines, size_z // 2, OFFSETS), F32),
        in_specs=[SMEM] + [HBM] * len(blocks),
        out_specs=pl.BlockSpec((1, 2 * lines, size_z // 2, OFFSETS), lambda i: (i, 0, 0, 0)),
        scratch_shapes=[
            pltpu.VMEM((len(blocks) // 3, 2, rows + 2 * HALF, lines, size_z), F32),
            pltpu.VMEM((8 * OFFSET_ROWS, size_z), F32),
            pltpu.SemaphoreType.DMA((len(blocks),)),
        ],
        compiler_params=params(24),
        cost_estimate=cost(16 * 2**20, 16 * 2**20),
        name="image",
    )(place, *blocks)


def on_device(source_now, source_before, receiver_now, receiver_before, courant):
    size = lax.axis_size("gx")
    place = jnp.stack(
        [lax.axis_index("shot"), lax.axis_index("gy"), lax.axis_index("gx") % 2]
    ).astype(jnp.int32)
    up_pairs = [(i, i + 1) for i in range(size - 1)]
    down_pairs = [(j, i) for i, j in up_pairs]
    partner = [(i, i ^ 1) for i in range(size)]
    onward = [(i, i + 2) for i in range(0, size - 2, 2)] + [(i, i - 2) for i in range(3, size, 2)]
    both = [(0, 1), (1, 0)]

    def exchange(array, axis, pairs):
        return lax.ppermute(array, axis, pairs)

    up, down = edges(source_now, receiver_now)
    keep, give, side = pack(place, source_now, receiver_now)
    left = exchange(up, "gx", up_pairs)
    right = exchange(down, "gx", down_pairs)
    side = exchange(side, "gy", both)
    other = exchange(give, "shot", both)
    left, right, side, other = lax.optimization_barrier((left, right, side, other))
    near_keep = exchange(keep, "gx", partner)
    near_other = exchange(other, "gx", partner)
    partial, kept_courant, up, down, side = steps(
        place, source_now, receiver_now, source_before, receiver_before, courant, left, right, side
    )
    up, down, side, near_keep = lax.optimization_barrier((up, down, side, near_keep))
    left = exchange(up, "gx", up_pairs)
    right = exchange(down, "gx", down_pairs)
    side = exchange(side, "gy", both)
    far_keep = exchange(near_keep, "gx", onward)
    left, right, side, near_other = lax.optimization_barrier((left, right, side, near_other))
    far_other = exchange(near_other, "gx", onward)
    blocks = [keep, near_keep, far_keep, other, near_other, far_other]
    keep, give = finish(place, partial, kept_courant, left, right, side)
    other = exchange(give, "shot", both)
    near_keep = exchange(keep, "gx", partner)
    near_other = exchange(other, "gx", partner)
    far_keep = exchange(near_keep, "gx", onward)
    far_other = exchange(near_other, "gx", onward)
    blocks += [keep, near_keep, far_keep, other, near_other, far_other]
    return jnp.transpose(image(place, blocks), (3, 0, 1, 2))


def solution(mesh):
    in_specs = (
        P("shot", "gx", "gy", None),
        P("shot", "gx", "gy", None),
        P("shot", "gx", "gy", None),
        P("shot", "gx", "gy", None),
        P("gx", "gy", None),
    )
    out_specs = P(None, "gx", "gy", "shot")
    return jax.shard_map(
        on_device, mesh=mesh, in_specs=in_specs, out_specs=out_specs, check_vma=False
    )
```

```python
import functools

import jax
import jax.numpy as jnp
from jax import lax
from jax.experimental import pallas as pl
from jax.experimental.pallas import tpu as pltpu
from jax.sharding import PartitionSpec as P

HALF = 32
REACH = 4
KEEP_EVERY = 4
OFFSETS = 2 * HALF + 1
OFFSET_ROWS = 72
WEIGHTS = (-205.0 / 72.0, 8.0 / 5.0, -1.0 / 5.0, 8.0 / 315.0, -1.0 / 560.0)
PAD = 8
F32 = jnp.float32
HBM = pl.BlockSpec(memory_space=pltpu.HBM)
VMEM = pl.BlockSpec(memory_space=pltpu.VMEM)
SMEM = pl.BlockSpec(memory_space=pltpu.SMEM)


def params(mib):
    return pltpu.CompilerParams(vmem_limit_bytes=mib * 2**20)


def cost(flops, nbytes):
    return pl.CostEstimate(flops=flops, bytes_accessed=nbytes, transcendentals=0)


def run_copies(copies):
    for copy in copies:
        copy.start()
    for copy in copies:
        copy.wait()


def z_halves(lines):
    count, size_z = lines.shape
    top, bottom = lines[: count // 2], lines[count // 2 :]
    low = lax.broadcasted_iota(jnp.int32, top.shape, 1) < size_z // 2
    first = jnp.where(low, top, pltpu.roll(bottom, size_z // 2, 1))
    second = jnp.where(low, pltpu.roll(top, size_z // 2, 1), bottom)
    return first, second


def pack_kernel(place, source, receiver, up, down, keep, give, side):
    shot, gy = place[0], place[1]
    rows, size_y, size_z = source.shape[1:]
    lines = size_y // KEEP_EVERY
    step, steps = pl.program_id(0), pl.num_programs(0)

    @pl.when(step == 0)
    def _():
        for field, ref in enumerate((source, receiver)):
            down[field] = ref[0, :REACH]

    @pl.when(step == steps - 1)
    def _():
        for field, ref in enumerate((source, receiver)):
            up[field] = ref[0, rows - REACH :]

    for row in range(rows):
        parts = []
        for field, ref in enumerate((source, receiver)):
            first, second = z_halves(ref[0, row, pl.ds(0, lines, stride=KEEP_EVERY), :])
            keep[field, row] = jnp.where(shot == 0, first, second)
            give[field, row] = jnp.where(shot == 0, second, first)
            low = ref[0, row, 0:REACH, :]
            high = ref[0, row, size_y - REACH : size_y, :]
            parts.append(jnp.where(gy == 0, high, low))
        side[row] = jnp.concatenate(parts, axis=0)


def pack(place, source, receiver):
    _, rows, size_y, size_z = source.shape
    lines = size_y // KEEP_EVERY // 2
    step = 8
    edge = jax.ShapeDtypeStruct((2, REACH, size_y, size_z), F32)
    half = jax.ShapeDtypeStruct((2, rows, lines, size_z), F32)
    edge_spec = pl.BlockSpec((2, REACH, size_y, size_z), lambda i: (0, 0, 0, 0))
    half_spec = pl.BlockSpec((2, step, lines, size_z), lambda i: (0, i, 0, 0))
    field_spec = pl.BlockSpec((1, step, size_y, size_z), lambda i: (0, i, 0, 0))
    return pl.pallas_call(
        pack_kernel,
        grid=(rows // step,),
        out_shape=(edge, edge, half, half, jax.ShapeDtypeStruct((rows, 2 * REACH, size_z), F32)),
        in_specs=[SMEM, field_spec, field_spec],
        out_specs=(
            edge_spec,
            edge_spec,
            half_spec,
            half_spec,
            pl.BlockSpec((step, 2 * REACH, size_z), lambda i: (i, 0, 0)),
        ),
        cost_estimate=cost(10**10, 7 * 2**20),
        name="pack",
    )(place, source, receiver)


def z_weights(size_z):
    z = lax.broadcasted_iota(jnp.int32, (8, size_z), 1)
    return [
        (jnp.where(z >= d, WEIGHTS[d], 0.0), jnp.where(z < size_z - d, WEIGHTS[d], 0.0))
        for d in range(1, REACH + 1)
    ]


def z_terms(center, masks):
    size_z = center.shape[1]
    total = None
    for d, (below, above) in enumerate(masks, start=1):
        term = below * pltpu.roll(center, d, 1) + above * pltpu.roll(center, size_z - d, 1)
        total = term if total is None else total + term
    return total


def first_step(now, row, before, before_row, scale, scale_row, after, after_row, field, masks):
    size_y = before.shape[2]
    for chunk in range(size_y // 8):
        at = PAD + 8 * chunk
        center = now[field, row, at : at + 8, :]
        total = (3.0 * WEIGHTS[0]) * center + z_terms(center, masks)
        for d in range(1, REACH + 1):
            around = (
                now[field, row + d, at : at + 8, :]
                + now[field, row - d, at : at + 8, :]
                + now[field, row, at + d : at + d + 8, :]
                + now[field, row, at - d : at - d + 8, :]
            )
            total = total + WEIGHTS[d] * around
        here = pl.ds(8 * chunk, 8)
        after[field, after_row, at : at + 8, :] = (
            2.0 * center - before[field, before_row, here, :] + scale[scale_row, here, :] * total
        )


def second_step(now, row, scale, scale_row, after, after_row, field, masks, store):
    size_y = scale.shape[1]
    for chunk in range(size_y // KEEP_EVERY // 8):
        at = PAD + 8 * KEEP_EVERY * chunk
        kept = lambda start: pl.ds(start, 8, stride=KEEP_EVERY)
        center = after[field, after_row, kept(at), :]
        total = (3.0 * WEIGHTS[0]) * center + z_terms(center, masks)
        for d in range(1, REACH + 1):
            around = (
                after[field, after_row + d, kept(at), :]
                + after[field, after_row - d, kept(at), :]
                + after[field, after_row, kept(at + d), :]
                + after[field, after_row, kept(at - d), :]
            )
            total = total + WEIGHTS[d] * around
        store(
            pl.ds(8 * chunk, 8),
            2.0 * center - now[field, row, kept(at), :] + scale[scale_row, kept(at - PAD), :] * total,
        )


def side_term(after, after_row, field, size_y, gy):
    lowest = WEIGHTS[REACH] * after[field, after_row, PAD : PAD + 1, :]
    highest = sum(
        WEIGHTS[d] * after[field, after_row, PAD + size_y - d : PAD + size_y - d + 1, :]
        for d in range(1, REACH + 1)
    )
    return jnp.where(gy == 0, highest, lowest)


def fill_sides(now, row, got, field, size_y, gy):
    blank = jnp.zeros_like(got)
    now[field, row, PAD - REACH : PAD, :] = jnp.where(gy == 0, blank, got)
    now[field, row, size_y + PAD : size_y + PAD + REACH, :] = jnp.where(gy == 0, got, blank)


def blank_sides(after, row, field, size_y):
    blank = jnp.zeros((REACH, after.shape[3]), F32)
    after[field, row, PAD - REACH : PAD, :] = blank
    after[field, row, size_y + PAD : size_y + PAD + REACH, :] = blank


def inner_kernel(
    place, source, receiver, source_before, receiver_before, courant, side,
    partial, kept_courant, side_out, border, now, before, scale, after, sems, out_sems,
):
    gy = place[1]
    rows, size_y, size_z = courant.shape
    lines = size_y // KEEP_EVERY
    copies = []

    def copy(src, dst):
        copies.append(pltpu.make_async_copy(src, dst, sems.at[len(copies)]))

    middle = pl.ds(PAD, size_y)
    for field, ref in enumerate((source, receiver)):
        copy(ref.at[0], now.at[field, :, middle])
    for field, ref in enumerate((source_before, receiver_before)):
        copy(ref.at[0], before.at[field])
    copy(courant, scale)
    for one in copies:
        one.start()

    def fill(row, carry):
        for field in range(2):
            got = side[row, field * REACH : (field + 1) * REACH, :]
            fill_sides(now, row, got, field, size_y, gy)
            blank_sides(after, row, field, size_y)
        return carry

    lax.fori_loop(0, rows, fill, 0)
    side_out[...] = jnp.zeros_like(side_out)
    for one in copies:
        one.wait()
    masks = z_weights(size_z)

    def first(row, carry):
        for field in range(2):
            first_step(now, row, before, row, scale, row, after, row, field, masks)
            side_out[field, pl.ds(row, 1), :] = side_term(after, row, field, size_y, gy)
        return carry

    lax.fori_loop(REACH, rows - REACH, first, 0)
    outs = []
    for field in range(2):
        for end, start in enumerate((REACH, rows - 3 * REACH)):
            outs.append(
                pltpu.make_async_copy(
                    after.at[field, pl.ds(start, 2 * REACH), middle],
                    border.at[field, end],
                    out_sems.at[len(outs)],
                )
            )
            outs[-1].start()

    def second(row, carry):
        for field in range(2):
            def store(here, value):
                partial[field, row - 2 * REACH, here, :] = value

            second_step(now, row, scale, row, after, row, field, masks, store)
        return carry

    lax.fori_loop(2 * REACH, rows - 2 * REACH, second, 0)

    def keep(row, carry):
        kept_courant[row] = scale[row, pl.ds(0, lines, stride=KEEP_EVERY), :]
        return carry

    lax.fori_loop(0, rows, keep, 0)
    for one in outs:
        one.wait()


def inner(place, source, receiver, source_before, receiver_before, courant, side):
    rows, size_y, size_z = courant.shape
    lines = size_y // KEEP_EVERY
    return pl.pallas_call(
        inner_kernel,
        out_shape=(
            jax.ShapeDtypeStruct((2, rows - 4 * REACH, lines, size_z), F32),
            jax.ShapeDtypeStruct((rows, lines, size_z), F32),
            jax.ShapeDtypeStruct((2, rows, size_z), F32),
            jax.ShapeDtypeStruct((2, 2, 2 * REACH, size_y, size_z), F32),
        ),
        in_specs=[SMEM] + [HBM] * 5 + [VMEM],
        out_specs=(VMEM,) * 3 + (HBM,),
        scratch_shapes=[
            pltpu.VMEM((2, rows, size_y + 2 * PAD, size_z), F32),
            pltpu.VMEM((2, rows, size_y, size_z), F32),
            pltpu.VMEM((rows, size_y, size_z), F32),
            pltpu.VMEM((2, rows, size_y + 2 * PAD, size_z), F32),
            pltpu.SemaphoreType.DMA((5,)),
            pltpu.SemaphoreType.DMA((4,)),
        ],
        compiler_params=params(60),
        cost_estimate=cost(10**6, 2**20),
        name="inner",
    )(place, source, receiver, source_before, receiver_before, courant, side)


def outer_kernel(
    place, source, receiver, source_before, receiver_before, courant, border, left, right, side, side_in,
    partial, up, down, side_out, now, before, scale, after, sems,
):
    gy = place[1]
    rows, size_y, size_z = courant.shape
    lines = size_y // KEEP_EVERY
    reach2 = 2 * REACH
    copies = []

    def copy(src, dst):
        copies.append(pltpu.make_async_copy(src, dst, sems.at[len(copies)]))

    middle = pl.ds(PAD, size_y)
    for field in range(2):
        ref = (source, receiver)[field]
        copy(ref.at[0, pl.ds(0, reach2)], now.at[field, pl.ds(REACH, reach2), middle])
        copy(left.at[field], now.at[field, pl.ds(0, REACH), middle])
        copy(ref.at[0, pl.ds(rows - reach2, reach2)], now.at[2 + field, pl.ds(0, reach2), middle])
        copy(right.at[field], now.at[2 + field, pl.ds(reach2, REACH), middle])
        ref = (source_before, receiver_before)[field]
        copy(ref.at[0, pl.ds(0, REACH)], before.at[field])
        copy(ref.at[0, pl.ds(rows - REACH, REACH)], before.at[2 + field])
        copy(border.at[field, 0], after.at[field, pl.ds(reach2, reach2), middle])
        copy(border.at[field, 1], after.at[2 + field, pl.ds(0, reach2), middle])
    copy(courant.at[pl.ds(0, reach2)], scale.at[pl.ds(0, reach2)])
    copy(courant.at[pl.ds(rows - reach2, reach2)], scale.at[pl.ds(reach2, reach2)])
    for one in copies:
        one.start()

    for field in range(2):
        for row in range(REACH):
            for end in range(2):
                after[2 * end + field, 3 * REACH * end + row] = jnp.zeros((size_y + 2 * PAD, size_z), F32)
        for row in range(reach2):
            low = side[row, field * REACH : (field + 1) * REACH, :]
            fill_sides(now, REACH + row, low, field, size_y, gy)
            high = side[rows - reach2 + row, field * REACH : (field + 1) * REACH, :]
            fill_sides(now, row, high, 2 + field, size_y, gy)
            for end in range(2):
                blank_sides(after, REACH + row, 2 * end + field, size_y)
    side_out[...] = side_in[...]
    for one in copies:
        one.wait()
    masks = z_weights(size_z)

    def first(row, carry):
        for field in range(2):
            for end in range(2):
                group = 2 * end + field
                to = REACH * (1 + end) + row
                first_step(
                    now, REACH + row, before, row, scale, (2 * end + end) * REACH + row,
                    after, to, group, masks,
                )
                side_out[field, pl.ds(end * (rows - REACH) + row, 1), :] = side_term(
                    after, to, group, size_y, gy
                )
        return carry

    lax.fori_loop(0, REACH, first, 0)
    kept_lines = pl.ds(PAD, lines, stride=KEEP_EVERY)
    for field in range(2):
        for row in range(REACH):
            down[field, row] = after[field, REACH + row, kept_lines, :]
            up[field, row] = after[2 + field, reach2 + row, kept_lines, :]

    def second(row, carry):
        for field in range(2):
            for end in range(2):
                group = 2 * end + field

                def store(here, value):
                    partial[field, end, row, here, :] = value

                second_step(
                    now, (1 - end) * REACH + row, scale, end * reach2 + row, after, REACH + row, group, masks, store
                )
        return carry

    lax.fori_loop(0, reach2, second, 0)


def outer(place, source, receiver, source_before, receiver_before, courant, border, left, right, side, side_in):
    rows, size_y, size_z = courant.shape
    lines = size_y // KEEP_EVERY
    halo = jax.ShapeDtypeStruct((2, REACH, lines, size_z), F32)
    return pl.pallas_call(
        outer_kernel,
        out_shape=(
            jax.ShapeDtypeStruct((2, 2, 2 * REACH, lines, size_z), F32),
            halo,
            halo,
            jax.ShapeDtypeStruct((2, rows, size_z), F32),
        ),
        in_specs=[SMEM] + [HBM] * 8 + [VMEM] * 2,
        out_specs=(VMEM,) * 4,
        scratch_shapes=[
            pltpu.VMEM((4, 3 * REACH, size_y + 2 * PAD, size_z), F32),
            pltpu.VMEM((4, REACH, size_y, size_z), F32),
            pltpu.VMEM((4 * REACH, size_y, size_z), F32),
            pltpu.VMEM((4, 4 * REACH, size_y + 2 * PAD, size_z), F32),
            pltpu.SemaphoreType.DMA((18,)),
        ],
        compiler_params=params(60),
        cost_estimate=cost(2 * 10**10, 16 * 2**20),
        name="outer",
    )(place, source, receiver, source_before, receiver_before, courant, border, left, right, side, side_in)


def pack_row(value, field, row, shot, keep, give):
    first, second = z_halves(value)
    keep[field, row] = jnp.where(shot == 0, first, second)
    give[field, row] = jnp.where(shot == 0, second, first)


def side_lines(side, field, row, gy, lines):
    line = lax.broadcasted_iota(jnp.int32, (lines, side.shape[2]), 0)
    meets = line == jnp.where(gy == 0, lines - 1, 0)
    return jnp.where(meets, side[field, pl.ds(row, 1), :], 0.0)


def middle_kernel(place, inside, ends, kept_courant, side, keep, give):
    shot, gy = place[0], place[1]
    rows, lines, _ = kept_courant.shape

    def one_row(row, values):
        for field in range(2):
            total = side_lines(side, field, row, gy, lines)
            pack_row(values[field] + kept_courant[row] * total, field, row - REACH, shot, keep, give)

    def middle(row, carry):
        one_row(row, [inside[field, row - 2 * REACH] for field in range(2)])
        return carry

    lax.fori_loop(2 * REACH, rows - 2 * REACH, middle, 0)
    for row in range(REACH, 2 * REACH):
        one_row(row, [ends[field, 0, row] for field in range(2)])
        one_row(rows - 1 - row, [ends[field, 1, 2 * REACH - 1 - row] for field in range(2)])


def finish_middle(place, inside, ends, kept_courant, side):
    rows, lines, size_z = kept_courant.shape
    half = jax.ShapeDtypeStruct((2, rows - 2 * REACH, lines // 2, size_z), F32)
    return pl.pallas_call(
        middle_kernel,
        out_shape=(half, half),
        in_specs=[SMEM] + [VMEM] * 4,
        out_specs=(VMEM,) * 2,
        compiler_params=params(24),
        cost_estimate=cost(10**10, 3 * 2**20),
        name="finish_middle",
    )(place, inside, ends, kept_courant, side)


def ends_kernel(place, ends, kept_courant, left, right, side, keep, give):
    shot, gy = place[0], place[1]
    rows, lines, _ = kept_courant.shape
    for field in range(2):
        for row in range(REACH):
            below = above = None
            for d in range(row + 1, REACH + 1):
                term = WEIGHTS[d] * left[field, REACH + row - d]
                below = term if below is None else below + term
                term = WEIGHTS[d] * right[field, d - 1 - row]
                above = term if above is None else above + term
            far = rows - 1 - row
            below = below + side_lines(side, field, row, gy, lines)
            above = above + side_lines(side, field, far, gy, lines)
            pack_row(ends[field, 0, row] + kept_courant[row] * below, field, row, shot, keep, give)
            pack_row(
                ends[field, 1, 2 * REACH - 1 - row] + kept_courant[far] * above,
                field, 2 * REACH - 1 - row, shot, keep, give,
            )


def finish_ends(place, ends, kept_courant, left, right, side):
    _, lines, size_z = kept_courant.shape
    half = jax.ShapeDtypeStruct((2, 2 * REACH, lines // 2, size_z), F32)
    return pl.pallas_call(
        ends_kernel,
        out_shape=(half, half),
        in_specs=[SMEM] + [VMEM] * 5,
        out_specs=(VMEM,) * 2,
        compiler_params=params(24),
        cost_estimate=cost(10**10, 3 * 2**20),
        name="finish_ends",
    )(place, ends, kept_courant, left, right, side)


def image_kernel(place, *refs):
    blocks, (out, rows_of, turned, sems) = refs[:12], refs[12:]
    parity = place[2]
    rows = blocks[0].shape[2]

    @pl.when(pl.program_id(0) == 0)
    def _():
        starts = (HALF, jnp.where(parity == 0, HALF + rows, 0), jnp.where(parity == 0, 0, HALF + rows))
        copies = []

        def copy(src, group, start, count):
            dst = rows_of.at[group, :, pl.ds(start, count)]
            copies.append(pltpu.make_async_copy(src, dst, sems.at[len(copies)]))

        for part in range(2):
            for kind in range(3):
                copy(blocks[kind].at[part], part, starts[kind], rows)
                copy(blocks[3 + 3 * part + kind], 2 + part, starts[kind] + REACH, rows - 2 * REACH)
            for kind, start in enumerate((HALF, 0, HALF + rows)):
                ends = blocks[9 + kind]
                copy(ends.at[part, :, pl.ds(0, REACH)], 2 + part, start, REACH)
                copy(ends.at[part, :, pl.ds(REACH, REACH)], 2 + part, start + rows - REACH, REACH)
        run_copies(copies)

    groups = rows_of.shape[0]
    lines, size_z = rows_of.shape[3], rows_of.shape[4]
    sample = 4 * pl.program_id(0)
    for chunk in range(lines // 8):
        here = pl.ds(8 * chunk, 8)
        for shift in range(OFFSETS):
            total = None
            for group in range(groups):
                term = (
                    rows_of[group, 0, 2 * HALF + sample - shift, here, :]
                    * rows_of[group, 1, sample + shift, here, :]
                )
                total = term if total is None else total + term
            turned[pl.ds(shift, 8, stride=OFFSET_ROWS), :] = total
        for line in range(8):
            values = turned[line * OFFSET_ROWS : (line + 1) * OFFSET_ROWS, :].T
            at = 8 * chunk + line
            out[0, at] = values[: size_z // 2, :OFFSETS]
            out[0, lines + at] = values[size_z // 2 :, :OFFSETS]


def image(place, blocks):
    rows, lines, size_z = blocks[0].shape[2:]
    samples = rows // 4
    return pl.pallas_call(
        image_kernel,
        grid=(samples,),
        out_shape=jax.ShapeDtypeStruct((samples, 2 * lines, size_z // 2, OFFSETS), F32),
        in_specs=[SMEM] + [HBM] * len(blocks),
        out_specs=pl.BlockSpec((1, 2 * lines, size_z // 2, OFFSETS), lambda i: (i, 0, 0, 0)),
        scratch_shapes=[
            pltpu.VMEM((4, 2, rows + 2 * HALF, lines, size_z), F32),
            pltpu.VMEM((8 * OFFSET_ROWS, size_z), F32),
            pltpu.SemaphoreType.DMA((24,)),
        ],
        compiler_params=params(24),
        cost_estimate=cost(16 * 2**20, 16 * 2**20),
        name="image",
    )(place, *blocks)


def in_order_kernel(place, *refs):
    refs[-1][...] = place[...]


def in_order(place, *arrays):
    return pl.pallas_call(
        in_order_kernel,
        out_shape=jax.ShapeDtypeStruct((8, 128), jnp.int32),
        in_specs=[VMEM] + [HBM] * len(arrays),
        out_specs=VMEM,
        cost_estimate=cost(10**10, 2**10),
        name="in_order",
    )(jnp.broadcast_to(jnp.pad(place, (0, 125)), (8, 128)), *arrays)[0, :3]


def on_device(source_now, source_before, receiver_now, receiver_before, courant):
    size = lax.axis_size("gx")
    place = jnp.stack(
        [lax.axis_index("shot"), lax.axis_index("gy"), lax.axis_index("gx") % 2]
    ).astype(jnp.int32)
    up_pairs = [(i, i + 1) for i in range(size - 1)]
    down_pairs = [(j, i) for i, j in up_pairs]
    partner = [(i, i ^ 1) for i in range(size)]
    onward = [(i, i + 2) for i in range(0, size - 2, 2)] + [(i, i - 2) for i in range(3, size, 2)]
    both = [(0, 1), (1, 0)]

    def exchange(array, axis, pairs):
        return lax.ppermute(array, axis, pairs)

    barrier = lax.optimization_barrier
    up, down, keep, give, side = pack(place, source_now, receiver_now)
    left = exchange(up, "gx", up_pairs)
    right = exchange(down, "gx", down_pairs)
    side = exchange(side, "gy", both)
    other = exchange(give, "shot", both)
    own = jnp.stack([keep, other])
    side, own = barrier((side, own))
    near = exchange(own, "gx", partner)
    inside, kept_courant, side_in, border = inner(
        place, source_now, receiver_now, source_before, receiver_before, courant, side
    )
    ends, up, down, side = outer(
        place, source_now, receiver_now, source_before, receiver_before, courant, border, left, right, side, side_in
    )
    left = exchange(up, "gx", up_pairs)
    right = exchange(down, "gx", down_pairs)
    side = exchange(side, "gy", both)

    keep, give = finish_middle(place, inside, ends, kept_courant, side)
    keep, give, near = barrier((keep, give, near))
    far = exchange(near, "gx", onward)
    other = exchange(give, "shot", both)
    near_keep = exchange(keep, "gx", partner)
    middle = [keep, other]

    keep, give = finish_ends(place, ends, kept_courant, left, right, side)
    middle[1], keep, give = barrier((middle[1], keep, give))
    near_other = exchange(middle[1], "gx", partner)
    other = exchange(give, "shot", both)
    blocks = [own, near, far]
    other, near_keep = barrier((other, near_keep))
    own = jnp.stack([keep, other])
    left = exchange(own, "gx", up_pairs)
    right = exchange(own, "gx", down_pairs)
    near_keep, far = barrier((near_keep, far))
    blocks[2] = far
    far_keep = exchange(near_keep, "gx", onward)
    far_other = exchange(near_other, "gx", onward)
    place = in_order(place, left, right, far_keep)
    keep, other = middle
    blocks[1] = near
    blocks += [keep, near_keep, far_keep, other, near_other, far_other, own, left, right]
    return jnp.transpose(image(place, blocks), (3, 0, 1, 2))


def solution(mesh):
    in_specs = (
        P("shot", "gx", "gy", None),
        P("shot", "gx", "gy", None),
        P("shot", "gx", "gy", None),
        P("shot", "gx", "gy", None),
        P("gx", "gy", None),
    )
    out_specs = P(None, "gx", "gy", "shot")
    return jax.shard_map(
        on_device, mesh=mesh, in_specs=in_specs, out_specs=out_specs, check_vma=False
    )
```

```python
import functools

import jax
import jax.numpy as jnp
from jax import lax
from jax.experimental import pallas as pl
from jax.experimental.pallas import tpu as pltpu
from jax.sharding import PartitionSpec as P

HALF = 32
REACH = 4
KEEP_EVERY = 4
OFFSETS = 2 * HALF + 1
OFFSET_ROWS = 72
WEIGHTS = (-205.0 / 72.0, 8.0 / 5.0, -1.0 / 5.0, 8.0 / 315.0, -1.0 / 560.0)
PAD = 8
F32 = jnp.float32
HBM = pl.BlockSpec(memory_space=pltpu.HBM)
ANY = pl.BlockSpec(memory_space=pl.ANY)
VMEM = pl.BlockSpec(memory_space=pltpu.VMEM)
SMEM = pl.BlockSpec(memory_space=pltpu.SMEM)


def params(mib):
    return pltpu.CompilerParams(vmem_limit_bytes=mib * 2**20)


def cost(flops, nbytes):
    return pl.CostEstimate(flops=flops, bytes_accessed=nbytes, transcendentals=0)


def run_copies(copies):
    for copy in copies:
        copy.start()
    for copy in copies:
        copy.wait()


def z_halves(lines):
    count, size_z = lines.shape
    top, bottom = lines[: count // 2], lines[count // 2 :]
    low = lax.broadcasted_iota(jnp.int32, top.shape, 1) < size_z // 2
    first = jnp.where(low, top, pltpu.roll(bottom, size_z // 2, 1))
    second = jnp.where(low, pltpu.roll(top, size_z // 2, 1), bottom)
    return first, second


def pack_kernel(place, source, receiver, up, down, keep, give, side):
    shot, gy = place[0], place[1]
    rows, size_y, size_z = source.shape[1:]
    lines = size_y // KEEP_EVERY
    step, steps = pl.program_id(0), pl.num_programs(0)

    @pl.when(step == 0)
    def _():
        for field, ref in enumerate((source, receiver)):
            down[field] = ref[0, :REACH]

    @pl.when(step == steps - 1)
    def _():
        for field, ref in enumerate((source, receiver)):
            up[field] = ref[0, rows - REACH :]

    for row in range(rows):
        parts = []
        for field, ref in enumerate((source, receiver)):
            first, second = z_halves(ref[0, row, pl.ds(0, lines, stride=KEEP_EVERY), :])
            keep[field, row] = jnp.where(shot == 0, first, second)
            give[field, row] = jnp.where(shot == 0, second, first)
            low = ref[0, row, 0:REACH, :]
            high = ref[0, row, size_y - REACH : size_y, :]
            parts.append(jnp.where(gy == 0, high, low))
        side[row] = jnp.concatenate(parts, axis=0)


def pack(place, source, receiver):
    _, rows, size_y, size_z = source.shape
    lines = size_y // KEEP_EVERY // 2
    step = 8
    edge = jax.ShapeDtypeStruct((2, REACH, size_y, size_z), F32)
    half = jax.ShapeDtypeStruct((2, rows, lines, size_z), F32)
    edge_spec = pl.BlockSpec((2, REACH, size_y, size_z), lambda i: (0, 0, 0, 0))
    half_spec = pl.BlockSpec((2, step, lines, size_z), lambda i: (0, i, 0, 0))
    field_spec = pl.BlockSpec((1, step, size_y, size_z), lambda i: (0, i, 0, 0))
    return pl.pallas_call(
        pack_kernel,
        grid=(rows // step,),
        out_shape=(edge, edge, half, half, jax.ShapeDtypeStruct((rows, 2 * REACH, size_z), F32)),
        in_specs=[SMEM, field_spec, field_spec],
        out_specs=(
            edge_spec,
            edge_spec,
            half_spec,
            half_spec,
            pl.BlockSpec((step, 2 * REACH, size_z), lambda i: (i, 0, 0)),
        ),
        cost_estimate=cost(10**10, 7 * 2**20),
        name="pack",
    )(place, source, receiver)


def z_weights(size_z):
    z = lax.broadcasted_iota(jnp.int32, (8, size_z), 1)
    return [
        (jnp.where(z >= d, WEIGHTS[d], 0.0), jnp.where(z < size_z - d, WEIGHTS[d], 0.0))
        for d in range(1, REACH + 1)
    ]


def z_terms(center, masks):
    size_z = center.shape[1]
    total = None
    for d, (below, above) in enumerate(masks, start=1):
        term = below * pltpu.roll(center, d, 1) + above * pltpu.roll(center, size_z - d, 1)
        total = term if total is None else total + term
    return total


def first_step(now, row, before, before_row, scale, scale_row, after, after_row, field, masks, zero):
    size_y = before.shape[2]
    for chunk in range(size_y // 8):
        at = PAD + 8 * chunk
        center = now[field, row, at : at + 8, :]
        total = (3.0 * WEIGHTS[0]) * center + z_terms(center, masks)
        for d in range(1, REACH + 1):
            around = (
                now[field, row + d, at : at + 8, :]
                + now[field, row - d, at : at + 8, :]
                + now[field, row, pl.ds(zero + (at + d), 8), :]
                + now[field, row, pl.ds(zero + (at - d), 8), :]
            )
            total = total + WEIGHTS[d] * around
        here = pl.ds(8 * chunk, 8)
        after[field, after_row, at : at + 8, :] = (
            2.0 * center - before[field, before_row, here, :] + scale[scale_row, here, :] * total
        )


def second_step(now, row, scale, scale_row, after, after_row, field, masks, store):
    size_y = scale.shape[1]
    for chunk in range(size_y // KEEP_EVERY // 8):
        at = PAD + 8 * KEEP_EVERY * chunk
        kept = lambda start: pl.ds(start, 8, stride=KEEP_EVERY)
        center = after[field, after_row, kept(at), :]
        total = (3.0 * WEIGHTS[0]) * center + z_terms(center, masks)
        for d in range(1, REACH + 1):
            around = (
                after[field, after_row + d, kept(at), :]
                + after[field, after_row - d, kept(at), :]
                + after[field, after_row, kept(at + d), :]
                + after[field, after_row, kept(at - d), :]
            )
            total = total + WEIGHTS[d] * around
        store(
            pl.ds(8 * chunk, 8),
            2.0 * center - now[field, row, kept(at), :] + scale[scale_row, kept(at - PAD), :] * total,
        )


def side_term(after, after_row, field, size_y, gy):
    lowest = WEIGHTS[REACH] * after[field, after_row, PAD : PAD + 1, :]
    highest = sum(
        WEIGHTS[d] * after[field, after_row, PAD + size_y - d : PAD + size_y - d + 1, :]
        for d in range(1, REACH + 1)
    )
    return jnp.where(gy == 0, highest, lowest)


def fill_sides(now, row, got, field, size_y, gy):
    blank = jnp.zeros_like(got)
    now[field, row, PAD - REACH : PAD, :] = jnp.where(gy == 0, blank, got)
    now[field, row, size_y + PAD : size_y + PAD + REACH, :] = jnp.where(gy == 0, got, blank)


def blank_sides(after, row, field, size_y):
    blank = jnp.zeros((REACH, after.shape[3]), F32)
    after[field, row, PAD - REACH : PAD, :] = blank
    after[field, row, size_y + PAD : size_y + PAD + REACH, :] = blank


def inner_kernel(
    place, source, receiver, source_before, receiver_before, courant, side,
    partial, kept_courant, side_out, border, now, before, scale, after, sems, out_sems,
):
    gy = place[1]
    rows, size_y, size_z = courant.shape
    lines = size_y // KEEP_EVERY
    copies = []

    def copy(src, dst):
        copies.append(pltpu.make_async_copy(src, dst, sems.at[len(copies)]))

    middle = pl.ds(PAD, size_y)
    for field, ref in enumerate((source, receiver)):
        copy(ref.at[0], now.at[field, :, middle])
    for field, ref in enumerate((source_before, receiver_before)):
        copy(ref.at[0], before.at[field])
    copy(courant, scale)
    for one in copies:
        one.start()

    def fill(row, carry):
        for field in range(2):
            got = side[row, field * REACH : (field + 1) * REACH, :]
            fill_sides(now, row, got, field, size_y, gy)
            blank_sides(after, row, field, size_y)
        return carry

    lax.fori_loop(0, rows, fill, 0)
    side_out[...] = jnp.zeros_like(side_out)
    for one in copies:
        one.wait()
    masks = z_weights(size_z)

    def first(row, carry):
        for field in range(2):
            first_step(now, row, before, row, scale, row, after, row, field, masks, place[3])
            side_out[field, pl.ds(row, 1), :] = side_term(after, row, field, size_y, gy)
        return carry

    lax.fori_loop(REACH, rows - REACH, first, 0)
    outs = []
    for field in range(2):
        for end, start in enumerate((REACH, rows - 3 * REACH)):
            outs.append(
                pltpu.make_async_copy(
                    after.at[field, pl.ds(start, 2 * REACH), middle],
                    border.at[field, end],
                    out_sems.at[len(outs)],
                )
            )
            outs[-1].start()

    def second(row, carry):
        for field in range(2):
            def store(here, value):
                partial[field, row - 2 * REACH, here, :] = value

            second_step(now, row, scale, row, after, row, field, masks, store)
        return carry

    lax.fori_loop(2 * REACH, rows - 2 * REACH, second, 0)

    def keep(row, carry):
        kept_courant[row] = scale[row, pl.ds(0, lines, stride=KEEP_EVERY), :]
        return carry

    lax.fori_loop(0, rows, keep, 0)
    for one in outs:
        one.wait()


def inner(place, source, receiver, source_before, receiver_before, courant, side):
    rows, size_y, size_z = courant.shape
    lines = size_y // KEEP_EVERY
    return pl.pallas_call(
        inner_kernel,
        out_shape=(
            jax.ShapeDtypeStruct((2, rows - 4 * REACH, lines, size_z), F32),
            jax.ShapeDtypeStruct((rows, lines, size_z), F32),
            jax.ShapeDtypeStruct((2, rows, size_z), F32),
            jax.ShapeDtypeStruct((2, 2, 2 * REACH, size_y, size_z), F32),
        ),
        in_specs=[SMEM] + [HBM] * 5 + [VMEM],
        out_specs=(VMEM,) * 3 + (HBM,),
        scratch_shapes=[
            pltpu.VMEM((2, rows, size_y + 2 * PAD, size_z), F32),
            pltpu.VMEM((2, rows, size_y, size_z), F32),
            pltpu.VMEM((rows, size_y, size_z), F32),
            pltpu.VMEM((2, rows, size_y + 2 * PAD, size_z), F32),
            pltpu.SemaphoreType.DMA((5,)),
            pltpu.SemaphoreType.DMA((4,)),
        ],
        compiler_params=params(60),
        cost_estimate=cost(2 * 10**10, 2**20),
        name="inner",
    )(place, source, receiver, source_before, receiver_before, courant, side)


def outer_kernel(
    place, source, receiver, source_before, receiver_before, courant, border, left, right, side, side_in,
    partial, up, down, side_out, now, before, scale, after, sems,
):
    gy = place[1]
    rows, size_y, size_z = courant.shape
    lines = size_y // KEEP_EVERY
    reach2 = 2 * REACH
    copies = []

    def copy(src, dst):
        copies.append(pltpu.make_async_copy(src, dst, sems.at[len(copies)]))

    middle = pl.ds(PAD, size_y)
    for field in range(2):
        ref = (source, receiver)[field]
        copy(ref.at[0, pl.ds(0, reach2)], now.at[field, pl.ds(REACH, reach2), middle])
        copy(left.at[field], now.at[field, pl.ds(0, REACH), middle])
        copy(ref.at[0, pl.ds(rows - reach2, reach2)], now.at[2 + field, pl.ds(0, reach2), middle])
        copy(right.at[field], now.at[2 + field, pl.ds(reach2, REACH), middle])
        ref = (source_before, receiver_before)[field]
        copy(ref.at[0, pl.ds(0, REACH)], before.at[field])
        copy(ref.at[0, pl.ds(rows - REACH, REACH)], before.at[2 + field])
        copy(border.at[field, 0], after.at[field, pl.ds(reach2, reach2), middle])
        copy(border.at[field, 1], after.at[2 + field, pl.ds(0, reach2), middle])
    copy(courant.at[pl.ds(0, reach2)], scale.at[pl.ds(0, reach2)])
    copy(courant.at[pl.ds(rows - reach2, reach2)], scale.at[pl.ds(reach2, reach2)])
    for one in copies:
        one.start()

    for field in range(2):
        for row in range(REACH):
            for end in range(2):
                after[2 * end + field, 3 * REACH * end + row] = jnp.zeros((size_y + 2 * PAD, size_z), F32)
        for row in range(reach2):
            low = side[row, field * REACH : (field + 1) * REACH, :]
            fill_sides(now, REACH + row, low, field, size_y, gy)
            high = side[rows - reach2 + row, field * REACH : (field + 1) * REACH, :]
            fill_sides(now, row, high, 2 + field, size_y, gy)
            for end in range(2):
                blank_sides(after, REACH + row, 2 * end + field, size_y)
    side_out[...] = side_in[...]
    for one in copies:
        one.wait()
    masks = z_weights(size_z)

    def first(row, carry):
        for field in range(2):
            for end in range(2):
                group = 2 * end + field
                to = REACH * (1 + end) + row
                first_step(
                    now, REACH + row, before, row, scale, (2 * end + end) * REACH + row,
                    after, to, group, masks, place[3],
                )
                side_out[field, pl.ds(end * (rows - REACH) + row, 1), :] = side_term(
                    after, to, group, size_y, gy
                )
        return carry

    lax.fori_loop(0, REACH, first, 0)
    kept_lines = pl.ds(PAD, lines, stride=KEEP_EVERY)
    for field in range(2):
        for row in range(REACH):
            down[field, row] = after[field, REACH + row, kept_lines, :]
            up[field, row] = after[2 + field, reach2 + row, kept_lines, :]

    def second(row, carry):
        for field in range(2):
            for end in range(2):
                group = 2 * end + field

                def store(here, value):
                    partial[field, end, row, here, :] = value

                second_step(
                    now, (1 - end) * REACH + row, scale, end * reach2 + row, after, REACH + row, group, masks, store
                )
        return carry

    lax.fori_loop(0, reach2, second, 0)


def outer(place, source, receiver, source_before, receiver_before, courant, border, left, right, side, side_in):
    rows, size_y, size_z = courant.shape
    lines = size_y // KEEP_EVERY
    halo = jax.ShapeDtypeStruct((2, REACH, lines, size_z), F32)
    return pl.pallas_call(
        outer_kernel,
        out_shape=(
            jax.ShapeDtypeStruct((2, 2, 2 * REACH, lines, size_z), F32),
            halo,
            halo,
            jax.ShapeDtypeStruct((2, rows, size_z), F32),
        ),
        in_specs=[SMEM] + [HBM] * 8 + [VMEM] * 2,
        out_specs=(VMEM,) * 4,
        scratch_shapes=[
            pltpu.VMEM((4, 3 * REACH, size_y + 2 * PAD, size_z), F32),
            pltpu.VMEM((4, REACH, size_y, size_z), F32),
            pltpu.VMEM((4 * REACH, size_y, size_z), F32),
            pltpu.VMEM((4, 4 * REACH, size_y + 2 * PAD, size_z), F32),
            pltpu.SemaphoreType.DMA((18,)),
        ],
        compiler_params=params(60),
        cost_estimate=cost(10**6, 2**20),
        name="outer",
    )(place, source, receiver, source_before, receiver_before, courant, border, left, right, side, side_in)


def pack_row(value, field, row, shot, keep, give):
    first, second = z_halves(value)
    keep[field, row] = jnp.where(shot == 0, first, second)
    give[field, row] = jnp.where(shot == 0, second, first)


def side_lines(side, field, row, gy, lines):
    line = lax.broadcasted_iota(jnp.int32, (lines, side.shape[2]), 0)
    meets = line == jnp.where(gy == 0, lines - 1, 0)
    return jnp.where(meets, side[field, pl.ds(row, 1), :], 0.0)


def middle_kernel(place, inside, ends, kept_courant, side, keep, give):
    shot, gy = place[0], place[1]
    rows, lines, _ = kept_courant.shape

    def one_row(row, values):
        for field in range(2):
            total = side_lines(side, field, row, gy, lines)
            pack_row(values[field] + kept_courant[row] * total, field, row - REACH, shot, keep, give)

    def middle(row, carry):
        one_row(row, [inside[field, row - 2 * REACH] for field in range(2)])
        return carry

    lax.fori_loop(2 * REACH, rows - 2 * REACH, middle, 0)
    for row in range(REACH, 2 * REACH):
        one_row(row, [ends[field, 0, row] for field in range(2)])
        one_row(rows - 1 - row, [ends[field, 1, 2 * REACH - 1 - row] for field in range(2)])


def finish_middle(place, inside, ends, kept_courant, side):
    rows, lines, size_z = kept_courant.shape
    half = jax.ShapeDtypeStruct((2, rows - 2 * REACH, lines // 2, size_z), F32)
    return pl.pallas_call(
        middle_kernel,
        out_shape=(half, half),
        in_specs=[SMEM] + [VMEM] * 4,
        out_specs=(VMEM,) * 2,
        compiler_params=params(24),
        cost_estimate=cost(10**10, 3 * 2**20),
        name="finish_middle",
    )(place, inside, ends, kept_courant, side)


def ends_kernel(place, ends, kept_courant, left, right, side, keep, give):
    shot, gy = place[0], place[1]
    rows, lines, _ = kept_courant.shape
    for field in range(2):
        for row in range(REACH):
            below = above = None
            for d in range(row + 1, REACH + 1):
                term = WEIGHTS[d] * left[field, REACH + row - d]
                below = term if below is None else below + term
                term = WEIGHTS[d] * right[field, d - 1 - row]
                above = term if above is None else above + term
            far = rows - 1 - row
            below = below + side_lines(side, field, row, gy, lines)
            above = above + side_lines(side, field, far, gy, lines)
            pack_row(ends[field, 0, row] + kept_courant[row] * below, field, row, shot, keep, give)
            pack_row(
                ends[field, 1, 2 * REACH - 1 - row] + kept_courant[far] * above,
                field, 2 * REACH - 1 - row, shot, keep, give,
            )


def finish_ends(place, ends, kept_courant, left, right, side):
    _, lines, size_z = kept_courant.shape
    half = jax.ShapeDtypeStruct((2, 2 * REACH, lines // 2, size_z), F32)
    return pl.pallas_call(
        ends_kernel,
        out_shape=(half, half),
        in_specs=[SMEM] + [VMEM] * 5,
        out_specs=(VMEM,) * 2,
        compiler_params=params(24),
        cost_estimate=cost(10**10, 3 * 2**20),
        name="finish_ends",
    )(place, ends, kept_courant, left, right, side)


def block_starts(place, rows):
    even = place[2] == 0
    return HALF, jnp.where(even, HALF + rows, 0), jnp.where(even, 0, HALF + rows)


def products(rows_of, sample, shift, here):
    total = None
    for group in range(rows_of.shape[0]):
        term = (
            rows_of[group, 0, 2 * HALF + sample - shift, here, :]
            * rows_of[group, 1, sample + shift, here, :]
        )
        total = term if total is None else total + term
    return total


def first_image_kernel(place, *refs):
    blocks, (out, rows_of, sems) = refs[:6], refs[6:]
    rows = blocks[0].shape[1]

    @pl.when(pl.program_id(0) == 0)
    def _():
        starts = block_starts(place, rows)
        copies = []
        for index, ref in enumerate(blocks):
            dst = rows_of.at[index // 3, :, pl.ds(starts[index % 3], rows)]
            copies.append(pltpu.make_async_copy(ref, dst, sems.at[index]))
        run_copies(copies)

    sample = 4 * pl.program_id(0)
    for chunk in range(rows_of.shape[3] // 8):
        here = pl.ds(8 * chunk, 8)
        for shift in range(OFFSETS):
            out[0, shift, here, :] = products(rows_of, sample, shift, here)


def first_image(place, blocks):
    _, rows, lines, size_z = blocks[0].shape
    samples = rows // 4
    return pl.pallas_call(
        first_image_kernel,
        grid=(samples,),
        out_shape=jax.ShapeDtypeStruct((samples, OFFSETS, lines, size_z), F32),
        in_specs=[SMEM] + [ANY] * len(blocks),
        out_specs=pl.BlockSpec((1, OFFSETS, lines, size_z), lambda i: (i, 0, 0, 0)),
        scratch_shapes=[
            pltpu.VMEM((2, 2, rows + 2 * HALF, lines, size_z), F32),
            pltpu.SemaphoreType.DMA((6,)),
        ],
        compiler_params=params(16),
        cost_estimate=cost(10**10, 8 * 2**20),
        name="first_image",
    )(place, *blocks)


def image_kernel(place, first, *refs):
    blocks, (out, rows_of, turned, sems) = refs[:9], refs[9:]
    rows = blocks[0].shape[1] + 2 * REACH

    @pl.when(pl.program_id(0) == 0)
    def _():
        starts = block_starts(place, rows)
        copies = []

        def copy(src, group, start, count):
            dst = rows_of.at[group, :, pl.ds(start, count)]
            copies.append(pltpu.make_async_copy(src, dst, sems.at[len(copies)]))

        for part in range(2):
            for kind in range(3):
                copy(blocks[3 * part + kind], part, starts[kind] + REACH, rows - 2 * REACH)
            for kind, start in enumerate((HALF, 0, HALF + rows)):
                ends = blocks[6 + kind]
                copy(ends.at[part, :, pl.ds(0, REACH)], part, start, REACH)
                copy(ends.at[part, :, pl.ds(REACH, REACH)], part, start + rows - REACH, REACH)
        run_copies(copies)

    lines, size_z = rows_of.shape[3], rows_of.shape[4]
    sample = 4 * pl.program_id(0)
    for chunk in range(lines // 8):
        here = pl.ds(8 * chunk, 8)
        for shift in range(OFFSETS):
            total = first[0, shift, here, :] + products(rows_of, sample, shift, here)
            turned[pl.ds(shift, 8, stride=OFFSET_ROWS), :] = total
        for line in range(8):
            values = turned[line * OFFSET_ROWS : (line + 1) * OFFSET_ROWS, :].T
            at = 8 * chunk + line
            out[0, at] = values[: size_z // 2, :OFFSETS]
            out[0, lines + at] = values[size_z // 2 :, :OFFSETS]


def image(place, first, blocks):
    samples, _, lines, size_z = first.shape
    rows = 4 * samples
    return pl.pallas_call(
        image_kernel,
        grid=(samples,),
        out_shape=jax.ShapeDtypeStruct((samples, 2 * lines, size_z // 2, OFFSETS), F32),
        in_specs=[SMEM, pl.BlockSpec((1, OFFSETS, lines, size_z), lambda i: (i, 0, 0, 0))] + [ANY] * len(blocks),
        out_specs=pl.BlockSpec((1, 2 * lines, size_z // 2, OFFSETS), lambda i: (i, 0, 0, 0)),
        scratch_shapes=[
            pltpu.VMEM((2, 2, rows + 2 * HALF, lines, size_z), F32),
            pltpu.VMEM((8 * OFFSET_ROWS, size_z), F32),
            pltpu.SemaphoreType.DMA((18,)),
        ],
        compiler_params=params(20),
        cost_estimate=cost(10**10, 16 * 2**20),
        name="image",
    )(place, first, *blocks)


def in_order_kernel(place, *refs):
    for index in range(place.shape[0]):
        refs[-1][index] = place[index]


def in_order(place, *arrays):
    return pl.pallas_call(
        in_order_kernel,
        out_shape=jax.ShapeDtypeStruct(place.shape, jnp.int32),
        in_specs=[SMEM] + [ANY] * len(arrays),
        out_specs=SMEM,
        cost_estimate=cost(10**10, 2**10),
        name="in_order",
    )(place, *arrays)


def on_device(source_now, source_before, receiver_now, receiver_before, courant):
    size = lax.axis_size("gx")
    place = jnp.stack(
        [lax.axis_index("shot"), lax.axis_index("gy"), lax.axis_index("gx") % 2, 0]
    ).astype(jnp.int32)
    up_pairs = [(i, i + 1) for i in range(size - 1)]
    down_pairs = [(j, i) for i, j in up_pairs]
    partner = [(i, i ^ 1) for i in range(size)]
    onward = [(i, i + 2) for i in range(0, size - 2, 2)] + [(i, i - 2) for i in range(3, size, 2)]
    both = [(0, 1), (1, 0)]

    def exchange(array, axis, pairs):
        return lax.ppermute(array, axis, pairs)

    barrier = lax.optimization_barrier
    up, down, keep, give, side = pack(place, source_now, receiver_now)
    left = exchange(up, "gx", up_pairs)
    right = exchange(down, "gx", down_pairs)
    side = exchange(side, "gy", both)
    other = exchange(give, "shot", both)
    side, keep, other = barrier((side, keep, other))
    near_keep = exchange(keep, "gx", partner)
    near_other = exchange(other, "gx", partner)
    blocks = [keep, near_keep, None, other, near_other, None]
    inside, kept_courant, side_in, border = inner(
        place, source_now, receiver_now, source_before, receiver_before, courant, side
    )
    ends, up, down, side = outer(
        place, source_now, receiver_now, source_before, receiver_before, courant, border, left, right, side, side_in
    )
    left = exchange(up, "gx", up_pairs)
    right = exchange(down, "gx", down_pairs)
    side = exchange(side, "gy", both)
    side, near_keep = barrier((side, near_keep))
    far_keep = exchange(near_keep, "gx", onward)

    keep, give = finish_middle(place, inside, ends, kept_courant, side)
    keep, give, near_other = barrier((keep, give, near_other))
    blocks[5] = exchange(near_other, "gx", onward)
    other = exchange(give, "shot", both)
    near_keep = exchange(keep, "gx", partner)

    left, right, blocks[2] = barrier((left, right, far_keep))
    keep_ends, give_ends = finish_ends(place, ends, kept_courant, left, right, side)
    other, keep_ends, give_ends = barrier((other, keep_ends, give_ends))
    near_other = exchange(other, "gx", partner)
    other_ends = exchange(give_ends, "shot", both)
    other_ends, near_keep = barrier((other_ends, near_keep))
    own = jnp.stack([keep_ends, other_ends])
    left = exchange(own, "gx", up_pairs)
    right = exchange(own, "gx", down_pairs)
    far_keep = exchange(near_keep, "gx", onward)
    far_other = exchange(near_other, "gx", onward)
    first = first_image(place, blocks)
    place = in_order(place, first, left, right, far_keep)
    blocks = [keep, near_keep, far_keep, other, near_other, far_other, own, left, right]
    return jnp.transpose(image(place, first, blocks), (3, 0, 1, 2))


def solution(mesh):
    in_specs = (
        P("shot", "gx", "gy", None),
        P("shot", "gx", "gy", None),
        P("shot", "gx", "gy", None),
        P("shot", "gx", "gy", None),
        P("gx", "gy", None),
    )
    out_specs = P(None, "gx", "gy", "shot")
    return jax.shard_map(
        on_device, mesh=mesh, in_specs=in_specs, out_specs=out_specs, check_vma=False
    )
```

```python
import functools

import jax
import jax.numpy as jnp
from jax import lax
from jax.experimental import pallas as pl
from jax.experimental.pallas import tpu as pltpu
from jax.sharding import PartitionSpec as P

HALF = 32
REACH = 4
KEEP_EVERY = 4
OFFSETS = 2 * HALF + 1
OFFSET_ROWS = 72
LINES = 32
WEIGHTS = (-205.0 / 72.0, 8.0 / 5.0, -1.0 / 5.0, 8.0 / 315.0, -1.0 / 560.0)
PAD = 8
F32 = jnp.float32
HBM = pl.BlockSpec(memory_space=pltpu.HBM)
ANY = pl.BlockSpec(memory_space=pl.ANY)
VMEM = pl.BlockSpec(memory_space=pltpu.VMEM)
SMEM = pl.BlockSpec(memory_space=pltpu.SMEM)


def params(mib):
    return pltpu.CompilerParams(vmem_limit_bytes=mib * 2**20)


def cost(flops, nbytes):
    return pl.CostEstimate(flops=flops, bytes_accessed=nbytes, transcendentals=0)


def run_copies(copies):
    for copy in copies:
        copy.start()
    for copy in copies:
        copy.wait()


def z_halves(lines):
    count, size_z = lines.shape
    top, bottom = lines[: count // 2], lines[count // 2 :]
    low = lax.broadcasted_iota(jnp.int32, top.shape, 1) < size_z // 2
    first = jnp.where(low, top, pltpu.roll(bottom, size_z // 2, 1))
    second = jnp.where(low, pltpu.roll(top, size_z // 2, 1), bottom)
    return first, second


def pack_kernel(source, receiver, up, down, keep, give, side):
    shot, gy = lax.axis_index("shot"), lax.axis_index("gy")
    rows, size_y, size_z = source.shape[1:]
    lines = size_y // KEEP_EVERY
    step, steps = pl.program_id(0), pl.num_programs(0)

    @pl.when(step == 0)
    def _():
        for field, ref in enumerate((source, receiver)):
            down[field] = ref[0, :REACH]

    @pl.when(step == steps - 1)
    def _():
        for field, ref in enumerate((source, receiver)):
            up[field] = ref[0, rows - REACH :]

    for row in range(rows):
        parts = []
        for field, ref in enumerate((source, receiver)):
            first, second = z_halves(ref[0, row, pl.ds(0, lines, stride=KEEP_EVERY), :])
            keep[field, row] = jnp.where(shot == 0, first, second)
            give[field, row] = jnp.where(shot == 0, second, first)
            low = ref[0, row, 0:REACH, :]
            high = ref[0, row, size_y - REACH : size_y, :]
            parts.append(jnp.where(gy == 0, high, low))
        side[row] = jnp.concatenate(parts, axis=0)


def pack(source, receiver):
    _, rows, size_y, size_z = source.shape
    lines = size_y // KEEP_EVERY // 2
    step = 8
    edge = jax.ShapeDtypeStruct((2, REACH, size_y, size_z), F32)
    half = jax.ShapeDtypeStruct((2, rows, lines, size_z), F32)
    edge_spec = pl.BlockSpec((2, REACH, size_y, size_z), lambda i: (0, 0, 0, 0))
    half_spec = pl.BlockSpec((2, step, lines, size_z), lambda i: (0, i, 0, 0))
    field_spec = pl.BlockSpec((1, step, size_y, size_z), lambda i: (0, i, 0, 0))
    return pl.pallas_call(
        pack_kernel,
        grid=(rows // step,),
        out_shape=(edge, edge, half, half, jax.ShapeDtypeStruct((rows, 2 * REACH, size_z), F32)),
        in_specs=[field_spec, field_spec],
        out_specs=(
            edge_spec,
            edge_spec,
            half_spec,
            half_spec,
            pl.BlockSpec((step, 2 * REACH, size_z), lambda i: (i, 0, 0)),
        ),
        cost_estimate=cost(10**10, 7 * 2**20),
        name="pack",
    )(source, receiver)


def z_weights(size_z):
    z = lax.broadcasted_iota(jnp.int32, (8, size_z), 1)
    return [
        (jnp.where(z >= d, WEIGHTS[d], 0.0), jnp.where(z < size_z - d, WEIGHTS[d], 0.0))
        for d in range(1, REACH + 1)
    ]


def z_terms(center, masks):
    size_z = center.shape[1]
    center = center.reshape(-1, 8, size_z)
    total = None
    for d, (below, above) in enumerate(masks, start=1):
        term = below * pltpu.roll(center, d, 2) + above * pltpu.roll(center, size_z - d, 2)
        total = term if total is None else total + term
    return total.reshape(-1, size_z)


def first_step(now, row, before, before_row, scale, scale_row, after, after_row, field, masks):
    size_y = before.shape[2]
    for chunk in range(size_y // LINES):
        at = PAD + LINES * chunk
        center = now[field, row, at : at + LINES, :]
        total = (3.0 * WEIGHTS[0]) * center + z_terms(center, masks)
        for d in range(1, REACH + 1):
            around = (
                now[field, row + d, at : at + LINES, :]
                + now[field, row - d, at : at + LINES, :]
                + now[field, row, at + d : at + d + LINES, :]
                + now[field, row, at - d : at - d + LINES, :]
            )
            total = total + WEIGHTS[d] * around
        here = pl.ds(LINES * chunk, LINES)
        after[field, after_row, at : at + LINES, :] = (
            2.0 * center - before[field, before_row, here, :] + scale[scale_row, here, :] * total
        )


def second_step(now, row, scale, scale_row, after, after_row, field, masks, store):
    size_y = scale.shape[1]
    lines = size_y // KEEP_EVERY
    kept = lambda start: pl.ds(start, lines, stride=KEEP_EVERY)
    center = after[field, after_row, kept(PAD), :]
    total = (3.0 * WEIGHTS[0]) * center + z_terms(center, masks)
    for d in range(1, REACH + 1):
        around = (
            after[field, after_row + d, kept(PAD), :]
            + after[field, after_row - d, kept(PAD), :]
            + after[field, after_row, kept(PAD + d), :]
            + after[field, after_row, kept(PAD - d), :]
        )
        total = total + WEIGHTS[d] * around
    store(2.0 * center - now[field, row, kept(PAD), :] + scale[scale_row, kept(0), :] * total)


def side_term(after, after_row, field, size_y, gy):
    lowest = WEIGHTS[REACH] * after[field, after_row, PAD : PAD + 1, :]
    highest = sum(
        WEIGHTS[d] * after[field, after_row, PAD + size_y - d : PAD + size_y - d + 1, :]
        for d in range(1, REACH + 1)
    )
    return jnp.where(gy == 0, highest, lowest)


def fill_sides(now, row, got, field, size_y, gy):
    blank = jnp.zeros_like(got)
    now[field, row, PAD - REACH : PAD, :] = jnp.where(gy == 0, blank, got)
    now[field, row, size_y + PAD : size_y + PAD + REACH, :] = jnp.where(gy == 0, got, blank)


def blank_sides(after, row, field, size_y):
    blank = jnp.zeros((REACH, after.shape[3]), F32)
    after[field, row, PAD - REACH : PAD, :] = blank
    after[field, row, size_y + PAD : size_y + PAD + REACH, :] = blank


def inner_kernel(
    source, receiver, source_before, receiver_before, courant, side,
    partial, kept_courant, side_out, border, now, before, scale, after, sems, out_sems,
):
    gy = lax.axis_index("gy")
    rows, size_y, size_z = courant.shape
    lines = size_y // KEEP_EVERY
    copies = []

    def copy(src, dst):
        copies.append(pltpu.make_async_copy(src, dst, sems.at[len(copies)]))

    middle = pl.ds(PAD, size_y)
    for field, ref in enumerate((source, receiver)):
        copy(ref.at[0], now.at[field, :, middle])
    for field, ref in enumerate((source_before, receiver_before)):
        copy(ref.at[0], before.at[field])
    copy(courant, scale)
    for one in copies:
        one.start()

    def fill(row, carry):
        for field in range(2):
            got = side[row, field * REACH : (field + 1) * REACH, :]
            fill_sides(now, row, got, field, size_y, gy)
            blank_sides(after, row, field, size_y)
        return carry

    lax.fori_loop(0, rows, fill, 0)
    side_out[...] = jnp.zeros_like(side_out)
    for one in copies:
        one.wait()
    masks = z_weights(size_z)

    def first(row, carry):
        for field in range(2):
            first_step(now, row, before, row, scale, row, after, row, field, masks)
            side_out[field, pl.ds(row, 1), :] = side_term(after, row, field, size_y, gy)
        return carry

    lax.fori_loop(REACH, rows - REACH, first, 0)
    outs = []
    for field in range(2):
        for end, start in enumerate((REACH, rows - 3 * REACH)):
            outs.append(
                pltpu.make_async_copy(
                    after.at[field, pl.ds(start, 2 * REACH), middle],
                    border.at[field, end],
                    out_sems.at[len(outs)],
                )
            )
            outs[-1].start()

    def second(row, carry):
        for field in range(2):
            def store(value):
                partial[field, row - 2 * REACH] = value

            second_step(now, row, scale, row, after, row, field, masks, store)
        return carry

    lax.fori_loop(2 * REACH, rows - 2 * REACH, second, 0)

    def keep(row, carry):
        kept_courant[row] = scale[row, pl.ds(0, lines, stride=KEEP_EVERY), :]
        return carry

    lax.fori_loop(0, rows, keep, 0)
    for one in outs:
        one.wait()


def inner(source, receiver, source_before, receiver_before, courant, side):
    rows, size_y, size_z = courant.shape
    lines = size_y // KEEP_EVERY
    return pl.pallas_call(
        inner_kernel,
        out_shape=(
            jax.ShapeDtypeStruct((2, rows - 4 * REACH, lines, size_z), F32),
            jax.ShapeDtypeStruct((rows, lines, size_z), F32),
            jax.ShapeDtypeStruct((2, rows, size_z), F32),
            jax.ShapeDtypeStruct((2, 2, 2 * REACH, size_y, size_z), F32),
        ),
        in_specs=[HBM] * 5 + [VMEM],
        out_specs=(VMEM,) * 3 + (HBM,),
        scratch_shapes=[
            pltpu.VMEM((2, rows, size_y + 2 * PAD, size_z), F32),
            pltpu.VMEM((2, rows, size_y, size_z), F32),
            pltpu.VMEM((rows, size_y, size_z), F32),
            pltpu.VMEM((2, rows, size_y + 2 * PAD, size_z), F32),
            pltpu.SemaphoreType.DMA((5,)),
            pltpu.SemaphoreType.DMA((4,)),
        ],
        compiler_params=params(60),
        cost_estimate=cost(2 * 10**10, 2**20),
        name="inner",
    )(source, receiver, source_before, receiver_before, courant, side)


def outer_kernel(
    source, receiver, source_before, receiver_before, courant, border, left, right, side, side_in,
    partial, up, down, side_out, now, before, scale, after, sems,
):
    gy = lax.axis_index("gy")
    rows, size_y, size_z = courant.shape
    lines = size_y // KEEP_EVERY
    reach2 = 2 * REACH
    copies = []

    def copy(src, dst):
        copies.append(pltpu.make_async_copy(src, dst, sems.at[len(copies)]))

    middle = pl.ds(PAD, size_y)
    for field in range(2):
        ref = (source, receiver)[field]
        copy(ref.at[0, pl.ds(0, reach2)], now.at[field, pl.ds(REACH, reach2), middle])
        copy(left.at[field], now.at[field, pl.ds(0, REACH), middle])
        copy(ref.at[0, pl.ds(rows - reach2, reach2)], now.at[2 + field, pl.ds(0, reach2), middle])
        copy(right.at[field], now.at[2 + field, pl.ds(reach2, REACH), middle])
        ref = (source_before, receiver_before)[field]
        copy(ref.at[0, pl.ds(0, REACH)], before.at[field])
        copy(ref.at[0, pl.ds(rows - REACH, REACH)], before.at[2 + field])
        copy(border.at[field, 0], after.at[field, pl.ds(reach2, reach2), middle])
        copy(border.at[field, 1], after.at[2 + field, pl.ds(0, reach2), middle])
    copy(courant.at[pl.ds(0, reach2)], scale.at[pl.ds(0, reach2)])
    copy(courant.at[pl.ds(rows - reach2, reach2)], scale.at[pl.ds(reach2, reach2)])
    for one in copies:
        one.start()

    for field in range(2):
        for row in range(REACH):
            for end in range(2):
                after[2 * end + field, 3 * REACH * end + row] = jnp.zeros((size_y + 2 * PAD, size_z), F32)
        for row in range(reach2):
            low = side[row, field * REACH : (field + 1) * REACH, :]
            fill_sides(now, REACH + row, low, field, size_y, gy)
            high = side[rows - reach2 + row, field * REACH : (field + 1) * REACH, :]
            fill_sides(now, row, high, 2 + field, size_y, gy)
            for end in range(2):
                blank_sides(after, REACH + row, 2 * end + field, size_y)
    side_out[...] = side_in[...]
    for one in copies:
        one.wait()
    masks = z_weights(size_z)

    def first(row, carry):
        for field in range(2):
            for end in range(2):
                group = 2 * end + field
                to = REACH * (1 + end) + row
                first_step(
                    now, REACH + row, before, row, scale, (2 * end + end) * REACH + row,
                    after, to, group, masks,
                )
                side_out[field, pl.ds(end * (rows - REACH) + row, 1), :] = side_term(
                    after, to, group, size_y, gy
                )
        return carry

    lax.fori_loop(0, REACH, first, 0)
    kept_lines = pl.ds(PAD, lines, stride=KEEP_EVERY)
    for field in range(2):
        for row in range(REACH):
            down[field, row] = after[field, REACH + row, kept_lines, :]
            up[field, row] = after[2 + field, reach2 + row, kept_lines, :]

    def second(row, carry):
        for field in range(2):
            for end in range(2):
                group = 2 * end + field

                def store(value):
                    partial[field, end, row] = value

                second_step(
                    now, (1 - end) * REACH + row, scale, end * reach2 + row, after, REACH + row, group, masks, store
                )
        return carry

    lax.fori_loop(0, reach2, second, 0)


def outer(source, receiver, source_before, receiver_before, courant, border, left, right, side, side_in):
    rows, size_y, size_z = courant.shape
    lines = size_y // KEEP_EVERY
    halo = jax.ShapeDtypeStruct((2, REACH, lines, size_z), F32)
    return pl.pallas_call(
        outer_kernel,
        out_shape=(
            jax.ShapeDtypeStruct((2, 2, 2 * REACH, lines, size_z), F32),
            halo,
            halo,
            jax.ShapeDtypeStruct((2, rows, size_z), F32),
        ),
        in_specs=[HBM] * 8 + [VMEM] * 2,
        out_specs=(VMEM,) * 4,
        scratch_shapes=[
            pltpu.VMEM((4, 3 * REACH, size_y + 2 * PAD, size_z), F32),
            pltpu.VMEM((4, REACH, size_y, size_z), F32),
            pltpu.VMEM((4 * REACH, size_y, size_z), F32),
            pltpu.VMEM((4, 4 * REACH, size_y + 2 * PAD, size_z), F32),
            pltpu.SemaphoreType.DMA((18,)),
        ],
        compiler_params=params(60),
        cost_estimate=cost(10**6, 2**20),
        name="outer",
    )(source, receiver, source_before, receiver_before, courant, border, left, right, side, side_in)


def pack_row(value, field, row, shot, keep, give):
    first, second = z_halves(value)
    keep[field, row] = jnp.where(shot == 0, first, second)
    give[field, row] = jnp.where(shot == 0, second, first)


def side_lines(side, field, row, gy, lines):
    line = lax.broadcasted_iota(jnp.int32, (lines, side.shape[2]), 0)
    meets = line == jnp.where(gy == 0, lines - 1, 0)
    return jnp.where(meets, side[field, pl.ds(row, 1), :], 0.0)


def middle_kernel(inside, ends, kept_courant, side, keep, give):
    shot, gy = lax.axis_index("shot"), lax.axis_index("gy")
    rows, lines, _ = kept_courant.shape

    def one_row(row, values):
        for field in range(2):
            total = side_lines(side, field, row, gy, lines)
            pack_row(values[field] + kept_courant[row] * total, field, row - REACH, shot, keep, give)

    def middle(row, carry):
        one_row(row, [inside[field, row - 2 * REACH] for field in range(2)])
        return carry

    lax.fori_loop(2 * REACH, rows - 2 * REACH, middle, 0)
    for row in range(REACH, 2 * REACH):
        one_row(row, [ends[field, 0, row] for field in range(2)])
        one_row(rows - 1 - row, [ends[field, 1, 2 * REACH - 1 - row] for field in range(2)])


def finish_middle(inside, ends, kept_courant, side):
    rows, lines, size_z = kept_courant.shape
    half = jax.ShapeDtypeStruct((2, rows - 2 * REACH, lines // 2, size_z), F32)
    return pl.pallas_call(
        middle_kernel,
        out_shape=(half, half),
        in_specs=[VMEM] * 4,
        out_specs=(VMEM,) * 2,
        compiler_params=params(24),
        cost_estimate=cost(10**10, 3 * 2**20),
        name="finish_middle",
    )(inside, ends, kept_courant, side)


def ends_kernel(ends, kept_courant, left, right, side, keep, give):
    shot, gy = lax.axis_index("shot"), lax.axis_index("gy")
    rows, lines, _ = kept_courant.shape
    for field in range(2):
        for row in range(REACH):
            below = above = None
            for d in range(row + 1, REACH + 1):
                term = WEIGHTS[d] * left[field, REACH + row - d]
                below = term if below is None else below + term
                term = WEIGHTS[d] * right[field, d - 1 - row]
                above = term if above is None else above + term
            far = rows - 1 - row
            below = below + side_lines(side, field, row, gy, lines)
            above = above + side_lines(side, field, far, gy, lines)
            pack_row(ends[field, 0, row] + kept_courant[row] * below, field, row, shot, keep, give)
            pack_row(
                ends[field, 1, 2 * REACH - 1 - row] + kept_courant[far] * above,
                field, 2 * REACH - 1 - row, shot, keep, give,
            )


def finish_ends(ends, kept_courant, left, right, side):
    _, lines, size_z = kept_courant.shape
    half = jax.ShapeDtypeStruct((2, 2 * REACH, lines // 2, size_z), F32)
    return pl.pallas_call(
        ends_kernel,
        out_shape=(half, half),
        in_specs=[VMEM] * 5,
        out_specs=(VMEM,) * 2,
        compiler_params=params(24),
        cost_estimate=cost(10**10, 3 * 2**20),
        name="finish_ends",
    )(ends, kept_courant, left, right, side)


def block_starts(rows):
    even = lax.axis_index("gx") % 2 == 0
    return HALF, jnp.where(even, HALF + rows, 0), jnp.where(even, 0, HALF + rows)


def products(rows_of, sample, shift, here):
    total = None
    for group in range(rows_of.shape[0]):
        term = (
            rows_of[group, 0, 2 * HALF + sample - shift, here, :]
            * rows_of[group, 1, sample + shift, here, :]
        )
        total = term if total is None else total + term
    return total


def first_image_kernel(*refs):
    blocks, (out, rows_of, sems) = refs[:6], refs[6:]
    rows = blocks[0].shape[1]

    @pl.when(pl.program_id(0) == 0)
    def _():
        starts = block_starts(rows)
        copies = []
        for index, ref in enumerate(blocks):
            dst = rows_of.at[index // 3, :, pl.ds(starts[index % 3], rows)]
            copies.append(pltpu.make_async_copy(ref, dst, sems.at[index]))
        run_copies(copies)

    sample = 4 * pl.program_id(0)
    for chunk in range(rows_of.shape[3] // 8):
        here = pl.ds(8 * chunk, 8)
        for shift in range(OFFSETS):
            out[0, shift, here, :] = products(rows_of, sample, shift, here)


def first_image(blocks):
    _, rows, lines, size_z = blocks[0].shape
    samples = rows // 4
    return pl.pallas_call(
        first_image_kernel,
        grid=(samples,),
        out_shape=jax.ShapeDtypeStruct((samples, OFFSETS, lines, size_z), F32),
        in_specs=[ANY] * len(blocks),
        out_specs=pl.BlockSpec((1, OFFSETS, lines, size_z), lambda i: (i, 0, 0, 0)),
        scratch_shapes=[
            pltpu.VMEM((2, 2, rows + 2 * HALF, lines, size_z), F32),
            pltpu.SemaphoreType.DMA((6,)),
        ],
        compiler_params=params(16),
        cost_estimate=cost(10**10, 8 * 2**20),
        name="first_image",
    )(*blocks)


def image_kernel(token, first, *refs):
    blocks, (out, rows_of, turned, sems) = refs[:9], refs[9:]
    rows = blocks[0].shape[1] + 2 * REACH

    @pl.when(pl.program_id(0) == 0)
    def _():
        starts = block_starts(rows)
        copies = []

        def copy(src, group, start, count):
            dst = rows_of.at[group, :, pl.ds(start, count)]
            copies.append(pltpu.make_async_copy(src, dst, sems.at[len(copies)]))

        for part in range(2):
            for kind in range(3):
                copy(blocks[3 * part + kind], part, starts[kind] + REACH, rows - 2 * REACH)
            for kind, start in enumerate((HALF, 0, HALF + rows)):
                ends = blocks[6 + kind]
                copy(ends.at[part, :, pl.ds(0, REACH)], part, start, REACH)
                copy(ends.at[part, :, pl.ds(REACH, REACH)], part, start + rows - REACH, REACH)
        run_copies(copies)

    lines, size_z = rows_of.shape[3], rows_of.shape[4]
    sample = 4 * pl.program_id(0)
    for chunk in range(lines // 8):
        here = pl.ds(8 * chunk, 8)
        for shift in range(OFFSETS):
            total = first[0, shift, here, :] + products(rows_of, sample, shift, here)
            turned[chunk, pl.ds(shift, 8, stride=OFFSET_ROWS), :] = total
        for line in range(8):
            values = turned[chunk, line * OFFSET_ROWS : (line + 1) * OFFSET_ROWS, :].T
            at = 8 * chunk + line
            out[0, at] = values[: size_z // 2, :OFFSETS]
            out[0, lines + at] = values[size_z // 2 :, :OFFSETS]


def image(token, first, blocks):
    samples, _, lines, size_z = first.shape
    rows = 4 * samples
    return pl.pallas_call(
        image_kernel,
        grid=(samples,),
        out_shape=jax.ShapeDtypeStruct((samples, 2 * lines, size_z // 2, OFFSETS), F32),
        in_specs=[SMEM, pl.BlockSpec((1, OFFSETS, lines, size_z), lambda i: (i, 0, 0, 0))] + [ANY] * len(blocks),
        out_specs=pl.BlockSpec((1, 2 * lines, size_z // 2, OFFSETS), lambda i: (i, 0, 0, 0)),
        scratch_shapes=[
            pltpu.VMEM((2, 2, rows + 2 * HALF, lines, size_z), F32),
            pltpu.VMEM((lines // 8, 8 * OFFSET_ROWS, size_z), F32),
            pltpu.SemaphoreType.DMA((18,)),
        ],
        compiler_params=params(20),
        cost_estimate=cost(10**10, 16 * 2**20),
        name="image",
    )(token, first, *blocks)


def in_order_kernel(*refs):
    refs[-1][0] = 0


def in_order(*arrays):
    return pl.pallas_call(
        in_order_kernel,
        out_shape=jax.ShapeDtypeStruct((1,), jnp.int32),
        in_specs=[ANY] * len(arrays),
        out_specs=SMEM,
        compiler_params=params(1),
        cost_estimate=cost(1, 1),
        name="in_order",
    )(*arrays)


def on_device(source_now, source_before, receiver_now, receiver_before, courant):
    size = lax.axis_size("gx")
    up_pairs = [(i, i + 1) for i in range(size - 1)]
    down_pairs = [(j, i) for i, j in up_pairs]
    partner = [(i, i ^ 1) for i in range(size)]
    onward = [(i, i + 2) for i in range(0, size - 2, 2)] + [(i, i - 2) for i in range(3, size, 2)]
    both = [(0, 1), (1, 0)]

    def exchange(array, axis, pairs):
        return lax.ppermute(array, axis, pairs)

    barrier = lax.optimization_barrier
    up, down, keep, give, side = pack(source_now, receiver_now)
    left = exchange(up, "gx", up_pairs)
    right = exchange(down, "gx", down_pairs)
    side = exchange(side, "gy", both)
    other = exchange(give, "shot", both)
    side, keep, other = barrier((side, keep, other))
    near_keep = exchange(keep, "gx", partner)
    near_other = exchange(other, "gx", partner)
    blocks = [keep, near_keep, None, other, near_other, None]
    inside, kept_courant, side_in, border = inner(
        source_now, receiver_now, source_before, receiver_before, courant, side
    )
    ends, up, down, side = outer(
        source_now, receiver_now, source_before, receiver_before, courant, border, left, right, side, side_in
    )
    left = exchange(up, "gx", up_pairs)
    right = exchange(down, "gx", down_pairs)
    side = exchange(side, "gy", both)
    side, near_keep = barrier((side, near_keep))
    far_keep = exchange(near_keep, "gx", onward)

    keep, give = finish_middle(inside, ends, kept_courant, side)
    keep, give, near_other = barrier((keep, give, near_other))
    blocks[5] = exchange(near_other, "gx", onward)
    other = exchange(give, "shot", both)
    near_keep = exchange(keep, "gx", partner)

    left, right, blocks[2] = barrier((left, right, far_keep))
    keep_ends, give_ends = finish_ends(ends, kept_courant, left, right, side)
    other, keep_ends, give_ends = barrier((other, keep_ends, give_ends))
    near_other = exchange(other, "gx", partner)
    other_ends = exchange(give_ends, "shot", both)
    other_ends, near_keep = barrier((other_ends, near_keep))
    own = jnp.stack([keep_ends, other_ends])
    left = exchange(own, "gx", up_pairs)
    right = exchange(own, "gx", down_pairs)
    far_keep = exchange(near_keep, "gx", onward)
    far_other = exchange(near_other, "gx", onward)
    first = first_image(blocks)
    token = in_order(first, left, right, far_keep)
    blocks = [keep, near_keep, far_keep, other, near_other, far_other, own, left, right]
    return jnp.transpose(image(token, first, blocks), (3, 0, 1, 2))


def solution(mesh):
    in_specs = (
        P("shot", "gx", "gy", None),
        P("shot", "gx", "gy", None),
        P("shot", "gx", "gy", None),
        P("shot", "gx", "gy", None),
        P("gx", "gy", None),
    )
    out_specs = P(None, "gx", "gy", "shot")
    return jax.shard_map(
        on_device, mesh=mesh, in_specs=in_specs, out_specs=out_specs, check_vma=False
    )
```

```python
import functools

import jax
import jax.numpy as jnp
from jax import lax
from jax.experimental import pallas as pl
from jax.experimental.pallas import tpu as pltpu
from jax.sharding import PartitionSpec as P

HALF = 32
REACH = 4
KEEP_EVERY = 4
OFFSETS = 2 * HALF + 1
OFFSET_ROWS = 72
LINES = 32
STEPS_MIB = 40
WEIGHTS = (-205.0 / 72.0, 8.0 / 5.0, -1.0 / 5.0, 8.0 / 315.0, -1.0 / 560.0)
PAD = 8
F32 = jnp.float32
HBM = pl.BlockSpec(memory_space=pltpu.HBM)
ANY = pl.BlockSpec(memory_space=pl.ANY)
VMEM = pl.BlockSpec(memory_space=pltpu.VMEM)
SMEM = pl.BlockSpec(memory_space=pltpu.SMEM)


def params(mib):
    return pltpu.CompilerParams(vmem_limit_bytes=mib * 2**20)


def cost(flops, nbytes):
    return pl.CostEstimate(flops=flops, bytes_accessed=nbytes, transcendentals=0)


def run_copies(copies):
    for copy in copies:
        copy.start()
    for copy in copies:
        copy.wait()


def z_halves(lines):
    count, size_z = lines.shape
    top, bottom = lines[: count // 2], lines[count // 2 :]
    low = lax.broadcasted_iota(jnp.int32, top.shape, 1) < size_z // 2
    first = jnp.where(low, top, pltpu.roll(bottom, size_z // 2, 1))
    second = jnp.where(low, pltpu.roll(top, size_z // 2, 1), bottom)
    return first, second


def pack_kernel(source, receiver, up, down, keep, give, side):
    shot, gy = lax.axis_index("shot"), lax.axis_index("gy")
    rows, size_y, size_z = source.shape[1:]
    lines = size_y // KEEP_EVERY
    step, steps = pl.program_id(0), pl.num_programs(0)

    @pl.when(step == 0)
    def _():
        for field, ref in enumerate((source, receiver)):
            down[field] = ref[0, :REACH]

    @pl.when(step == steps - 1)
    def _():
        for field, ref in enumerate((source, receiver)):
            up[field] = ref[0, rows - REACH :]

    for row in range(rows):
        parts = []
        for field, ref in enumerate((source, receiver)):
            first, second = z_halves(ref[0, row, pl.ds(0, lines, stride=KEEP_EVERY), :])
            keep[field, row] = jnp.where(shot == 0, first, second)
            give[field, row] = jnp.where(shot == 0, second, first)
            low = ref[0, row, 0:REACH, :]
            high = ref[0, row, size_y - REACH : size_y, :]
            parts.append(jnp.where(gy == 0, high, low))
        side[row] = jnp.concatenate(parts, axis=0)


def pack(source, receiver):
    _, rows, size_y, size_z = source.shape
    lines = size_y // KEEP_EVERY // 2
    step = 8
    edge = jax.ShapeDtypeStruct((2, REACH, size_y, size_z), F32)
    half = jax.ShapeDtypeStruct((2, rows, lines, size_z), F32)
    edge_spec = pl.BlockSpec((2, REACH, size_y, size_z), lambda i: (0, 0, 0, 0))
    half_spec = pl.BlockSpec((2, step, lines, size_z), lambda i: (0, i, 0, 0))
    field_spec = pl.BlockSpec((1, step, size_y, size_z), lambda i: (0, i, 0, 0))
    return pl.pallas_call(
        pack_kernel,
        grid=(rows // step,),
        out_shape=(edge, edge, half, half, jax.ShapeDtypeStruct((rows, 2 * REACH, size_z), F32)),
        in_specs=[field_spec, field_spec],
        out_specs=(
            edge_spec,
            edge_spec,
            half_spec,
            half_spec,
            pl.BlockSpec((step, 2 * REACH, size_z), lambda i: (i, 0, 0)),
        ),
        cost_estimate=cost(10**10, 7 * 2**20),
        name="pack",
    )(source, receiver)


def z_weights(size_z):
    z = lax.broadcasted_iota(jnp.int32, (8, size_z), 1)
    return [
        (jnp.where(z >= d, WEIGHTS[d], 0.0), jnp.where(z < size_z - d, WEIGHTS[d], 0.0))
        for d in range(1, REACH + 1)
    ]


def z_terms(center, masks):
    size_z = center.shape[1]
    center = center.reshape(-1, 8, size_z)
    total = None
    for d, (below, above) in enumerate(masks, start=1):
        term = below * pltpu.roll(center, d, 2) + above * pltpu.roll(center, size_z - d, 2)
        total = term if total is None else total + term
    return total.reshape(-1, size_z)


def first_step(now, row, before, before_row, scale, scale_row, after, after_row, field, masks):
    size_y = before.shape[2]
    for chunk in range(size_y // LINES):
        at = PAD + LINES * chunk
        center = now[field, row, at : at + LINES, :]
        total = (3.0 * WEIGHTS[0]) * center + z_terms(center, masks)
        for d in range(1, REACH + 1):
            around = (
                now[field, row + d, at : at + LINES, :]
                + now[field, row - d, at : at + LINES, :]
                + now[field, row, at + d : at + d + LINES, :]
                + now[field, row, at - d : at - d + LINES, :]
            )
            total = total + WEIGHTS[d] * around
        here = pl.ds(LINES * chunk, LINES)
        after[field, after_row, at : at + LINES, :] = (
            2.0 * center - before[field, before_row, here, :] + scale[scale_row, here, :] * total
        )


def second_step(now, row, scale, scale_row, after, after_row, field, masks, store):
    size_y = scale.shape[1]
    lines = size_y // KEEP_EVERY
    kept = lambda start: pl.ds(start, lines, stride=KEEP_EVERY)
    center = after[field, after_row, kept(PAD), :]
    total = (3.0 * WEIGHTS[0]) * center + z_terms(center, masks)
    for d in range(1, REACH + 1):
        around = (
            after[field, after_row + d, kept(PAD), :]
            + after[field, after_row - d, kept(PAD), :]
            + after[field, after_row, kept(PAD + d), :]
            + after[field, after_row, kept(PAD - d), :]
        )
        total = total + WEIGHTS[d] * around
    store(2.0 * center - now[field, row, kept(PAD), :] + scale[scale_row, kept(0), :] * total)


def side_term(after, after_row, field, size_y, gy):
    lowest = WEIGHTS[REACH] * after[field, after_row, PAD : PAD + 1, :]
    highest = sum(
        WEIGHTS[d] * after[field, after_row, PAD + size_y - d : PAD + size_y - d + 1, :]
        for d in range(1, REACH + 1)
    )
    return jnp.where(gy == 0, highest, lowest)


def fill_sides(now, row, got, field, size_y, gy):
    blank = jnp.zeros_like(got)
    now[field, row, PAD - REACH : PAD, :] = jnp.where(gy == 0, blank, got)
    now[field, row, size_y + PAD : size_y + PAD + REACH, :] = jnp.where(gy == 0, got, blank)


def blank_sides(after, row, field, size_y):
    blank = jnp.zeros((REACH, after.shape[3]), F32)
    after[field, row, PAD - REACH : PAD, :] = blank
    after[field, row, size_y + PAD : size_y + PAD + REACH, :] = blank


def steps_kernel(
    source, receiver, source_before, receiver_before, courant, side,
    partial, kept_courant, edge_courant, edge, side_out, now, before, scale, after, sems,
):
    gy = lax.axis_index("gy")
    rows, size_y, size_z = courant.shape
    lines = size_y // KEEP_EVERY
    piece = 2 * REACH
    middle = pl.ds(PAD, size_y)

    def copies(index):
        part = pl.ds(piece * index, piece)
        found = []
        for field in range(2):
            src = (source, receiver)[field].at[0, part]
            dst = now.at[field, pl.ds(REACH + piece * index, piece), middle]
            found.append(pltpu.make_async_copy(src, dst, sems.at[index, field]))
        for field in range(2):
            src = (source_before, receiver_before)[field].at[0, part]
            found.append(pltpu.make_async_copy(src, before.at[field, part], sems.at[index, 2 + field]))
        found.append(pltpu.make_async_copy(courant.at[part], scale.at[part], sems.at[index, 4]))
        return found

    for index in range(rows // piece):
        for one in copies(index):
            one.start()

    for field in range(2):
        for row in list(range(REACH)) + list(range(rows + REACH, rows + 2 * REACH)):
            now[field, row] = jnp.zeros((size_y + 2 * PAD, size_z), F32)
            after[field, row] = jnp.zeros((size_y + 2 * PAD, size_z), F32)

    def fill(row, carry):
        for field in range(2):
            got = side[row, field * REACH : (field + 1) * REACH, :]
            fill_sides(now, row + REACH, got, field, size_y, gy)
            blank_sides(after, row + REACH, field, size_y)
        return carry

    lax.fori_loop(0, rows, fill, 0)
    masks = z_weights(size_z)
    for one in copies(0)[:2]:
        one.wait()

    def first(row, carry):
        @pl.when(row % piece == 0)
        def _():
            index = row // piece
            for one in copies(index)[2:]:
                one.wait()

            @pl.when(index + 1 < rows // piece)
            def _():
                for one in copies(index + 1)[:2]:
                    one.wait()

        at = row + REACH
        for field in range(2):
            first_step(now, at, before, row, scale, row, after, at, field, masks)
            side_out[field, pl.ds(row, 1), :] = side_term(after, at, field, size_y, gy)
        return carry

    lax.fori_loop(0, rows, first, 0)

    def second(row, carry):
        at = row + REACH
        kept_courant[row] = scale[row, pl.ds(0, lines, stride=KEEP_EVERY), :]
        for field in range(2):
            def store(value):
                partial[field, row] = value

            second_step(now, at, scale, row, after, at, field, masks, store)
        return carry

    lax.fori_loop(0, rows, second, 0)
    for end in range(2):
        for row in range(REACH):
            at = rows - 1 - row if end else row
            edge_courant[end, row] = scale[at]
            for field in range(2):
                edge[field, end, row] = after[field, REACH + at, pl.ds(PAD, lines, stride=KEEP_EVERY), :]


def steps(source, receiver, source_before, receiver_before, courant, side):
    rows, size_y, size_z = courant.shape
    lines = size_y // KEEP_EVERY
    return pl.pallas_call(
        steps_kernel,
        out_shape=(
            jax.ShapeDtypeStruct((2, rows, lines, size_z), F32),
            jax.ShapeDtypeStruct((rows, lines, size_z), F32),
            jax.ShapeDtypeStruct((2, REACH, size_y, size_z), F32),
            jax.ShapeDtypeStruct((2, 2, REACH, lines, size_z), F32),
            jax.ShapeDtypeStruct((2, rows, size_z), F32),
        ),
        in_specs=[HBM] * 5 + [VMEM],
        out_specs=(VMEM,) * 5,
        scratch_shapes=[
            pltpu.VMEM((2, rows + 2 * REACH, size_y + 2 * PAD, size_z), F32),
            pltpu.VMEM((2, rows, size_y, size_z), F32),
            pltpu.VMEM((rows, size_y, size_z), F32),
            pltpu.VMEM((2, rows + 2 * REACH, size_y + 2 * PAD, size_z), F32),
            pltpu.SemaphoreType.DMA((rows // (2 * REACH), 5)),
        ],
        compiler_params=params(STEPS_MIB),
        cost_estimate=cost(2 * 10**10, 2**20),
        name="steps",
    )(source, receiver, source_before, receiver_before, courant, side)


def mend_kernel(
    left, right, partial, kept_courant, edge_courant, edge, side_in,
    ends, up, down, side_out, added,
):
    gy = lax.axis_index("gy")
    rows, lines, size_z = kept_courant.shape
    size_y = KEEP_EVERY * lines
    masks = z_weights(size_z)
    kept = lambda start: pl.ds(start, lines, stride=KEEP_EVERY)
    side_out[...] = side_in[...]
    for end in range(2):
        for field in range(2):
            group = 2 * end + field
            for row in range(REACH):
                blank_sides(added, row, group, size_y)
                for chunk in range(size_y // LINES):
                    here = pl.ds(LINES * chunk, LINES)
                    total = None
                    for d in range(row + 1, REACH + 1):
                        beyond = d - row - 1
                        halo = right[field, beyond, here, :] if end else left[field, REACH - 1 - beyond, here, :]
                        term = WEIGHTS[d] * halo
                        total = term if total is None else total + term
                    added[group, row, pl.ds(PAD + LINES * chunk, LINES), :] = edge_courant[end, row, here, :] * total
            for row in range(2 * REACH):
                at = rows - 1 - row if end else row
                total = None
                for other in range(REACH):
                    if 0 < abs(row - other) <= REACH:
                        term = WEIGHTS[abs(row - other)] * added[group, other, kept(PAD), :]
                        total = term if total is None else total + term
                value = partial[field, at]
                if row < REACH:
                    center = added[group, row, kept(PAD), :]
                    total = total + (3.0 * WEIGHTS[0]) * center + z_terms(center, masks)
                    for d in range(1, REACH + 1):
                        around = added[group, row, kept(PAD + d), :] + added[group, row, kept(PAD - d), :]
                        total = total + WEIGHTS[d] * around
                    value = value + 2.0 * center
                    first = edge[field, end, row] + center
                    if end:
                        up[field, REACH - 1 - row] = first
                    else:
                        down[field, row] = first
                    side_out[field, at : at + 1, :] = side_in[field, at : at + 1, :] + side_term(
                        added, row, group, size_y, gy
                    )
                ends[field, end, row] = value + kept_courant[at] * total


def mend(left, right, partial, kept_courant, edge_courant, edge, side_in):
    rows, lines, size_z = kept_courant.shape
    halo = jax.ShapeDtypeStruct((2, REACH, lines, size_z), F32)
    return pl.pallas_call(
        mend_kernel,
        out_shape=(
            jax.ShapeDtypeStruct((2, 2, 2 * REACH, lines, size_z), F32),
            halo,
            halo,
            jax.ShapeDtypeStruct((2, rows, size_z), F32),
        ),
        in_specs=[VMEM] * 7,
        out_specs=(VMEM,) * 4,
        scratch_shapes=[pltpu.VMEM((4, REACH, KEEP_EVERY * lines + 2 * PAD, size_z), F32)],
        compiler_params=params(24),
        cost_estimate=cost(10**6, 2**20),
        name="mend",
    )(left, right, partial, kept_courant, edge_courant, edge, side_in)


def pack_row(value, field, row, shot, keep, give):
    first, second = z_halves(value)
    keep[field, row] = jnp.where(shot == 0, first, second)
    give[field, row] = jnp.where(shot == 0, second, first)


def side_lines(side, field, row, gy, lines):
    line = lax.broadcasted_iota(jnp.int32, (lines, side.shape[2]), 0)
    meets = line == jnp.where(gy == 0, lines - 1, 0)
    return jnp.where(meets, side[field, pl.ds(row, 1), :], 0.0)


def middle_kernel(partial, ends, kept_courant, side, keep, give):
    shot, gy = lax.axis_index("shot"), lax.axis_index("gy")
    rows, lines, _ = kept_courant.shape

    def one_row(row, values):
        for field in range(2):
            total = side_lines(side, field, row, gy, lines)
            pack_row(values[field] + kept_courant[row] * total, field, row - REACH, shot, keep, give)

    def middle(row, carry):
        one_row(row, [partial[field, row] for field in range(2)])
        return carry

    lax.fori_loop(2 * REACH, rows - 2 * REACH, middle, 0)
    for row in range(REACH, 2 * REACH):
        one_row(row, [ends[field, 0, row] for field in range(2)])
        one_row(rows - 1 - row, [ends[field, 1, row] for field in range(2)])


def finish_middle(partial, ends, kept_courant, side):
    rows, lines, size_z = kept_courant.shape
    half = jax.ShapeDtypeStruct((2, rows - 2 * REACH, lines // 2, size_z), F32)
    return pl.pallas_call(
        middle_kernel,
        out_shape=(half, half),
        in_specs=[VMEM] * 4,
        out_specs=(VMEM,) * 2,
        compiler_params=params(24),
        cost_estimate=cost(10**10, 3 * 2**20),
        name="finish_middle",
    )(partial, ends, kept_courant, side)


def ends_kernel(ends, kept_courant, left, right, side, keep, give):
    shot, gy = lax.axis_index("shot"), lax.axis_index("gy")
    rows, lines, _ = kept_courant.shape
    for field in range(2):
        for row in range(REACH):
            below = above = None
            for d in range(row + 1, REACH + 1):
                term = WEIGHTS[d] * left[field, REACH + row - d]
                below = term if below is None else below + term
                term = WEIGHTS[d] * right[field, d - 1 - row]
                above = term if above is None else above + term
            far = rows - 1 - row
            below = below + side_lines(side, field, row, gy, lines)
            above = above + side_lines(side, field, far, gy, lines)
            pack_row(ends[field, 0, row] + kept_courant[row] * below, field, row, shot, keep, give)
            pack_row(
                ends[field, 1, row] + kept_courant[far] * above,
                field, 2 * REACH - 1 - row, shot, keep, give,
            )


def finish_ends(ends, kept_courant, left, right, side):
    _, lines, size_z = kept_courant.shape
    half = jax.ShapeDtypeStruct((2, 2 * REACH, lines // 2, size_z), F32)
    return pl.pallas_call(
        ends_kernel,
        out_shape=(half, half),
        in_specs=[VMEM] * 5,
        out_specs=(VMEM,) * 2,
        compiler_params=params(24),
        cost_estimate=cost(10**10, 3 * 2**20),
        name="finish_ends",
    )(ends, kept_courant, left, right, side)


def block_starts(rows):
    even = lax.axis_index("gx") % 2 == 0
    return HALF, jnp.where(even, HALF + rows, 0), jnp.where(even, 0, HALF + rows)


def products(rows_of, sample, shift, here):
    total = None
    for group in range(rows_of.shape[0]):
        term = (
            rows_of[group, 0, 2 * HALF + sample - shift, here, :]
            * rows_of[group, 1, sample + shift, here, :]
        )
        total = term if total is None else total + term
    return total


def first_image_kernel(*refs):
    blocks, (out, rows_of, sems) = refs[:6], refs[6:]
    rows = blocks[0].shape[1]

    @pl.when(pl.program_id(0) == 0)
    def _():
        starts = block_starts(rows)
        copies = []
        for index, ref in enumerate(blocks):
            dst = rows_of.at[index // 3, :, pl.ds(starts[index % 3], rows)]
            copies.append(pltpu.make_async_copy(ref, dst, sems.at[index]))
        run_copies(copies)

    sample = 4 * pl.program_id(0)
    for chunk in range(rows_of.shape[3] // 8):
        here = pl.ds(8 * chunk, 8)
        for shift in range(OFFSETS):
            out[0, shift, here, :] = products(rows_of, sample, shift, here)


def first_image(blocks):
    _, rows, lines, size_z = blocks[0].shape
    samples = rows // 4
    return pl.pallas_call(
        first_image_kernel,
        grid=(samples,),
        out_shape=jax.ShapeDtypeStruct((samples, OFFSETS, lines, size_z), F32),
        in_specs=[ANY] * len(blocks),
        out_specs=pl.BlockSpec((1, OFFSETS, lines, size_z), lambda i: (i, 0, 0, 0)),
        scratch_shapes=[
            pltpu.VMEM((2, 2, rows + 2 * HALF, lines, size_z), F32),
            pltpu.SemaphoreType.DMA((6,)),
        ],
        compiler_params=params(16),
        cost_estimate=cost(10**10, 8 * 2**20),
        name="first_image",
    )(*blocks)


def image_kernel(token, first, *refs):
    blocks, (out, rows_of, turned, sems) = refs[:9], refs[9:]
    rows = blocks[0].shape[1] + 2 * REACH

    @pl.when(pl.program_id(0) == 0)
    def _():
        starts = block_starts(rows)
        copies = []

        def copy(src, group, start, count):
            dst = rows_of.at[group, :, pl.ds(start, count)]
            copies.append(pltpu.make_async_copy(src, dst, sems.at[len(copies)]))

        for part in range(2):
            for kind in range(3):
                copy(blocks[3 * part + kind], part, starts[kind] + REACH, rows - 2 * REACH)
            for kind, start in enumerate((HALF, 0, HALF + rows)):
                ends = blocks[6 + kind]
                copy(ends.at[part, :, pl.ds(0, REACH)], part, start, REACH)
                copy(ends.at[part, :, pl.ds(REACH, REACH)], part, start + rows - REACH, REACH)
        run_copies(copies)

    lines, size_z = rows_of.shape[3], rows_of.shape[4]
    sample = 4 * pl.program_id(0)
    for chunk in range(lines // 8):
        here = pl.ds(8 * chunk, 8)
        for shift in range(OFFSETS):
            total = first[0, shift, here, :] + products(rows_of, sample, shift, here)
            turned[chunk, pl.ds(shift, 8, stride=OFFSET_ROWS), :] = total
        for line in range(8):
            values = turned[chunk, line * OFFSET_ROWS : (line + 1) * OFFSET_ROWS, :].T
            at = 8 * chunk + line
            out[0, at] = values[: size_z // 2, :OFFSETS]
            out[0, lines + at] = values[size_z // 2 :, :OFFSETS]


def image(token, first, blocks):
    samples, _, lines, size_z = first.shape
    rows = 4 * samples
    return pl.pallas_call(
        image_kernel,
        grid=(samples,),
        out_shape=jax.ShapeDtypeStruct((samples, 2 * lines, size_z // 2, OFFSETS), F32),
        in_specs=[SMEM, pl.BlockSpec((1, OFFSETS, lines, size_z), lambda i: (i, 0, 0, 0))] + [ANY] * len(blocks),
        out_specs=pl.BlockSpec((1, 2 * lines, size_z // 2, OFFSETS), lambda i: (i, 0, 0, 0)),
        scratch_shapes=[
            pltpu.VMEM((2, 2, rows + 2 * HALF, lines, size_z), F32),
            pltpu.VMEM((lines // 8, 8 * OFFSET_ROWS, size_z), F32),
            pltpu.SemaphoreType.DMA((18,)),
        ],
        compiler_params=params(20),
        cost_estimate=cost(10**10, 16 * 2**20),
        name="image",
    )(token, first, *blocks)


def in_order_kernel(*refs):
    refs[-1][0] = 0


def in_order(*arrays):
    return pl.pallas_call(
        in_order_kernel,
        out_shape=jax.ShapeDtypeStruct((1,), jnp.int32),
        in_specs=[ANY] * len(arrays),
        out_specs=SMEM,
        compiler_params=params(1),
        cost_estimate=cost(1, 1),
        name="in_order",
    )(*arrays)


def on_device(source_now, source_before, receiver_now, receiver_before, courant):
    size = lax.axis_size("gx")
    up_pairs = [(i, i + 1) for i in range(size - 1)]
    down_pairs = [(j, i) for i, j in up_pairs]
    partner = [(i, i ^ 1) for i in range(size)]
    onward = [(i, i + 2) for i in range(0, size - 2, 2)] + [(i, i - 2) for i in range(3, size, 2)]
    both = [(0, 1), (1, 0)]

    def exchange(array, axis, pairs):
        return lax.ppermute(array, axis, pairs)

    barrier = lax.optimization_barrier
    up, down, keep, give, side = pack(source_now, receiver_now)
    left = exchange(up, "gx", up_pairs)
    right = exchange(down, "gx", down_pairs)
    side = exchange(side, "gy", both)
    other = exchange(give, "shot", both)
    side, keep, other = barrier((side, keep, other))
    near_keep = exchange(keep, "gx", partner)
    near_other = exchange(other, "gx", partner)
    blocks = [keep, near_keep, None, other, near_other, None]
    partial, kept_courant, edge_courant, edge, side = steps(
        source_now, receiver_now, source_before, receiver_before, courant, side
    )
    ends, up, down, side = mend(left, right, partial, kept_courant, edge_courant, edge, side)
    left = exchange(up, "gx", up_pairs)
    right = exchange(down, "gx", down_pairs)
    side = exchange(side, "gy", both)
    side, near_keep = barrier((side, near_keep))
    far_keep = exchange(near_keep, "gx", onward)

    keep, give = finish_middle(partial, ends, kept_courant, side)
    keep, give, near_other = barrier((keep, give, near_other))
    blocks[5] = exchange(near_other, "gx", onward)
    other = exchange(give, "shot", both)
    near_keep = exchange(keep, "gx", partner)

    left, right, blocks[2] = barrier((left, right, far_keep))
    keep_ends, give_ends = finish_ends(ends, kept_courant, left, right, side)
    other, keep_ends, give_ends = barrier((other, keep_ends, give_ends))
    near_other = exchange(other, "gx", partner)
    other_ends = exchange(give_ends, "shot", both)
    other_ends, near_keep = barrier((other_ends, near_keep))
    own = jnp.stack([keep_ends, other_ends])
    left = exchange(own, "gx", up_pairs)
    right = exchange(own, "gx", down_pairs)
    far_keep = exchange(near_keep, "gx", onward)
    far_other = exchange(near_other, "gx", onward)
    first = first_image(blocks)
    token = in_order(first, left, right, far_keep)
    blocks = [keep, near_keep, far_keep, other, near_other, far_other, own, left, right]
    return jnp.transpose(image(token, first, blocks), (3, 0, 1, 2))


def solution(mesh):
    in_specs = (
        P("shot", "gx", "gy", None),
        P("shot", "gx", "gy", None),
        P("shot", "gx", "gy", None),
        P("shot", "gx", "gy", None),
        P("gx", "gy", None),
    )
    out_specs = P(None, "gx", "gy", "shot")
    return jax.shard_map(
        on_device, mesh=mesh, in_specs=in_specs, out_specs=out_specs, check_vma=False
    )
```

```python
import functools

import jax
import jax.numpy as jnp
from jax import lax
from jax.experimental import pallas as pl
from jax.experimental.pallas import tpu as pltpu
from jax.sharding import PartitionSpec as P

HALF = 32
REACH = 4
KEEP_EVERY = 4
OFFSETS = 2 * HALF + 1
OFFSET_ROWS = 72
LINES = 32
STEPS_MIB = 50
WEIGHTS = (-205.0 / 72.0, 8.0 / 5.0, -1.0 / 5.0, 8.0 / 315.0, -1.0 / 560.0)
PAD = 8
F32 = jnp.float32
HBM = pl.BlockSpec(memory_space=pltpu.HBM)
ANY = pl.BlockSpec(memory_space=pl.ANY)
VMEM = pl.BlockSpec(memory_space=pltpu.VMEM)
SMEM = pl.BlockSpec(memory_space=pltpu.SMEM)


def params(mib):
    return pltpu.CompilerParams(vmem_limit_bytes=mib * 2**20)


def cost(flops, nbytes):
    return pl.CostEstimate(flops=flops, bytes_accessed=nbytes, transcendentals=0)


def run_copies(copies):
    for copy in copies:
        copy.start()
    for copy in copies:
        copy.wait()


def z_halves(lines):
    count, size_z = lines.shape
    top, bottom = lines[: count // 2], lines[count // 2 :]
    low = lax.broadcasted_iota(jnp.int32, top.shape, 1) < size_z // 2
    first = jnp.where(low, top, pltpu.roll(bottom, size_z // 2, 1))
    second = jnp.where(low, pltpu.roll(top, size_z // 2, 1), bottom)
    return first, second


def pack_kernel(source, receiver, up, down, keep, give, side, fields, sems):
    shot, gy = lax.axis_index("shot"), lax.axis_index("gy")
    _, rows, size_y, _ = fields.shape
    lines = size_y // KEEP_EVERY
    pieces = sems.shape[0]
    count = rows // pieces
    order = [0, pieces - 1] + list(range(1, pieces - 1))
    copies = {}
    for index in order:
        part = pl.ds(count * index, count)
        for field, ref in enumerate((source, receiver)):
            copies[index, field] = pltpu.make_async_copy(
                ref.at[0, part], fields.at[field, part], sems.at[index, field]
            )
            copies[index, field].start()

    def one_row(row, carry):
        parts = []
        for field in range(2):
            first, second = z_halves(fields[field, row, pl.ds(0, lines, stride=KEEP_EVERY), :])
            keep[field, row] = jnp.where(shot == 0, first, second)
            give[field, row] = jnp.where(shot == 0, second, first)
            low = fields[field, row, 0:REACH, :]
            high = fields[field, row, size_y - REACH : size_y, :]
            parts.append(jnp.where(gy == 0, high, low))
        side[row] = jnp.concatenate(parts, axis=0)
        return carry

    for index in order:
        for field in range(2):
            copies[index, field].wait()
            if index == 0:
                down[field] = fields[field, :REACH]
            if index == pieces - 1:
                up[field] = fields[field, rows - REACH :]
        lax.fori_loop(count * index, count * (index + 1), one_row, 0, unroll=4)


def pack(source, receiver):
    _, rows, size_y, size_z = source.shape
    lines = size_y // KEEP_EVERY // 2
    edge = jax.ShapeDtypeStruct((2, REACH, size_y, size_z), F32)
    half = jax.ShapeDtypeStruct((2, rows, lines, size_z), F32)
    return pl.pallas_call(
        pack_kernel,
        out_shape=(edge, edge, half, half, jax.ShapeDtypeStruct((rows, 2 * REACH, size_z), F32)),
        in_specs=[HBM, HBM],
        out_specs=(VMEM,) * 5,
        scratch_shapes=[
            pltpu.VMEM((2, rows, size_y, size_z), F32),
            pltpu.SemaphoreType.DMA((4, 2)),
        ],
        compiler_params=params(48),
        cost_estimate=cost(10**10, 7 * 2**20),
        name="pack",
    )(source, receiver)


def z_weights(size_z):
    z = lax.broadcasted_iota(jnp.int32, (8, size_z), 1)
    return [
        (jnp.where(z >= d, WEIGHTS[d], 0.0), jnp.where(z < size_z - d, WEIGHTS[d], 0.0))
        for d in range(1, REACH + 1)
    ]


def z_terms(center, masks):
    size_z = center.shape[1]
    center = center.reshape(-1, 8, size_z)
    total = None
    for d, (below, above) in enumerate(masks, start=1):
        term = below * pltpu.roll(center, d, 2) + above * pltpu.roll(center, size_z - d, 2)
        total = term if total is None else total + term
    return total.reshape(-1, size_z)


def first_step(now, row, before, before_row, scale, scale_row, after, after_row, field, masks):
    size_y = before.shape[2]
    for chunk in range(size_y // LINES):
        at = PAD + LINES * chunk
        center = now[field, row, at : at + LINES, :]
        total = (3.0 * WEIGHTS[0]) * center + z_terms(center, masks)
        for d in range(1, REACH + 1):
            around = (
                now[field, row + d, at : at + LINES, :]
                + now[field, row - d, at : at + LINES, :]
                + now[field, row, at + d : at + d + LINES, :]
                + now[field, row, at - d : at - d + LINES, :]
            )
            total = total + WEIGHTS[d] * around
        here = pl.ds(LINES * chunk, LINES)
        after[field, after_row, at : at + LINES, :] = (
            2.0 * center - before[field, before_row, here, :] + scale[scale_row, here, :] * total
        )


def second_step(now, row, scale, scale_row, after, after_row, field, masks, store):
    size_y = scale.shape[1]
    lines = size_y // KEEP_EVERY
    kept = lambda start: pl.ds(start, lines, stride=KEEP_EVERY)
    center = after[field, after_row, kept(PAD), :]
    total = (3.0 * WEIGHTS[0]) * center + z_terms(center, masks)
    for d in range(1, REACH + 1):
        around = (
            after[field, after_row + d, kept(PAD), :]
            + after[field, after_row - d, kept(PAD), :]
            + after[field, after_row, kept(PAD + d), :]
            + after[field, after_row, kept(PAD - d), :]
        )
        total = total + WEIGHTS[d] * around
    store(2.0 * center - now[field, row, kept(PAD), :] + scale[scale_row, kept(0), :] * total)


def side_term(after, after_row, field, size_y, gy):
    lowest = WEIGHTS[REACH] * after[field, after_row, PAD : PAD + 1, :]
    highest = sum(
        WEIGHTS[d] * after[field, after_row, PAD + size_y - d : PAD + size_y - d + 1, :]
        for d in range(1, REACH + 1)
    )
    return jnp.where(gy == 0, highest, lowest)


def fill_sides(now, row, got, field, size_y, gy):
    blank = jnp.zeros_like(got)
    now[field, row, PAD - REACH : PAD, :] = jnp.where(gy == 0, blank, got)
    now[field, row, size_y + PAD : size_y + PAD + REACH, :] = jnp.where(gy == 0, got, blank)


def blank_sides(after, row, field, size_y):
    blank = jnp.zeros((REACH, after.shape[3]), F32)
    after[field, row, PAD - REACH : PAD, :] = blank
    after[field, row, size_y + PAD : size_y + PAD + REACH, :] = blank


def steps_kernel(
    source, receiver, source_before, receiver_before, courant, side,
    partial, kept_courant, edge_courant, edge, side_out, now, before, scale, after, sems,
):
    gy = lax.axis_index("gy")
    rows, size_y, size_z = courant.shape
    lines = size_y // KEEP_EVERY
    piece = 2 * REACH
    middle = pl.ds(PAD, size_y)

    def copies(index):
        part = pl.ds(piece * index, piece)
        found = []
        for field in range(2):
            src = (source, receiver)[field].at[0, part]
            dst = now.at[field, pl.ds(REACH + piece * index, piece), middle]
            found.append(pltpu.make_async_copy(src, dst, sems.at[index, field]))
        for field in range(2):
            src = (source_before, receiver_before)[field].at[0, part]
            found.append(pltpu.make_async_copy(src, before.at[field, part], sems.at[index, 2 + field]))
        found.append(pltpu.make_async_copy(courant.at[part], scale.at[part], sems.at[index, 4]))
        return found

    for index in range(rows // piece):
        for one in copies(index):
            one.start()

    for field in range(2):
        for row in list(range(REACH)) + list(range(rows + REACH, rows + 2 * REACH)):
            now[field, row] = jnp.zeros((size_y + 2 * PAD, size_z), F32)
            after[field, row] = jnp.zeros((size_y + 2 * PAD, size_z), F32)

    def fill(row, carry):
        for field in range(2):
            got = side[row, field * REACH : (field + 1) * REACH, :]
            fill_sides(now, row + REACH, got, field, size_y, gy)
            blank_sides(after, row + REACH, field, size_y)
        return carry

    lax.fori_loop(0, rows, fill, 0)
    masks = z_weights(size_z)
    for one in copies(0)[:2]:
        one.wait()

    def first(row, carry):
        @pl.when(row % piece == 0)
        def _():
            index = row // piece
            for one in copies(index)[2:]:
                one.wait()

            @pl.when(index + 1 < rows // piece)
            def _():
                for one in copies(index + 1)[:2]:
                    one.wait()

        at = row + REACH
        for field in range(2):
            first_step(now, at, before, row, scale, row, after, at, field, masks)
            side_out[field, pl.ds(row, 1), :] = side_term(after, at, field, size_y, gy)
        return carry

    lax.fori_loop(0, rows, first, 0)

    def second(row, carry):
        at = row + REACH
        kept_courant[row] = scale[row, pl.ds(0, lines, stride=KEEP_EVERY), :]
        for field in range(2):
            def store(value):
                partial[field, row] = value

            second_step(now, at, scale, row, after, at, field, masks, store)
        return carry

    lax.fori_loop(0, rows, second, 0)
    for end in range(2):
        for row in range(REACH):
            at = rows - 1 - row if end else row
            edge_courant[end, row] = scale[at]
            for field in range(2):
                edge[field, end, row] = after[field, REACH + at, pl.ds(PAD, lines, stride=KEEP_EVERY), :]


def steps(source, receiver, source_before, receiver_before, courant, side):
    rows, size_y, size_z = courant.shape
    lines = size_y // KEEP_EVERY
    return pl.pallas_call(
        steps_kernel,
        out_shape=(
            jax.ShapeDtypeStruct((2, rows, lines, size_z), F32),
            jax.ShapeDtypeStruct((rows, lines, size_z), F32),
            jax.ShapeDtypeStruct((2, REACH, size_y, size_z), F32),
            jax.ShapeDtypeStruct((2, 2, REACH, lines, size_z), F32),
            jax.ShapeDtypeStruct((2, rows, size_z), F32),
        ),
        in_specs=[HBM] * 5 + [VMEM],
        out_specs=(VMEM,) * 5,
        scratch_shapes=[
            pltpu.VMEM((2, rows + 2 * REACH, size_y + 2 * PAD, size_z), F32),
            pltpu.VMEM((2, rows, size_y, size_z), F32),
            pltpu.VMEM((rows, size_y, size_z), F32),
            pltpu.VMEM((2, rows + 2 * REACH, size_y + 2 * PAD, size_z), F32),
            pltpu.SemaphoreType.DMA((rows // (2 * REACH), 5)),
        ],
        compiler_params=params(STEPS_MIB),
        cost_estimate=cost(2 * 10**10, 2**20),
        name="steps",
    )(source, receiver, source_before, receiver_before, courant, side)


def mend_kernel(
    left, right, partial, kept_courant, edge_courant, edge, side_in,
    ends, up, down, side_out, added,
):
    gy = lax.axis_index("gy")
    rows, lines, size_z = kept_courant.shape
    size_y = KEEP_EVERY * lines
    masks = z_weights(size_z)
    kept = lambda start: pl.ds(start, lines, stride=KEEP_EVERY)
    side_out[...] = side_in[...]
    for end in range(2):
        for field in range(2):
            group = 2 * end + field
            for row in range(REACH):
                blank_sides(added, row, group, size_y)
                for chunk in range(size_y // LINES):
                    here = pl.ds(LINES * chunk, LINES)
                    total = None
                    for d in range(row + 1, REACH + 1):
                        beyond = d - row - 1
                        halo = right[field, beyond, here, :] if end else left[field, REACH - 1 - beyond, here, :]
                        term = WEIGHTS[d] * halo
                        total = term if total is None else total + term
                    added[group, row, pl.ds(PAD + LINES * chunk, LINES), :] = edge_courant[end, row, here, :] * total
            for row in range(2 * REACH):
                at = rows - 1 - row if end else row
                total = None
                for other in range(REACH):
                    if 0 < abs(row - other) <= REACH:
                        term = WEIGHTS[abs(row - other)] * added[group, other, kept(PAD), :]
                        total = term if total is None else total + term
                value = partial[field, at]
                if row < REACH:
                    center = added[group, row, kept(PAD), :]
                    total = total + (3.0 * WEIGHTS[0]) * center + z_terms(center, masks)
                    for d in range(1, REACH + 1):
                        around = added[group, row, kept(PAD + d), :] + added[group, row, kept(PAD - d), :]
                        total = total + WEIGHTS[d] * around
                    value = value + 2.0 * center
                    first = edge[field, end, row] + center
                    if end:
                        up[field, REACH - 1 - row] = first
                    else:
                        down[field, row] = first
                    side_out[field, at : at + 1, :] = side_in[field, at : at + 1, :] + side_term(
                        added, row, group, size_y, gy
                    )
                ends[field, end, row] = value + kept_courant[at] * total


def mend(left, right, partial, kept_courant, edge_courant, edge, side_in):
    rows, lines, size_z = kept_courant.shape
    halo = jax.ShapeDtypeStruct((2, REACH, lines, size_z), F32)
    return pl.pallas_call(
        mend_kernel,
        out_shape=(
            jax.ShapeDtypeStruct((2, 2, 2 * REACH, lines, size_z), F32),
            halo,
            halo,
            jax.ShapeDtypeStruct((2, rows, size_z), F32),
        ),
        in_specs=[VMEM] * 7,
        out_specs=(VMEM,) * 4,
        scratch_shapes=[pltpu.VMEM((4, REACH, KEEP_EVERY * lines + 2 * PAD, size_z), F32)],
        compiler_params=params(24),
        cost_estimate=cost(10**6, 2**20),
        name="mend",
    )(left, right, partial, kept_courant, edge_courant, edge, side_in)


def pack_row(value, field, row, shot, keep, give):
    first, second = z_halves(value)
    keep[field, row] = jnp.where(shot == 0, first, second)
    give[field, row] = jnp.where(shot == 0, second, first)


def side_lines(side, field, row, gy, lines):
    line = lax.broadcasted_iota(jnp.int32, (lines, side.shape[2]), 0)
    meets = line == jnp.where(gy == 0, lines - 1, 0)
    return jnp.where(meets, side[field, pl.ds(row, 1), :], 0.0)


def middle_kernel(partial, ends, kept_courant, side, keep, give):
    shot, gy = lax.axis_index("shot"), lax.axis_index("gy")
    rows, lines, _ = kept_courant.shape

    def one_row(row, values):
        for field in range(2):
            total = side_lines(side, field, row, gy, lines)
            pack_row(values[field] + kept_courant[row] * total, field, row - REACH, shot, keep, give)

    def middle(row, carry):
        one_row(row, [partial[field, row] for field in range(2)])
        return carry

    lax.fori_loop(2 * REACH, rows - 2 * REACH, middle, 0)
    for row in range(REACH, 2 * REACH):
        one_row(row, [ends[field, 0, row] for field in range(2)])
        one_row(rows - 1 - row, [ends[field, 1, row] for field in range(2)])


def finish_middle(partial, ends, kept_courant, side):
    rows, lines, size_z = kept_courant.shape
    half = jax.ShapeDtypeStruct((2, rows - 2 * REACH, lines // 2, size_z), F32)
    return pl.pallas_call(
        middle_kernel,
        out_shape=(half, half),
        in_specs=[VMEM] * 4,
        out_specs=(VMEM,) * 2,
        compiler_params=params(24),
        cost_estimate=cost(10**10, 3 * 2**20),
        name="finish_middle",
    )(partial, ends, kept_courant, side)


def ends_kernel(ends, kept_courant, left, right, side, keep, give):
    shot, gy = lax.axis_index("shot"), lax.axis_index("gy")
    rows, lines, _ = kept_courant.shape
    for field in range(2):
        for row in range(REACH):
            below = above = None
            for d in range(row + 1, REACH + 1):
                term = WEIGHTS[d] * left[field, REACH + row - d]
                below = term if below is None else below + term
                term = WEIGHTS[d] * right[field, d - 1 - row]
                above = term if above is None else above + term
            far = rows - 1 - row
            below = below + side_lines(side, field, row, gy, lines)
            above = above + side_lines(side, field, far, gy, lines)
            pack_row(ends[field, 0, row] + kept_courant[row] * below, field, row, shot, keep, give)
            pack_row(
                ends[field, 1, row] + kept_courant[far] * above,
                field, 2 * REACH - 1 - row, shot, keep, give,
            )


def finish_ends(ends, kept_courant, left, right, side):
    _, lines, size_z = kept_courant.shape
    half = jax.ShapeDtypeStruct((2, 2 * REACH, lines // 2, size_z), F32)
    return pl.pallas_call(
        ends_kernel,
        out_shape=(half, half),
        in_specs=[VMEM] * 5,
        out_specs=(VMEM,) * 2,
        compiler_params=params(24),
        cost_estimate=cost(10**10, 3 * 2**20),
        name="finish_ends",
    )(ends, kept_courant, left, right, side)


def block_starts(rows):
    even = lax.axis_index("gx") % 2 == 0
    return HALF, jnp.where(even, HALF + rows, 0), jnp.where(even, 0, HALF + rows)


def products(rows_of, sample, shift, here):
    total = None
    for group in range(rows_of.shape[0]):
        term = (
            rows_of[group, 0, 2 * HALF + sample - shift, here, :]
            * rows_of[group, 1, sample + shift, here, :]
        )
        total = term if total is None else total + term
    return total


def first_image_kernel(*refs):
    blocks, (out, rows_of, sems) = refs[:6], refs[6:]
    rows = blocks[0].shape[1]

    @pl.when(pl.program_id(0) == 0)
    def _():
        starts = block_starts(rows)
        copies = []
        for index, ref in enumerate(blocks):
            dst = rows_of.at[index // 3, :, pl.ds(starts[index % 3], rows)]
            copies.append(pltpu.make_async_copy(ref, dst, sems.at[index]))
        run_copies(copies)

    sample = 4 * pl.program_id(0)
    for chunk in range(rows_of.shape[3] // 8):
        here = pl.ds(8 * chunk, 8)
        for shift in range(OFFSETS):
            out[0, shift, here, :] = products(rows_of, sample, shift, here)


def first_image(blocks):
    _, rows, lines, size_z = blocks[0].shape
    samples = rows // 4
    return pl.pallas_call(
        first_image_kernel,
        grid=(samples,),
        out_shape=jax.ShapeDtypeStruct((samples, OFFSETS, lines, size_z), F32),
        in_specs=[ANY] * len(blocks),
        out_specs=pl.BlockSpec((1, OFFSETS, lines, size_z), lambda i: (i, 0, 0, 0)),
        scratch_shapes=[
            pltpu.VMEM((2, 2, rows + 2 * HALF, lines, size_z), F32),
            pltpu.SemaphoreType.DMA((6,)),
        ],
        compiler_params=params(16),
        cost_estimate=cost(10**10, 8 * 2**20),
        name="first_image",
    )(*blocks)


def image_kernel(token, first, *refs):
    blocks, (out, rows_of, turned, staged, sems, out_sems) = refs[:9], refs[9:]
    rows = blocks[0].shape[1] + 2 * REACH
    step, steps_in_all = pl.program_id(0), pl.num_programs(0)

    @pl.when(step == 0)
    def _():
        starts = block_starts(rows)
        copies = []

        def copy(src, group, start, count):
            dst = rows_of.at[group, :, pl.ds(start, count)]
            copies.append(pltpu.make_async_copy(src, dst, sems.at[len(copies)]))

        for part in range(2):
            for kind in range(3):
                copy(blocks[3 * part + kind], part, starts[kind] + REACH, rows - 2 * REACH)
            for kind, start in enumerate((HALF, 0, HALF + rows)):
                ends = blocks[6 + kind]
                copy(ends.at[part, :, pl.ds(0, REACH)], part, start, REACH)
                copy(ends.at[part, :, pl.ds(REACH, REACH)], part, start + rows - REACH, REACH)
        run_copies(copies)

    lines, size_z = rows_of.shape[3], rows_of.shape[4]
    chunks = lines // 8

    def leave(at_step, chunk, half):
        slot = at_step % 2
        here = pl.ds(half * lines + 8 * chunk, 8)
        return pltpu.make_async_copy(staged.at[slot, here], out.at[at_step, here], out_sems.at[slot, chunk, half])

    sample = 4 * step
    for chunk in range(chunks):
        here = pl.ds(8 * chunk, 8)
        for shift in range(OFFSETS):
            total = first[0, shift, here, :] + products(rows_of, sample, shift, here)
            turned[chunk, pl.ds(shift, 8, stride=OFFSET_ROWS), :] = total

        @pl.when(step >= 2)
        def _():
            for half in range(2):
                leave(step - 2, chunk, half).wait()

        for line in range(8):
            values = turned[chunk, line * OFFSET_ROWS : (line + 1) * OFFSET_ROWS, :].T
            at = 8 * chunk + line
            staged[step % 2, at] = values[: size_z // 2, :OFFSETS]
            staged[step % 2, lines + at] = values[size_z // 2 :, :OFFSETS]
        for half in range(2):
            leave(step, chunk, half).start()

    @pl.when(step == steps_in_all - 1)
    def _():
        for back in (1, 0):
            for chunk in range(chunks):
                for half in range(2):
                    leave(step - back, chunk, half).wait()


def image(token, first, blocks):
    samples, _, lines, size_z = first.shape
    rows = 4 * samples
    return pl.pallas_call(
        image_kernel,
        grid=(samples,),
        out_shape=jax.ShapeDtypeStruct((samples, 2 * lines, size_z // 2, OFFSETS), F32),
        in_specs=[SMEM, pl.BlockSpec((1, OFFSETS, lines, size_z), lambda i: (i, 0, 0, 0))] + [ANY] * len(blocks),
        out_specs=HBM,
        scratch_shapes=[
            pltpu.VMEM((2, 2, rows + 2 * HALF, lines, size_z), F32),
            pltpu.VMEM((lines // 8, 8 * OFFSET_ROWS, size_z), F32),
            pltpu.VMEM((2, 2 * lines, size_z // 2, OFFSETS), F32),
            pltpu.SemaphoreType.DMA((18,)),
            pltpu.SemaphoreType.DMA((2, lines // 8, 2)),
        ],
        compiler_params=params(20),
        cost_estimate=cost(10**10, 16 * 2**20),
        name="image",
    )(token, first, *blocks)


def in_order_kernel(*refs):
    refs[-1][0] = 0


def in_order(*arrays):
    return pl.pallas_call(
        in_order_kernel,
        out_shape=jax.ShapeDtypeStruct((1,), jnp.int32),
        in_specs=[ANY] * len(arrays),
        out_specs=SMEM,
        compiler_params=params(1),
        cost_estimate=cost(1, 1),
        name="in_order",
    )(*arrays)


def on_device(source_now, source_before, receiver_now, receiver_before, courant):
    size = lax.axis_size("gx")
    up_pairs = [(i, i + 1) for i in range(size - 1)]
    down_pairs = [(j, i) for i, j in up_pairs]
    partner = [(i, i ^ 1) for i in range(size)]
    onward = [(i, i + 2) for i in range(0, size - 2, 2)] + [(i, i - 2) for i in range(3, size, 2)]
    both = [(0, 1), (1, 0)]

    def exchange(array, axis, pairs):
        return lax.ppermute(array, axis, pairs)

    barrier = lax.optimization_barrier
    up, down, keep, give, side = pack(source_now, receiver_now)
    left = exchange(up, "gx", up_pairs)
    right = exchange(down, "gx", down_pairs)
    side = exchange(side, "gy", both)
    other = exchange(give, "shot", both)
    side, keep, other = barrier((side, keep, other))
    near_keep = exchange(keep, "gx", partner)
    near_other = exchange(other, "gx", partner)
    blocks = [keep, near_keep, None, other, near_other, None]
    partial, kept_courant, edge_courant, edge, side = steps(
        source_now, receiver_now, source_before, receiver_before, courant, side
    )
    ends, up, down, side = mend(left, right, partial, kept_courant, edge_courant, edge, side)
    left = exchange(up, "gx", up_pairs)
    right = exchange(down, "gx", down_pairs)
    side = exchange(side, "gy", both)
    side, near_keep = barrier((side, near_keep))
    far_keep = exchange(near_keep, "gx", onward)

    keep, give = finish_middle(partial, ends, kept_courant, side)
    keep, give, near_other = barrier((keep, give, near_other))
    blocks[5] = exchange(near_other, "gx", onward)
    other = exchange(give, "shot", both)
    near_keep = exchange(keep, "gx", partner)

    left, right, blocks[2] = barrier((left, right, far_keep))
    keep_ends, give_ends = finish_ends(ends, kept_courant, left, right, side)
    other, keep_ends, give_ends = barrier((other, keep_ends, give_ends))
    near_other = exchange(other, "gx", partner)
    other_ends = exchange(give_ends, "shot", both)
    other_ends, near_keep = barrier((other_ends, near_keep))
    own = jnp.stack([keep_ends, other_ends])
    far_keep = exchange(near_keep, "gx", onward)
    left = exchange(own, "gx", up_pairs)
    right = exchange(own, "gx", down_pairs)
    far_other = exchange(near_other, "gx", onward)
    blocks[5], far_keep = lax.optimization_barrier((blocks[5], far_keep))
    first = first_image(blocks)
    token = in_order(left, right, first)
    blocks = [keep, near_keep, far_keep, other, near_other, far_other, own, left, right]
    return jnp.transpose(image(token, first, blocks), (3, 0, 1, 2))


def solution(mesh):
    in_specs = (
        P("shot", "gx", "gy", None),
        P("shot", "gx", "gy", None),
        P("shot", "gx", "gy", None),
        P("shot", "gx", "gy", None),
        P("gx", "gy", None),
    )
    out_specs = P(None, "gx", "gy", "shot")
    return jax.shard_map(
        on_device, mesh=mesh, in_specs=in_specs, out_specs=out_specs, check_vma=False
    )
```

```python
import functools

import jax
import jax.numpy as jnp
import numpy as np
from jax import lax
from jax.experimental import pallas as pl
from jax.experimental.pallas import tpu as pltpu
from jax.sharding import PartitionSpec as P

HALF = 32
REACH = 4
KEEP_EVERY = 4
OFFSETS = 2 * HALF + 1
OFFSET_ROWS = 72
LINES = 32
STEPS_MIB = 50
WEIGHTS = (-205.0 / 72.0, 8.0 / 5.0, -1.0 / 5.0, 8.0 / 315.0, -1.0 / 560.0)
PAD = 8
F32 = jnp.float32
HBM = pl.BlockSpec(memory_space=pltpu.HBM)
ANY = pl.BlockSpec(memory_space=pl.ANY)
VMEM = pl.BlockSpec(memory_space=pltpu.VMEM)
SMEM = pl.BlockSpec(memory_space=pltpu.SMEM)


def params(mib):
    return pltpu.CompilerParams(vmem_limit_bytes=mib * 2**20)


def cost(flops, nbytes):
    return pl.CostEstimate(flops=flops, bytes_accessed=nbytes, transcendentals=0)


def run_copies(copies):
    for copy in copies:
        copy.start()
    for copy in copies:
        copy.wait()


def z_halves(lines):
    count, size_z = lines.shape
    top, bottom = lines[: count // 2], lines[count // 2 :]
    low = lax.broadcasted_iota(jnp.int32, top.shape, 1) < size_z // 2
    first = jnp.where(low, top, pltpu.roll(bottom, size_z // 2, 1))
    second = jnp.where(low, pltpu.roll(top, size_z // 2, 1), bottom)
    return first, second


def pack_kernel(
    source, receiver, up, down, edge, keep, keep_ends, give, give_ends, side, fields, sems
):
    shot, gy = lax.axis_index("shot"), lax.axis_index("gy")
    _, rows, size_y, _ = fields.shape
    lines = size_y // KEEP_EVERY
    pieces = sems.shape[0]
    count = rows // pieces
    order = [0, pieces - 1] + list(range(1, pieces - 1))
    copies = {}
    for index in order:
        part = pl.ds(count * index, count)
        for field, ref in enumerate((source, receiver)):
            copies[index, field] = pltpu.make_async_copy(
                ref.at[0, part], fields.at[field, part], sems.at[index, field]
            )
            copies[index, field].start()

    def one_row(row, keep_ref, give_ref, to):
        parts = []
        for field in range(2):
            first, second = z_halves(fields[field, row, pl.ds(0, lines, stride=KEEP_EVERY), :])
            keep_ref[field, to] = jnp.where(shot == 0, first, second)
            give_ref[field, to] = jnp.where(shot == 0, second, first)
            low = fields[field, row, 0:REACH, :]
            high = fields[field, row, size_y - REACH : size_y, :]
            parts.append(jnp.where(gy == 0, high, low))
        side[row] = jnp.concatenate(parts, axis=0)

    def middle_row(row, carry):
        one_row(row, keep, give, row - REACH)
        return carry

    def end_rows(out, start, to):
        for row in range(REACH):
            for field in range(2):
                edge[field, to + row] = fields[field, start + row, pl.ds(0, lines, stride=KEEP_EVERY), :]
                for phase in range(1, KEEP_EVERY):
                    out[field, row, (phase - 1) * lines : phase * lines, :] = fields[
                        field, start + row, pl.ds(phase, lines, stride=KEEP_EVERY), :
                    ]
            one_row(start + row, keep_ends, give_ends, to + row)

    for index in order:
        for field in range(2):
            copies[index, field].wait()
        low, high = count * index, count * (index + 1)
        if index == 0:
            end_rows(down, 0, 0)
            low += REACH
        if index == pieces - 1:
            end_rows(up, rows - REACH, REACH)
            high -= REACH
        lax.fori_loop(low, high, middle_row, 0, unroll=4)


def pack(source, receiver):
    _, rows, size_y, size_z = source.shape
    lines = size_y // KEEP_EVERY
    apart = jax.ShapeDtypeStruct((2, REACH, size_y - lines, size_z), F32)
    middle = jax.ShapeDtypeStruct((2, rows - 2 * REACH, lines // 2, size_z), F32)
    ends = jax.ShapeDtypeStruct((2, 2 * REACH, lines // 2, size_z), F32)
    return pl.pallas_call(
        pack_kernel,
        out_shape=(
            apart,
            apart,
            jax.ShapeDtypeStruct((2, 2 * REACH, lines, size_z), F32),
            middle,
            ends,
            middle,
            ends,
            jax.ShapeDtypeStruct((rows, 2 * REACH, size_z), F32),
        ),
        in_specs=[HBM, HBM],
        out_specs=(VMEM,) * 8,
        scratch_shapes=[
            pltpu.VMEM((2, rows, size_y, size_z), F32),
            pltpu.SemaphoreType.DMA((4, 2)),
        ],
        compiler_params=params(56),
        cost_estimate=cost(10**10, 7 * 2**20),
        name="pack",
    )(source, receiver)


def z_weights(size_z):
    z = lax.broadcasted_iota(jnp.int32, (8, size_z), 1)
    return [
        (jnp.where(z >= d, WEIGHTS[d], 0.0), jnp.where(z < size_z - d, WEIGHTS[d], 0.0))
        for d in range(1, REACH + 1)
    ]


def z_terms(center, masks):
    size_z = center.shape[1]
    center = center.reshape(-1, 8, size_z)
    total = None
    for d, (below, above) in enumerate(masks, start=1):
        term = below * pltpu.roll(center, d, 2) + above * pltpu.roll(center, size_z - d, 2)
        total = term if total is None else total + term
    return total.reshape(-1, size_z)


def z_matrix(size_z):
    z = np.arange(size_z)
    apart = np.abs(z[:, None] - z[None, :])
    weights = np.array((0.0,) + WEIGHTS[1:] + (0.0,), np.float32)[np.minimum(apart, REACH + 1)]
    high = weights.astype(jnp.bfloat16)
    low = (weights - high.astype(np.float32)).astype(jnp.bfloat16)
    return jnp.asarray(np.block([[high, low], [high, np.zeros_like(low)]]))


def z_product(lines, matrix):
    size_z = lines.shape[1]
    high = lines.astype(jnp.bfloat16)
    low = (lines - high.astype(F32)).astype(jnp.bfloat16)
    both = jnp.dot(jnp.concatenate([high, low], axis=1), matrix, preferred_element_type=F32)
    return both[:, :size_z] + both[:, size_z:]


def first_step(now, row, z_sums, before, before_row, scale, scale_row, after, field):
    size_y = before.shape[2]
    lines = size_y // KEEP_EVERY
    for phase in range(KEEP_EVERY):
        kept = lambda start: pl.ds(start, lines, stride=KEEP_EVERY)
        at = PAD + phase
        center = now[field, row, kept(at), :]
        total = (3.0 * WEIGHTS[0]) * center + z_sums[field, kept(phase), :]
        for d in range(1, REACH + 1):
            around = (
                now[field, row + d, kept(at), :]
                + now[field, row - d, kept(at), :]
                + now[field, row, kept(at + d), :]
                + now[field, row, kept(at - d), :]
            )
            total = total + WEIGHTS[d] * around
        after[field, row, kept(at), :] = (
            2.0 * center
            - before[field, before_row, kept(phase), :]
            + scale[scale_row, kept(phase), :] * total
        )


def second_step(now, row, scale, scale_row, after, field, z_sum):
    size_y = scale.shape[1]
    lines = size_y // KEEP_EVERY
    kept = lambda start: pl.ds(start, lines, stride=KEEP_EVERY)
    center = after[field, row, kept(PAD), :]
    total = (3.0 * WEIGHTS[0]) * center + z_sum
    for d in range(1, REACH + 1):
        around = (
            after[field, row + d, kept(PAD), :]
            + after[field, row - d, kept(PAD), :]
            + after[field, row, kept(PAD + d), :]
            + after[field, row, kept(PAD - d), :]
        )
        total = total + WEIGHTS[d] * around
    return 2.0 * center - now[field, row, kept(PAD), :] + scale[scale_row, kept(0), :] * total


def side_term(after, after_row, field, size_y, gy):
    lowest = WEIGHTS[REACH] * after[field, after_row, PAD : PAD + 1, :]
    highest = sum(
        WEIGHTS[d] * after[field, after_row, PAD + size_y - d : PAD + size_y - d + 1, :]
        for d in range(1, REACH + 1)
    )
    return jnp.where(gy == 0, highest, lowest)


def fill_sides(now, row, got, field, size_y, gy):
    blank = jnp.zeros_like(got)
    now[field, row, PAD - REACH : PAD, :] = jnp.where(gy == 0, blank, got)
    now[field, row, size_y + PAD : size_y + PAD + REACH, :] = jnp.where(gy == 0, got, blank)


def blank_sides(after, row, field, size_y):
    blank = jnp.zeros((REACH, after.shape[3]), F32)
    after[field, row, PAD - REACH : PAD, :] = blank
    after[field, row, size_y + PAD : size_y + PAD + REACH, :] = blank


def steps_kernel(
    source, receiver, source_before, receiver_before, courant, side, matrix,
    partial, kept_courant, edge_courant, edge, side_out, now, before, scale, after, z_sums, sems,
):
    gy = lax.axis_index("gy")
    rows, size_y, size_z = courant.shape
    lines = size_y // KEEP_EVERY
    piece = 2 * REACH
    middle = pl.ds(PAD, size_y)

    def copies(index):
        part = pl.ds(piece * index, piece)
        found = []
        for field in range(2):
            src = (source, receiver)[field].at[0, part]
            dst = now.at[field, pl.ds(REACH + piece * index, piece), middle]
            found.append(pltpu.make_async_copy(src, dst, sems.at[index, field]))
        for field in range(2):
            src = (source_before, receiver_before)[field].at[0, part]
            found.append(pltpu.make_async_copy(src, before.at[field, part], sems.at[index, 2 + field]))
        found.append(pltpu.make_async_copy(courant.at[part], scale.at[part], sems.at[index, 4]))
        return found

    for index in range(rows // piece):
        for one in copies(index):
            one.start()

    for field in range(2):
        for row in list(range(REACH)) + list(range(rows + REACH, rows + 2 * REACH)):
            now[field, row] = jnp.zeros((size_y + 2 * PAD, size_z), F32)
            after[field, row] = jnp.zeros((size_y + 2 * PAD, size_z), F32)

    def fill(row, carry):
        for field in range(2):
            got = side[row, field * REACH : (field + 1) * REACH, :]
            fill_sides(now, row + REACH, got, field, size_y, gy)
            blank_sides(after, row + REACH, field, size_y)
        return carry

    lax.fori_loop(0, rows, fill, 0)
    for one in copies(0)[:2]:
        one.wait()

    def z_next(row):
        found = z_product(
            jnp.concatenate([now[field, row + REACH, middle, :] for field in range(2)], axis=0), matrix[...]
        )
        for field in range(2):
            z_sums[row % 2, field] = found[field * size_y : (field + 1) * size_y]

    z_next(0)

    def first(row, carry):
        @pl.when(row % piece == 0)
        def _():
            index = row // piece
            for one in copies(index)[2:]:
                one.wait()

            @pl.when(index + 1 < rows // piece)
            def _():
                for one in copies(index + 1)[:2]:
                    one.wait()

        at = row + REACH
        for field in range(2):
            first_step(now, at, z_sums.at[row % 2], before, row, scale, row, after, field)
        z_next(row + 1)
        for field in range(2):
            side_out[field, pl.ds(row, 1), :] = side_term(after, at, field, size_y, gy)
        return carry

    lax.fori_loop(0, rows, first, 0)

    def second(row, carry):
        at = row + REACH
        kept_courant[row] = scale[row, pl.ds(0, lines, stride=KEEP_EVERY), :]
        centers = [after[field, at, pl.ds(PAD, lines, stride=KEEP_EVERY), :] for field in range(2)]
        z_sum = z_product(jnp.concatenate(centers, axis=0), matrix[...])
        for field in range(2):
            partial[field, row] = second_step(
                now, at, scale, row, after, field, z_sum[field * lines : (field + 1) * lines]
            )
        return carry

    lax.fori_loop(0, rows, second, 0, unroll=2)
    for end in range(2):
        for row in range(REACH):
            at = rows - 1 - row if end else row
            edge_courant[end, row] = scale[at]
            for field in range(2):
                edge[field, end, row] = after[field, REACH + at, pl.ds(PAD, lines, stride=KEEP_EVERY), :]


def steps(source, receiver, source_before, receiver_before, courant, side):
    rows, size_y, size_z = courant.shape
    lines = size_y // KEEP_EVERY
    return pl.pallas_call(
        steps_kernel,
        out_shape=(
            jax.ShapeDtypeStruct((2, rows, lines, size_z), F32),
            jax.ShapeDtypeStruct((rows, lines, size_z), F32),
            jax.ShapeDtypeStruct((2, REACH, size_y, size_z), F32),
            jax.ShapeDtypeStruct((2, 2, REACH, lines, size_z), F32),
            jax.ShapeDtypeStruct((2, rows, size_z), F32),
        ),
        in_specs=[HBM] * 5 + [VMEM] * 2,
        out_specs=(VMEM,) * 5,
        scratch_shapes=[
            pltpu.VMEM((2, rows + 2 * REACH, size_y + 2 * PAD, size_z), F32),
            pltpu.VMEM((2, rows, size_y, size_z), F32),
            pltpu.VMEM((rows, size_y, size_z), F32),
            pltpu.VMEM((2, rows + 2 * REACH, size_y + 2 * PAD, size_z), F32),
            pltpu.VMEM((2, 2, size_y, size_z), F32),
            pltpu.SemaphoreType.DMA((rows // (2 * REACH), 5)),
        ],
        compiler_params=params(STEPS_MIB),
        cost_estimate=cost(2 * 10**10, 2**20),
        name="steps",
    )(source, receiver, source_before, receiver_before, courant, side, z_matrix(size_z))


def mend_kernel(
    left, right, near, far, partial, kept_courant, edge_courant, edge, side_in,
    ends, up, down, side_out, keep, give, added,
):
    gy, shot = lax.axis_index("gy"), lax.axis_index("shot")
    even = lax.axis_index("gx") % 2 == 0
    rows, lines, size_z = kept_courant.shape
    size_y = KEEP_EVERY * lines
    masks = z_weights(size_z)
    kept = lambda start: pl.ds(start, lines, stride=KEEP_EVERY)
    side_out[...] = side_in[...]
    for end in range(2):
        for field in range(2):
            group = 2 * end + field
            for row in range(REACH):
                blank_sides(added, row, group, size_y)
                for phase in range(KEEP_EVERY):
                    total = None
                    for d in range(row + 1, REACH + 1):
                        beyond = d - row - 1
                        at = beyond if end else REACH - 1 - beyond
                        if phase:
                            halo = (right if end else left)[field, at, (phase - 1) * lines : phase * lines, :]
                        elif end:
                            halo = jnp.where(even, near[field, at], far[field, at])
                        else:
                            halo = jnp.where(even, far[field, REACH + at], near[field, REACH + at])
                        term = WEIGHTS[d] * halo
                        total = term if total is None else total + term
                    scaled = edge_courant[end, row, pl.ds(phase, lines, stride=KEEP_EVERY), :]
                    added[group, row, kept(PAD + phase), :] = scaled * total
            for row in range(2 * REACH):
                at = rows - 1 - row if end else row
                total = None
                for other in range(REACH):
                    if 0 < abs(row - other) <= REACH:
                        term = WEIGHTS[abs(row - other)] * added[group, other, kept(PAD), :]
                        total = term if total is None else total + term
                value = partial[field, at]
                if row < REACH:
                    center = added[group, row, kept(PAD), :]
                    total = total + (3.0 * WEIGHTS[0]) * center + z_terms(center, masks)
                    for d in range(1, REACH + 1):
                        around = added[group, row, kept(PAD + d), :] + added[group, row, kept(PAD - d), :]
                        total = total + WEIGHTS[d] * around
                    value = value + 2.0 * center
                    first = edge[field, end, row] + center
                    if end:
                        up[field, REACH - 1 - row] = first
                    else:
                        down[field, row] = first
                    side_out[field, at : at + 1, :] = side_in[field, at : at + 1, :] + side_term(
                        added, row, group, size_y, gy
                    )
                ends[field, end, row] = value + kept_courant[at] * total
    for kind, ref in enumerate((near, far)):
        for field in range(2):
            for row in range(2 * REACH):
                pack_row(ref[field, row], field, row, shot, keep.at[kind], give.at[kind])


def mend(left, right, near, far, partial, kept_courant, edge_courant, edge, side_in):
    rows, lines, size_z = kept_courant.shape
    halo = jax.ShapeDtypeStruct((2, REACH, lines, size_z), F32)
    half = jax.ShapeDtypeStruct((2, 2, 2 * REACH, lines // 2, size_z), F32)
    return pl.pallas_call(
        mend_kernel,
        out_shape=(
            jax.ShapeDtypeStruct((2, 2, 2 * REACH, lines, size_z), F32),
            halo,
            halo,
            jax.ShapeDtypeStruct((2, rows, size_z), F32),
            half,
            half,
        ),
        in_specs=[VMEM] * 9,
        out_specs=(VMEM,) * 6,
        scratch_shapes=[pltpu.VMEM((4, REACH, KEEP_EVERY * lines + 2 * PAD, size_z), F32)],
        compiler_params=params(24),
        cost_estimate=cost(10**6, 2**20),
        name="mend",
    )(left, right, near, far, partial, kept_courant, edge_courant, edge, side_in)


def pack_row(value, field, row, shot, keep, give):
    first, second = z_halves(value)
    keep[field, row] = jnp.where(shot == 0, first, second)
    give[field, row] = jnp.where(shot == 0, second, first)


def side_lines(side, field, row, gy, lines):
    line = lax.broadcasted_iota(jnp.int32, (lines, side.shape[2]), 0)
    meets = line == jnp.where(gy == 0, lines - 1, 0)
    return jnp.where(meets, side[field, pl.ds(row, 1), :], 0.0)


def middle_kernel(partial, ends, kept_courant, side, keep, give):
    shot, gy = lax.axis_index("shot"), lax.axis_index("gy")
    rows, lines, _ = kept_courant.shape

    def one_row(row, values):
        for field in range(2):
            total = side_lines(side, field, row, gy, lines)
            pack_row(values[field] + kept_courant[row] * total, field, row - REACH, shot, keep, give)

    def middle(row, carry):
        one_row(row, [partial[field, row] for field in range(2)])
        return carry

    lax.fori_loop(2 * REACH, rows - 2 * REACH, middle, 0)
    for row in range(REACH, 2 * REACH):
        one_row(row, [ends[field, 0, row] for field in range(2)])
        one_row(rows - 1 - row, [ends[field, 1, row] for field in range(2)])


def finish_middle(partial, ends, kept_courant, side):
    rows, lines, size_z = kept_courant.shape
    half = jax.ShapeDtypeStruct((2, rows - 2 * REACH, lines // 2, size_z), F32)
    return pl.pallas_call(
        middle_kernel,
        out_shape=(half, half),
        in_specs=[VMEM] * 4,
        out_specs=(VMEM,) * 2,
        compiler_params=params(24),
        cost_estimate=cost(10**10, 3 * 2**20),
        name="finish_middle",
    )(partial, ends, kept_courant, side)


def ends_kernel(ends, kept_courant, left, right, side, keep, give):
    shot, gy = lax.axis_index("shot"), lax.axis_index("gy")
    rows, lines, _ = kept_courant.shape
    for field in range(2):
        for row in range(REACH):
            below = above = None
            for d in range(row + 1, REACH + 1):
                term = WEIGHTS[d] * left[field, REACH + row - d]
                below = term if below is None else below + term
                term = WEIGHTS[d] * right[field, d - 1 - row]
                above = term if above is None else above + term
            far = rows - 1 - row
            below = below + side_lines(side, field, row, gy, lines)
            above = above + side_lines(side, field, far, gy, lines)
            pack_row(ends[field, 0, row] + kept_courant[row] * below, field, row, shot, keep, give)
            pack_row(
                ends[field, 1, row] + kept_courant[far] * above,
                field, 2 * REACH - 1 - row, shot, keep, give,
            )


def finish_ends(ends, kept_courant, left, right, side):
    _, lines, size_z = kept_courant.shape
    half = jax.ShapeDtypeStruct((2, 2 * REACH, lines // 2, size_z), F32)
    return pl.pallas_call(
        ends_kernel,
        out_shape=(half, half),
        in_specs=[VMEM] * 5,
        out_specs=(VMEM,) * 2,
        compiler_params=params(24),
        cost_estimate=cost(10**10, 3 * 2**20),
        name="finish_ends",
    )(ends, kept_courant, left, right, side)


def block_starts(rows):
    even = lax.axis_index("gx") % 2 == 0
    return HALF, jnp.where(even, HALF + rows, 0), jnp.where(even, 0, HALF + rows)


def products(rows_of, sample, shift, here):
    total = None
    for group in range(rows_of.shape[0]):
        term = (
            rows_of[group, 0, 2 * HALF + sample - shift, here, :]
            * rows_of[group, 1, sample + shift, here, :]
        )
        total = term if total is None else total + term
    return total


def layout_copies(middles, ends, middle_starts, end_starts, rows_of, sems):
    copies = []

    def copy(src, part, start, count):
        dst = rows_of.at[part, :, pl.ds(start, count)]
        copies.append(pltpu.make_async_copy(src, dst, sems.at[len(copies)]))

    count = middles[0][0].shape[1]
    for part in range(2):
        for src, start in zip(middles[part], middle_starts):
            copy(src, part, start + REACH, count)
        for src, start in zip(ends[part], end_starts):
            copy(src.at[:, pl.ds(0, REACH)], part, start, REACH)
            copy(src.at[:, pl.ds(REACH, REACH)], part, start + REACH + count, REACH)
    return copies


def first_image_kernel(*refs):
    blocks, (out, rows_of, sems) = refs[:10], refs[10:]
    rows = blocks[0].shape[1] + 2 * REACH

    @pl.when(pl.program_id(0) == 0)
    def _():
        starts = block_starts(rows)
        ends = [[blocks[6 + part], blocks[8 + part].at[0], blocks[8 + part].at[1]] for part in range(2)]
        run_copies(layout_copies([blocks[:3], blocks[3:6]], ends, starts, starts, rows_of, sems))

    sample = 4 * pl.program_id(0)
    for chunk in range(rows_of.shape[3] // 8):
        here = pl.ds(8 * chunk, 8)
        for shift in range(OFFSETS):
            out[0, shift, here, :] = products(rows_of, sample, shift, here)


def first_image(blocks):
    _, middle_rows, lines, size_z = blocks[0].shape
    rows = middle_rows + 2 * REACH
    samples = rows // 4
    return pl.pallas_call(
        first_image_kernel,
        grid=(samples,),
        out_shape=jax.ShapeDtypeStruct((samples, OFFSETS, lines, size_z), F32),
        in_specs=[ANY] * len(blocks),
        out_specs=pl.BlockSpec((1, OFFSETS, lines, size_z), lambda i: (i, 0, 0, 0)),
        scratch_shapes=[
            pltpu.VMEM((2, 2, rows + 2 * HALF, lines, size_z), F32),
            pltpu.SemaphoreType.DMA((18,)),
        ],
        compiler_params=params(16),
        cost_estimate=cost(10**10, 8 * 2**20),
        name="first_image",
    )(*blocks)


def image_kernel(token, first, *refs):
    blocks, (out, rows_of, turned, staged, sems, out_sems) = refs[:9], refs[9:]
    rows = blocks[0].shape[1] + 2 * REACH
    step, steps_in_all = pl.program_id(0), pl.num_programs(0)

    @pl.when(step == 0)
    def _():
        ends = [[ref.at[part] for ref in blocks[6:]] for part in range(2)]
        end_starts = (HALF, 0, HALF + rows)
        run_copies(
            layout_copies([blocks[:3], blocks[3:6]], ends, block_starts(rows), end_starts, rows_of, sems)
        )

    lines, size_z = rows_of.shape[3], rows_of.shape[4]
    chunks = lines // 8

    def leave(at_step, chunk, half):
        slot = at_step % 2
        here = pl.ds(half * lines + 8 * chunk, 8)
        return pltpu.make_async_copy(staged.at[slot, here], out.at[at_step, here], out_sems.at[slot, chunk, half])

    sample = 4 * step
    for chunk in range(chunks):
        here = pl.ds(8 * chunk, 8)
        for shift in range(OFFSETS):
            total = first[0, shift, here, :] + products(rows_of, sample, shift, here)
            turned[chunk, pl.ds(shift, 8, stride=OFFSET_ROWS), :] = total

        @pl.when(step >= 2)
        def _():
            for half in range(2):
                leave(step - 2, chunk, half).wait()

        for line in range(8):
            values = turned[chunk, line * OFFSET_ROWS : (line + 1) * OFFSET_ROWS, :].T
            at = 8 * chunk + line
            staged[step % 2, at] = values[: size_z // 2, :OFFSETS]
            staged[step % 2, lines + at] = values[size_z // 2 :, :OFFSETS]
        for half in range(2):
            leave(step, chunk, half).start()

    @pl.when(step == steps_in_all - 1)
    def _():
        for back in (1, 0):
            for chunk in range(chunks):
                for half in range(2):
                    leave(step - back, chunk, half).wait()


def image(token, first, blocks):
    samples, _, lines, size_z = first.shape
    rows = 4 * samples
    return pl.pallas_call(
        image_kernel,
        grid=(samples,),
        out_shape=jax.ShapeDtypeStruct((samples, 2 * lines, size_z // 2, OFFSETS), F32),
        in_specs=[SMEM, pl.BlockSpec((1, OFFSETS, lines, size_z), lambda i: (i, 0, 0, 0))] + [ANY] * len(blocks),
        out_specs=HBM,
        scratch_shapes=[
            pltpu.VMEM((2, 2, rows + 2 * HALF, lines, size_z), F32),
            pltpu.VMEM((lines // 8, 8 * OFFSET_ROWS, size_z), F32),
            pltpu.VMEM((2, 2 * lines, size_z // 2, OFFSETS), F32),
            pltpu.SemaphoreType.DMA((18,)),
            pltpu.SemaphoreType.DMA((2, lines // 8, 2)),
        ],
        compiler_params=params(20),
        cost_estimate=cost(10**10, 16 * 2**20),
        name="image",
    )(token, first, *blocks)


def in_order_kernel(*refs):
    refs[-1][0] = 0


def in_order(*arrays):
    return pl.pallas_call(
        in_order_kernel,
        out_shape=jax.ShapeDtypeStruct((1,), jnp.int32),
        in_specs=[ANY] * len(arrays),
        out_specs=SMEM,
        compiler_params=params(1),
        cost_estimate=cost(1, 1),
        name="in_order",
    )(*arrays)


def on_device(source_now, source_before, receiver_now, receiver_before, courant):
    size = lax.axis_size("gx")
    up_pairs = [(i, i + 1) for i in range(size - 1)]
    down_pairs = [(j, i) for i, j in up_pairs]
    partner = [(i, i ^ 1) for i in range(size)]
    onward = [(i, i + 2) for i in range(0, size - 2, 2)] + [(i, i - 2) for i in range(3, size, 2)]
    both = [(0, 1), (1, 0)]

    def exchange(array, axis, pairs):
        return lax.ppermute(array, axis, pairs)

    barrier = lax.optimization_barrier
    up, down, edge, keep, keep_ends, give, give_ends, side = pack(source_now, receiver_now)
    near_edge = exchange(edge, "gx", partner)
    left = exchange(up, "gx", up_pairs)
    right = exchange(down, "gx", down_pairs)
    side = exchange(side, "gy", both)
    other = exchange(give, "shot", both)
    other_ends = exchange(give_ends, "shot", both)
    side, keep, other = barrier((side, keep, other))
    near_keep = exchange(keep, "gx", partner)
    near_other = exchange(other, "gx", partner)
    far_edge = exchange(near_edge, "gx", onward)
    blocks = [keep, near_keep, None, other, near_other, None, keep_ends, other_ends]
    partial, kept_courant, edge_courant, edge, side = steps(
        source_now, receiver_now, source_before, receiver_before, courant, side
    )
    ends, up, down, side, keep_edges, give_edges = mend(
        left, right, near_edge, far_edge, partial, kept_courant, edge_courant, edge, side
    )
    blocks += [keep_edges, exchange(give_edges, "shot", both)]
    left = exchange(up, "gx", up_pairs)
    right = exchange(down, "gx", down_pairs)
    side = exchange(side, "gy", both)
    side, near_keep, blocks[7], blocks[9] = barrier((side, near_keep, blocks[7], blocks[9]))
    far_keep = exchange(near_keep, "gx", onward)

    keep, give = finish_middle(partial, ends, kept_courant, side)
    keep, give, near_other = barrier((keep, give, near_other))
    blocks[5] = exchange(near_other, "gx", onward)
    other = exchange(give, "shot", both)
    near_keep = exchange(keep, "gx", partner)

    left, right, blocks[2] = barrier((left, right, far_keep))
    keep_ends, give_ends = finish_ends(ends, kept_courant, left, right, side)
    other, keep_ends, give_ends = barrier((other, keep_ends, give_ends))
    near_other = exchange(other, "gx", partner)
    other_ends = exchange(give_ends, "shot", both)
    other_ends, near_keep = barrier((other_ends, near_keep))
    own = jnp.stack([keep_ends, other_ends])
    far_keep = exchange(near_keep, "gx", onward)
    left = exchange(own, "gx", up_pairs)
    right = exchange(own, "gx", down_pairs)
    far_other = exchange(near_other, "gx", onward)
    blocks[5], far_keep = lax.optimization_barrier((blocks[5], far_keep))
    first = first_image(blocks)
    token = in_order(left, right, first)
    blocks = [keep, near_keep, far_keep, other, near_other, far_other, own, left, right]
    return jnp.transpose(image(token, first, blocks), (3, 0, 1, 2))


def solution(mesh):
    in_specs = (
        P("shot", "gx", "gy", None),
        P("shot", "gx", "gy", None),
        P("shot", "gx", "gy", None),
        P("shot", "gx", "gy", None),
        P("gx", "gy", None),
    )
    out_specs = P(None, "gx", "gy", "shot")
    return jax.shard_map(
        on_device, mesh=mesh, in_specs=in_specs, out_specs=out_specs, check_vma=False
    )
```

```python
import functools

import jax
import jax.numpy as jnp
import numpy as np
from jax import lax
from jax.experimental import pallas as pl
from jax.experimental.pallas import tpu as pltpu
from jax.sharding import PartitionSpec as P

HALF = 32
REACH = 4
KEEP_EVERY = 4
OFFSETS = 2 * HALF + 1
OFFSET_ROWS = 72
LINES = 32
STEPS_MIB = 50
WEIGHTS = (-205.0 / 72.0, 8.0 / 5.0, -1.0 / 5.0, 8.0 / 315.0, -1.0 / 560.0)
PAD = 8
F32 = jnp.float32
HBM = pl.BlockSpec(memory_space=pltpu.HBM)
ANY = pl.BlockSpec(memory_space=pl.ANY)
VMEM = pl.BlockSpec(memory_space=pltpu.VMEM)
SMEM = pl.BlockSpec(memory_space=pltpu.SMEM)


def params(mib):
    return pltpu.CompilerParams(vmem_limit_bytes=mib * 2**20)


def cost(flops, nbytes):
    return pl.CostEstimate(flops=flops, bytes_accessed=nbytes, transcendentals=0)


def run_copies(copies):
    for copy in copies:
        copy.start()
    for copy in copies:
        copy.wait()


def z_halves(lines):
    count, size_z = lines.shape
    top, bottom = lines[: count // 2], lines[count // 2 :]
    low = lax.broadcasted_iota(jnp.int32, top.shape, 1) < size_z // 2
    first = jnp.where(low, top, pltpu.roll(bottom, size_z // 2, 1))
    second = jnp.where(low, pltpu.roll(top, size_z // 2, 1), bottom)
    return first, second


def pack_kernel(
    source, receiver, up, down, edge, keep, keep_ends, give, give_ends, side, fields, sems
):
    shot, gy = lax.axis_index("shot"), lax.axis_index("gy")
    _, rows, size_y, _ = fields.shape
    lines = size_y // KEEP_EVERY
    pieces = sems.shape[0]
    count = rows // pieces
    order = [0, pieces - 1] + list(range(1, pieces - 1))
    copies = {}
    for index in order:
        part = pl.ds(count * index, count)
        for field, ref in enumerate((source, receiver)):
            copies[index, field] = pltpu.make_async_copy(
                ref.at[0, part], fields.at[field, part], sems.at[index, field]
            )
            copies[index, field].start()

    def one_row(row, keep_ref, give_ref, to):
        parts = []
        for field in range(2):
            first, second = z_halves(fields[field, row, pl.ds(0, lines, stride=KEEP_EVERY), :])
            keep_ref[field, to] = jnp.where(shot == 0, first, second)
            give_ref[field, to] = jnp.where(shot == 0, second, first)
            low = fields[field, row, 0:REACH, :]
            high = fields[field, row, size_y - REACH : size_y, :]
            parts.append(jnp.where(gy == 0, high, low))
        side[row] = jnp.concatenate(parts, axis=0)

    def middle_row(row, carry):
        one_row(row, keep, give, row - REACH)
        return carry

    def end_rows(out, start, to):
        for row in range(REACH):
            for field in range(2):
                edge[field, to + row] = fields[field, start + row, pl.ds(0, lines, stride=KEEP_EVERY), :]
                for phase in range(1, KEEP_EVERY):
                    out[field, row, (phase - 1) * lines : phase * lines, :] = fields[
                        field, start + row, pl.ds(phase, lines, stride=KEEP_EVERY), :
                    ]
            one_row(start + row, keep_ends, give_ends, to + row)

    for index in order:
        for field in range(2):
            copies[index, field].wait()
        low, high = count * index, count * (index + 1)
        if index == 0:
            end_rows(down, 0, 0)
            low += REACH
        if index == pieces - 1:
            end_rows(up, rows - REACH, REACH)
            high -= REACH
        lax.fori_loop(low, high, middle_row, 0, unroll=4)


def pack(source, receiver):
    _, rows, size_y, size_z = source.shape
    lines = size_y // KEEP_EVERY
    apart = jax.ShapeDtypeStruct((2, REACH, size_y - lines, size_z), F32)
    middle = jax.ShapeDtypeStruct((2, rows - 2 * REACH, lines // 2, size_z), F32)
    ends = jax.ShapeDtypeStruct((2, 2 * REACH, lines // 2, size_z), F32)
    return pl.pallas_call(
        pack_kernel,
        out_shape=(
            apart,
            apart,
            jax.ShapeDtypeStruct((2, 2 * REACH, lines, size_z), F32),
            middle,
            ends,
            middle,
            ends,
            jax.ShapeDtypeStruct((rows, 2 * REACH, size_z), F32),
        ),
        in_specs=[HBM, HBM],
        out_specs=(VMEM,) * 8,
        scratch_shapes=[
            pltpu.VMEM((2, rows, size_y, size_z), F32),
            pltpu.SemaphoreType.DMA((4, 2)),
        ],
        compiler_params=params(56),
        cost_estimate=cost(10**10, 7 * 2**20),
        name="pack",
    )(source, receiver)


def z_weights(size_z):
    z = lax.broadcasted_iota(jnp.int32, (8, size_z), 1)
    return [
        (jnp.where(z >= d, WEIGHTS[d], 0.0), jnp.where(z < size_z - d, WEIGHTS[d], 0.0))
        for d in range(1, REACH + 1)
    ]


def z_terms(center, masks):
    size_z = center.shape[1]
    center = center.reshape(-1, 8, size_z)
    total = None
    for d, (below, above) in enumerate(masks, start=1):
        term = below * pltpu.roll(center, d, 2) + above * pltpu.roll(center, size_z - d, 2)
        total = term if total is None else total + term
    return total.reshape(-1, size_z)


def z_matrix(size_z):
    z = np.arange(size_z)
    apart = np.abs(z[:, None] - z[None, :])
    weights = np.array((0.0,) + WEIGHTS[1:] + (0.0,), np.float32)[np.minimum(apart, REACH + 1)]
    high = weights.astype(jnp.bfloat16)
    low = (weights - high.astype(np.float32)).astype(jnp.bfloat16)
    return jnp.asarray(np.block([[high, low], [high, np.zeros_like(low)]]))


def z_product(lines, matrix):
    size_z = lines.shape[1]
    high = lines.astype(jnp.bfloat16)
    low = (lines - high.astype(F32)).astype(jnp.bfloat16)
    both = jnp.dot(jnp.concatenate([high, low], axis=1), matrix, preferred_element_type=F32)
    return both[:, :size_z] + both[:, size_z:]


def first_step(now, row, z_sums, before, before_row, scale, scale_row, after, field):
    size_y = before.shape[2]
    lines = size_y // KEEP_EVERY
    for phase in range(KEEP_EVERY):
        kept = lambda start: pl.ds(start, lines, stride=KEEP_EVERY)
        at = PAD + phase
        center = now[field, row, kept(at), :]
        total = (3.0 * WEIGHTS[0]) * center + z_sums[field, kept(phase), :]
        for d in range(1, REACH + 1):
            around = (
                now[field, row + d, kept(at), :]
                + now[field, row - d, kept(at), :]
                + now[field, row, kept(at + d), :]
                + now[field, row, kept(at - d), :]
            )
            total = total + WEIGHTS[d] * around
        after[field, row, kept(at), :] = (
            2.0 * center
            - before[field, before_row, kept(phase), :]
            + scale[scale_row, kept(phase), :] * total
        )


def second_step(now, row, scale, scale_row, after, field, z_sum):
    size_y = scale.shape[1]
    lines = size_y // KEEP_EVERY
    kept = lambda start: pl.ds(start, lines, stride=KEEP_EVERY)
    center = after[field, row, kept(PAD), :]
    total = (3.0 * WEIGHTS[0]) * center + z_sum
    for d in range(1, REACH + 1):
        around = (
            after[field, row + d, kept(PAD), :]
            + after[field, row - d, kept(PAD), :]
            + after[field, row, kept(PAD + d), :]
            + after[field, row, kept(PAD - d), :]
        )
        total = total + WEIGHTS[d] * around
    return 2.0 * center - now[field, row, kept(PAD), :] + scale[scale_row, kept(0), :] * total


def side_term(after, after_row, field, size_y, gy):
    lowest = WEIGHTS[REACH] * after[field, after_row, PAD : PAD + 1, :]
    highest = sum(
        WEIGHTS[d] * after[field, after_row, PAD + size_y - d : PAD + size_y - d + 1, :]
        for d in range(1, REACH + 1)
    )
    return jnp.where(gy == 0, highest, lowest)


def fill_sides(now, row, got, field, size_y, gy):
    blank = jnp.zeros_like(got)
    now[field, row, PAD - REACH : PAD, :] = jnp.where(gy == 0, blank, got)
    now[field, row, size_y + PAD : size_y + PAD + REACH, :] = jnp.where(gy == 0, got, blank)


def blank_sides(after, row, field, size_y):
    blank = jnp.zeros((REACH, after.shape[3]), F32)
    after[field, row, PAD - REACH : PAD, :] = blank
    after[field, row, size_y + PAD : size_y + PAD + REACH, :] = blank


def steps_kernel(
    source, receiver, source_before, receiver_before, courant, side, matrix,
    partial, kept_courant, edge_courant, edge, side_out, now, before, scale, after, z_sums, sems,
):
    gy = lax.axis_index("gy")
    rows, size_y, size_z = courant.shape
    lines = size_y // KEEP_EVERY
    piece = 2 * REACH
    middle = pl.ds(PAD, size_y)

    def copies(index):
        part = pl.ds(piece * index, piece)
        found = []
        for field in range(2):
            src = (source, receiver)[field].at[0, part]
            dst = now.at[field, pl.ds(REACH + piece * index, piece), middle]
            found.append(pltpu.make_async_copy(src, dst, sems.at[index, field]))
        for field in range(2):
            src = (source_before, receiver_before)[field].at[0, part]
            found.append(pltpu.make_async_copy(src, before.at[field, part], sems.at[index, 2 + field]))
        found.append(pltpu.make_async_copy(courant.at[part], scale.at[part], sems.at[index, 4]))
        return found

    for index in range(rows // piece):
        for one in copies(index):
            one.start()

    for field in range(2):
        for row in list(range(REACH)) + list(range(rows + REACH, rows + 2 * REACH)):
            now[field, row] = jnp.zeros((size_y + 2 * PAD, size_z), F32)
            after[field, row] = jnp.zeros((size_y + 2 * PAD, size_z), F32)

    def fill(row, carry):
        for field in range(2):
            got = side[row, field * REACH : (field + 1) * REACH, :]
            fill_sides(now, row + REACH, got, field, size_y, gy)
            blank_sides(after, row + REACH, field, size_y)
        return carry

    lax.fori_loop(0, rows, fill, 0)
    for one in copies(0)[:2]:
        one.wait()

    def z_next(row):
        found = z_product(
            jnp.concatenate([now[field, row + REACH, middle, :] for field in range(2)], axis=0), matrix[...]
        )
        for field in range(2):
            z_sums[row % 2, field] = found[field * size_y : (field + 1) * size_y]

    z_next(0)

    def first(row, carry):
        @pl.when(row % piece == 0)
        def _():
            index = row // piece
            for one in copies(index)[2:]:
                one.wait()

            @pl.when(index + 1 < rows // piece)
            def _():
                for one in copies(index + 1)[:2]:
                    one.wait()

        at = row + REACH
        for field in range(2):
            first_step(now, at, z_sums.at[row % 2], before, row, scale, row, after, field)
        z_next(row + 1)
        for field in range(2):
            side_out[field, pl.ds(row, 1), :] = side_term(after, at, field, size_y, gy)
        return carry

    lax.fori_loop(0, rows, first, 0)

    def second(row, carry):
        at = row + REACH
        kept_courant[row] = scale[row, pl.ds(0, lines, stride=KEEP_EVERY), :]
        centers = [after[field, at, pl.ds(PAD, lines, stride=KEEP_EVERY), :] for field in range(2)]
        z_sum = z_product(jnp.concatenate(centers, axis=0), matrix[...])
        for field in range(2):
            partial[field, row] = second_step(
                now, at, scale, row, after, field, z_sum[field * lines : (field + 1) * lines]
            )
        return carry

    lax.fori_loop(0, rows, second, 0, unroll=2)
    for end in range(2):
        for row in range(REACH):
            at = rows - 1 - row if end else row
            edge_courant[end, row] = scale[at]
            for field in range(2):
                edge[field, end, row] = after[field, REACH + at, pl.ds(PAD, lines, stride=KEEP_EVERY), :]


def steps(source, receiver, source_before, receiver_before, courant, side):
    rows, size_y, size_z = courant.shape
    lines = size_y // KEEP_EVERY
    return pl.pallas_call(
        steps_kernel,
        out_shape=(
            jax.ShapeDtypeStruct((2, rows, lines, size_z), F32),
            jax.ShapeDtypeStruct((rows, lines, size_z), F32),
            jax.ShapeDtypeStruct((2, REACH, size_y, size_z), F32),
            jax.ShapeDtypeStruct((2, 2, REACH, lines, size_z), F32),
            jax.ShapeDtypeStruct((2, rows, size_z), F32),
        ),
        in_specs=[HBM] * 5 + [VMEM] * 2,
        out_specs=(VMEM,) * 5,
        scratch_shapes=[
            pltpu.VMEM((2, rows + 2 * REACH, size_y + 2 * PAD, size_z), F32),
            pltpu.VMEM((2, rows, size_y, size_z), F32),
            pltpu.VMEM((rows, size_y, size_z), F32),
            pltpu.VMEM((2, rows + 2 * REACH, size_y + 2 * PAD, size_z), F32),
            pltpu.VMEM((2, 2, size_y, size_z), F32),
            pltpu.SemaphoreType.DMA((rows // (2 * REACH), 5)),
        ],
        compiler_params=params(STEPS_MIB),
        cost_estimate=cost(2 * 10**10, 2**20),
        name="steps",
    )(source, receiver, source_before, receiver_before, courant, side, z_matrix(size_z))


def mend_kernel(
    left, right, near, far, partial, kept_courant, edge_courant, edge, side_in,
    ends, up, down, side_out, keep, give, added,
):
    gy, shot = lax.axis_index("gy"), lax.axis_index("shot")
    even = lax.axis_index("gx") % 2 == 0
    rows, lines, size_z = kept_courant.shape
    size_y = KEEP_EVERY * lines
    masks = z_weights(size_z)
    kept = lambda start: pl.ds(start, lines, stride=KEEP_EVERY)
    side_out[...] = side_in[...]
    for end in range(2):
        for field in range(2):
            group = 2 * end + field
            for row in range(REACH):
                blank_sides(added, row, group, size_y)
                for phase in range(KEEP_EVERY):
                    total = None
                    for d in range(row + 1, REACH + 1):
                        beyond = d - row - 1
                        at = beyond if end else REACH - 1 - beyond
                        if phase:
                            halo = (right if end else left)[field, at, (phase - 1) * lines : phase * lines, :]
                        elif end:
                            halo = jnp.where(even, near[field, at], far[field, at])
                        else:
                            halo = jnp.where(even, far[field, REACH + at], near[field, REACH + at])
                        term = WEIGHTS[d] * halo
                        total = term if total is None else total + term
                    scaled = edge_courant[end, row, pl.ds(phase, lines, stride=KEEP_EVERY), :]
                    added[group, row, kept(PAD + phase), :] = scaled * total
            for row in range(2 * REACH):
                at = rows - 1 - row if end else row
                total = None
                for other in range(REACH):
                    if 0 < abs(row - other) <= REACH:
                        term = WEIGHTS[abs(row - other)] * added[group, other, kept(PAD), :]
                        total = term if total is None else total + term
                value = partial[field, at]
                if row < REACH:
                    center = added[group, row, kept(PAD), :]
                    total = total + (3.0 * WEIGHTS[0]) * center + z_terms(center, masks)
                    for d in range(1, REACH + 1):
                        around = added[group, row, kept(PAD + d), :] + added[group, row, kept(PAD - d), :]
                        total = total + WEIGHTS[d] * around
                    value = value + 2.0 * center
                    first = edge[field, end, row] + center
                    if end:
                        up[field, REACH - 1 - row] = first
                    else:
                        down[field, row] = first
                    side_out[field, at : at + 1, :] = side_in[field, at : at + 1, :] + side_term(
                        added, row, group, size_y, gy
                    )
                ends[field, end, row] = value + kept_courant[at] * total
    for kind, ref in enumerate((near, far)):
        for field in range(2):
            for row in range(2 * REACH):
                pack_row(ref[field, row], field, row, shot, keep.at[kind], give.at[kind])


def mend(left, right, near, far, partial, kept_courant, edge_courant, edge, side_in):
    rows, lines, size_z = kept_courant.shape
    halo = jax.ShapeDtypeStruct((2, REACH, lines, size_z), F32)
    half = jax.ShapeDtypeStruct((2, 2, 2 * REACH, lines // 2, size_z), F32)
    return pl.pallas_call(
        mend_kernel,
        out_shape=(
            jax.ShapeDtypeStruct((2, 2, 2 * REACH, lines, size_z), F32),
            halo,
            halo,
            jax.ShapeDtypeStruct((2, rows, size_z), F32),
            half,
            half,
        ),
        in_specs=[VMEM] * 9,
        out_specs=(VMEM,) * 6,
        scratch_shapes=[pltpu.VMEM((4, REACH, KEEP_EVERY * lines + 2 * PAD, size_z), F32)],
        compiler_params=params(24),
        cost_estimate=cost(10**6, 2**20),
        name="mend",
    )(left, right, near, far, partial, kept_courant, edge_courant, edge, side_in)


def pack_row(value, field, row, shot, keep, give):
    first, second = z_halves(value)
    keep[field, row] = jnp.where(shot == 0, first, second)
    give[field, row] = jnp.where(shot == 0, second, first)


def side_lines(side, field, row, gy, lines):
    line = lax.broadcasted_iota(jnp.int32, (lines, side.shape[2]), 0)
    meets = line == jnp.where(gy == 0, lines - 1, 0)
    return jnp.where(meets, side[field, pl.ds(row, 1), :], 0.0)


def middle_kernel(partial, ends, kept_courant, side, keep, give):
    shot, gy = lax.axis_index("shot"), lax.axis_index("gy")
    rows, lines, _ = kept_courant.shape

    def one_row(row, values):
        for field in range(2):
            total = side_lines(side, field, row, gy, lines)
            pack_row(values[field] + kept_courant[row] * total, field, row - REACH, shot, keep, give)

    def middle(row, carry):
        one_row(row, [partial[field, row] for field in range(2)])
        return carry

    lax.fori_loop(2 * REACH, rows - 2 * REACH, middle, 0)
    for row in range(REACH, 2 * REACH):
        one_row(row, [ends[field, 0, row] for field in range(2)])
        one_row(rows - 1 - row, [ends[field, 1, row] for field in range(2)])


def finish_middle(partial, ends, kept_courant, side):
    rows, lines, size_z = kept_courant.shape
    half = jax.ShapeDtypeStruct((2, rows - 2 * REACH, lines // 2, size_z), F32)
    return pl.pallas_call(
        middle_kernel,
        out_shape=(half, half),
        in_specs=[VMEM] * 4,
        out_specs=(VMEM,) * 2,
        compiler_params=params(24),
        cost_estimate=cost(10**10, 3 * 2**20),
        name="finish_middle",
    )(partial, ends, kept_courant, side)


def ends_kernel(ends, kept_courant, left, right, side, keep, give):
    shot, gy = lax.axis_index("shot"), lax.axis_index("gy")
    rows, lines, _ = kept_courant.shape
    for field in range(2):
        for row in range(REACH):
            below = above = None
            for d in range(row + 1, REACH + 1):
                term = WEIGHTS[d] * left[field, REACH + row - d]
                below = term if below is None else below + term
                term = WEIGHTS[d] * right[field, d - 1 - row]
                above = term if above is None else above + term
            far = rows - 1 - row
            below = below + side_lines(side, field, row, gy, lines)
            above = above + side_lines(side, field, far, gy, lines)
            pack_row(ends[field, 0, row] + kept_courant[row] * below, field, row, shot, keep, give)
            pack_row(
                ends[field, 1, row] + kept_courant[far] * above,
                field, 2 * REACH - 1 - row, shot, keep, give,
            )


def finish_ends(ends, kept_courant, left, right, side):
    _, lines, size_z = kept_courant.shape
    half = jax.ShapeDtypeStruct((2, 2 * REACH, lines // 2, size_z), F32)
    return pl.pallas_call(
        ends_kernel,
        out_shape=(half, half),
        in_specs=[VMEM] * 5,
        out_specs=(VMEM,) * 2,
        compiler_params=params(24),
        cost_estimate=cost(10**10, 3 * 2**20),
        name="finish_ends",
    )(ends, kept_courant, left, right, side)


def block_starts(rows):
    even = lax.axis_index("gx") % 2 == 0
    return HALF, jnp.where(even, HALF + rows, 0), jnp.where(even, 0, HALF + rows)


def products(rows_of, sample, shift, here):
    total = None
    for group in range(rows_of.shape[0]):
        term = (
            rows_of[group, 0, 2 * HALF + sample - shift, here, :]
            * rows_of[group, 1, sample + shift, here, :]
        )
        total = term if total is None else total + term
    return total


def layout_copies(middles, ends, middle_starts, end_starts, rows_of, sems):
    copies = []

    def copy(src, part, start, count):
        dst = rows_of.at[part, :, pl.ds(start, count)]
        copies.append(pltpu.make_async_copy(src, dst, sems.at[len(copies)]))

    count = middles[0][0].shape[1]
    for part in range(2):
        for src, start in zip(middles[part], middle_starts):
            copy(src, part, start + REACH, count)
        for src, start in zip(ends[part], end_starts):
            copy(src.at[:, pl.ds(0, REACH)], part, start, REACH)
            copy(src.at[:, pl.ds(REACH, REACH)], part, start + REACH + count, REACH)
    return copies


def first_image_kernel(*refs):
    blocks, (out, rows_of, sems) = refs[:10], refs[10:]
    rows = blocks[0].shape[1] + 2 * REACH

    @pl.when(pl.program_id(0) == 0)
    def _():
        starts = block_starts(rows)
        ends = [[blocks[6 + part], blocks[8 + part].at[0], blocks[8 + part].at[1]] for part in range(2)]
        run_copies(layout_copies([blocks[:3], blocks[3:6]], ends, starts, starts, rows_of, sems))

    sample = 4 * pl.program_id(0)
    for chunk in range(rows_of.shape[3] // 8):
        here = pl.ds(8 * chunk, 8)
        for shift in range(OFFSETS):
            out[0, shift, here, :] = products(rows_of, sample, shift, here)


def first_image(blocks):
    _, middle_rows, lines, size_z = blocks[0].shape
    rows = middle_rows + 2 * REACH
    samples = rows // 4
    return pl.pallas_call(
        first_image_kernel,
        grid=(samples,),
        out_shape=jax.ShapeDtypeStruct((samples, OFFSETS, lines, size_z), F32),
        in_specs=[ANY] * len(blocks),
        out_specs=pl.BlockSpec((1, OFFSETS, lines, size_z), lambda i: (i, 0, 0, 0)),
        scratch_shapes=[
            pltpu.VMEM((2, 2, rows + 2 * HALF, lines, size_z), F32),
            pltpu.SemaphoreType.DMA((18,)),
        ],
        compiler_params=params(16),
        cost_estimate=cost(10**10, 8 * 2**20),
        name="first_image",
    )(*blocks)


def image_kernel(token, first, *refs):
    blocks, (out, rows_of, turned, staged, sems, out_sems) = refs[:9], refs[9:]
    rows = blocks[0].shape[1] + 2 * REACH
    step, steps_in_all = pl.program_id(0), pl.num_programs(0)

    @pl.when(step == 0)
    def _():
        ends = [[ref.at[part] for ref in blocks[6:]] for part in range(2)]
        end_starts = (HALF, 0, HALF + rows)
        run_copies(
            layout_copies([blocks[:3], blocks[3:6]], ends, block_starts(rows), end_starts, rows_of, sems)
        )

    lines, size_z = rows_of.shape[3], rows_of.shape[4]
    chunks = lines // 8

    def leave(at_step, chunk, half):
        slot = at_step % 2
        here = pl.ds(half * lines + 8 * chunk, 8)
        return pltpu.make_async_copy(staged.at[slot, here], out.at[at_step, here], out_sems.at[slot, chunk, half])

    sample = 4 * step
    for chunk in range(chunks):
        here = pl.ds(8 * chunk, 8)
        for shift in range(OFFSETS):
            total = first[0, shift, here, :] + products(rows_of, sample, shift, here)
            turned[chunk, pl.ds(shift, 8, stride=OFFSET_ROWS), :] = total

        @pl.when(step >= 2)
        def _():
            for half in range(2):
                leave(step - 2, chunk, half).wait()

        for line in range(8):
            values = turned[chunk, line * OFFSET_ROWS : (line + 1) * OFFSET_ROWS, :].T
            at = 8 * chunk + line
            staged[step % 2, at] = values[: size_z // 2, :OFFSETS]
            staged[step % 2, lines + at] = values[size_z // 2 :, :OFFSETS]
        for half in range(2):
            leave(step, chunk, half).start()

    @pl.when(step == steps_in_all - 1)
    def _():
        for back in (1, 0):
            for chunk in range(chunks):
                for half in range(2):
                    leave(step - back, chunk, half).wait()


def image(token, first, blocks):
    samples, _, lines, size_z = first.shape
    rows = 4 * samples
    return pl.pallas_call(
        image_kernel,
        grid=(samples,),
        out_shape=jax.ShapeDtypeStruct((samples, 2 * lines, size_z // 2, OFFSETS), F32),
        in_specs=[SMEM, pl.BlockSpec((1, OFFSETS, lines, size_z), lambda i: (i, 0, 0, 0))] + [ANY] * len(blocks),
        out_specs=HBM,
        scratch_shapes=[
            pltpu.VMEM((2, 2, rows + 2 * HALF, lines, size_z), F32),
            pltpu.VMEM((lines // 8, 8 * OFFSET_ROWS, size_z), F32),
            pltpu.VMEM((2, 2 * lines, size_z // 2, OFFSETS), F32),
            pltpu.SemaphoreType.DMA((18,)),
            pltpu.SemaphoreType.DMA((2, lines // 8, 2)),
        ],
        compiler_params=params(20),
        cost_estimate=cost(10**10, 16 * 2**20),
        name="image",
    )(token, first, *blocks)


def in_order_kernel(*refs):
    refs[-1][0] = 0


def in_order(*arrays):
    return pl.pallas_call(
        in_order_kernel,
        out_shape=jax.ShapeDtypeStruct((1,), jnp.int32),
        in_specs=[ANY] * len(arrays),
        out_specs=SMEM,
        compiler_params=params(1),
        cost_estimate=cost(1, 1),
        name="in_order",
    )(*arrays)


def on_device(source_now, source_before, receiver_now, receiver_before, courant):
    size = lax.axis_size("gx")
    up_pairs = [(i, i + 1) for i in range(size - 1)]
    down_pairs = [(j, i) for i, j in up_pairs]
    partner = [(i, i ^ 1) for i in range(size)]
    onward = [(i, i + 2) for i in range(0, size - 2, 2)] + [(i, i - 2) for i in range(3, size, 2)]
    both = [(0, 1), (1, 0)]

    def exchange(array, axis, pairs):
        return lax.ppermute(array, axis, pairs)

    barrier = lax.optimization_barrier
    up, down, edge, keep, keep_ends, give, give_ends, side = pack(source_now, receiver_now)
    near_edge = exchange(edge, "gx", partner)
    left = exchange(up, "gx", up_pairs)
    right = exchange(down, "gx", down_pairs)
    side = exchange(side, "gy", both)
    other = exchange(give, "shot", both)
    other_ends = exchange(give_ends, "shot", both)
    side, keep, other = barrier((side, keep, other))
    near_keep = exchange(keep, "gx", partner)
    near_other = exchange(other, "gx", partner)
    blocks = [keep, near_keep, None, other, near_other, None, keep_ends, other_ends]
    partial, kept_courant, edge_courant, edge, side = steps(
        source_now, receiver_now, source_before, receiver_before, courant, side
    )
    near_edge, side = barrier((near_edge, side))
    far_edge = exchange(near_edge, "gx", onward)
    ends, up, down, side, keep_edges, give_edges = mend(
        left, right, near_edge, far_edge, partial, kept_courant, edge_courant, edge, side
    )
    blocks += [keep_edges, exchange(give_edges, "shot", both)]
    left = exchange(up, "gx", up_pairs)
    right = exchange(down, "gx", down_pairs)
    side = exchange(side, "gy", both)
    side, near_keep, near_other, blocks[7], blocks[9] = barrier((side, near_keep, near_other, blocks[7], blocks[9]))
    far_keep = exchange(near_keep, "gx", onward)

    keep, give = finish_middle(partial, ends, kept_courant, side)
    blocks[5] = exchange(near_other, "gx", onward)
    other = exchange(give, "shot", both)
    near_keep = exchange(keep, "gx", partner)

    left, right, blocks[2] = barrier((left, right, far_keep))
    keep_ends, give_ends = finish_ends(ends, kept_courant, left, right, side)
    other, keep_ends, give_ends = barrier((other, keep_ends, give_ends))
    near_other = exchange(other, "gx", partner)
    other_ends = exchange(give_ends, "shot", both)
    other_ends, near_keep = barrier((other_ends, near_keep))
    own = jnp.stack([keep_ends, other_ends])
    far_keep = exchange(near_keep, "gx", onward)
    left = exchange(own, "gx", up_pairs)
    right = exchange(own, "gx", down_pairs)
    far_other = exchange(near_other, "gx", onward)
    blocks[5], far_keep = lax.optimization_barrier((blocks[5], far_keep))
    first = first_image(blocks)
    token = in_order(left, right, first)
    blocks = [keep, near_keep, far_keep, other, near_other, far_other, own, left, right]
    return jnp.transpose(image(token, first, blocks), (3, 0, 1, 2))


def solution(mesh):
    in_specs = (
        P("shot", "gx", "gy", None),
        P("shot", "gx", "gy", None),
        P("shot", "gx", "gy", None),
        P("shot", "gx", "gy", None),
        P("gx", "gy", None),
    )
    out_specs = P(None, "gx", "gy", "shot")
    return jax.shard_map(
        on_device, mesh=mesh, in_specs=in_specs, out_specs=out_specs, check_vma=False
    )
```

```python
import functools

import jax
import jax.numpy as jnp
import numpy as np
from jax import lax
from jax.experimental import pallas as pl
from jax.experimental.pallas import tpu as pltpu
from jax.sharding import PartitionSpec as P

HALF = 32
REACH = 4
KEEP_EVERY = 4
OFFSETS = 2 * HALF + 1
OFFSET_ROWS = 72
LINES = 32
STEPS_MIB = 50
WEIGHTS = (-205.0 / 72.0, 8.0 / 5.0, -1.0 / 5.0, 8.0 / 315.0, -1.0 / 560.0)
PAD = 8
F32 = jnp.float32
HBM = pl.BlockSpec(memory_space=pltpu.HBM)
ANY = pl.BlockSpec(memory_space=pl.ANY)
VMEM = pl.BlockSpec(memory_space=pltpu.VMEM)
SMEM = pl.BlockSpec(memory_space=pltpu.SMEM)


def params(mib):
    return pltpu.CompilerParams(vmem_limit_bytes=mib * 2**20)


def cost(flops, nbytes):
    return pl.CostEstimate(flops=flops, bytes_accessed=nbytes, transcendentals=0)


def run_copies(copies):
    for copy in copies:
        copy.start()
    for copy in copies:
        copy.wait()


def z_halves(lines):
    count, size_z = lines.shape
    top, bottom = lines[: count // 2], lines[count // 2 :]
    low = lax.broadcasted_iota(jnp.int32, top.shape, 1) < size_z // 2
    first = jnp.where(low, top, pltpu.roll(bottom, size_z // 2, 1))
    second = jnp.where(low, pltpu.roll(top, size_z // 2, 1), bottom)
    return first, second


def pack_kernel(
    source, receiver, up, down, edge, keep, keep_ends, give, give_ends, side, fields, sems
):
    shot, gy = lax.axis_index("shot"), lax.axis_index("gy")
    _, rows, size_y, _ = fields.shape
    lines = size_y // KEEP_EVERY
    pieces = sems.shape[0]
    count = rows // pieces
    order = [0, pieces - 1] + list(range(1, pieces - 1))
    copies = {}
    for index in order:
        part = pl.ds(count * index, count)
        for field, ref in enumerate((source, receiver)):
            copies[index, field] = pltpu.make_async_copy(
                ref.at[0, part], fields.at[field, part], sems.at[index, field]
            )
            copies[index, field].start()

    def one_row(row, keep_ref, give_ref, to):
        parts = []
        for field in range(2):
            first, second = z_halves(fields[field, row, pl.ds(0, lines, stride=KEEP_EVERY), :])
            keep_ref[field, to] = jnp.where(shot == 0, first, second)
            give_ref[field, to] = jnp.where(shot == 0, second, first)
            low = fields[field, row, 0:REACH, :]
            high = fields[field, row, size_y - REACH : size_y, :]
            parts.append(jnp.where(gy == 0, high, low))
        side[row] = jnp.concatenate(parts, axis=0)

    def middle_row(row, carry):
        one_row(row, keep, give, row - REACH)
        return carry

    def end_rows(out, start, to):
        for row in range(REACH):
            for field in range(2):
                edge[field, to + row] = fields[field, start + row, pl.ds(0, lines, stride=KEEP_EVERY), :]
                for phase in range(1, KEEP_EVERY):
                    out[field, row, (phase - 1) * lines : phase * lines, :] = fields[
                        field, start + row, pl.ds(phase, lines, stride=KEEP_EVERY), :
                    ]
            one_row(start + row, keep_ends, give_ends, to + row)

    for index in order:
        for field in range(2):
            copies[index, field].wait()
        low, high = count * index, count * (index + 1)
        if index == 0:
            end_rows(down, 0, 0)
            low += REACH
        if index == pieces - 1:
            end_rows(up, rows - REACH, REACH)
            high -= REACH
        lax.fori_loop(low, high, middle_row, 0, unroll=4)


def pack(source, receiver):
    _, rows, size_y, size_z = source.shape
    lines = size_y // KEEP_EVERY
    apart = jax.ShapeDtypeStruct((2, REACH, size_y - lines, size_z), F32)
    middle = jax.ShapeDtypeStruct((2, rows - 2 * REACH, lines // 2, size_z), F32)
    ends = jax.ShapeDtypeStruct((2, 2 * REACH, lines // 2, size_z), F32)
    return pl.pallas_call(
        pack_kernel,
        out_shape=(
            apart,
            apart,
            jax.ShapeDtypeStruct((2, 2 * REACH, lines, size_z), F32),
            middle,
            ends,
            middle,
            ends,
            jax.ShapeDtypeStruct((rows, 2 * REACH, size_z), F32),
        ),
        in_specs=[HBM, HBM],
        out_specs=(VMEM,) * 8,
        scratch_shapes=[
            pltpu.VMEM((2, rows, size_y, size_z), F32),
            pltpu.SemaphoreType.DMA((4, 2)),
        ],
        compiler_params=params(56),
        cost_estimate=cost(10**10, 7 * 2**20),
        name="pack",
    )(source, receiver)


def z_weights(size_z):
    z = lax.broadcasted_iota(jnp.int32, (8, size_z), 1)
    return [
        (jnp.where(z >= d, WEIGHTS[d], 0.0), jnp.where(z < size_z - d, WEIGHTS[d], 0.0))
        for d in range(1, REACH + 1)
    ]


def z_terms(center, masks):
    size_z = center.shape[1]
    center = center.reshape(-1, 8, size_z)
    total = None
    for d, (below, above) in enumerate(masks, start=1):
        term = below * pltpu.roll(center, d, 2) + above * pltpu.roll(center, size_z - d, 2)
        total = term if total is None else total + term
    return total.reshape(-1, size_z)


def z_matrix(size_z):
    z = np.arange(size_z)
    apart = np.abs(z[:, None] - z[None, :])
    weights = np.array((0.0,) + WEIGHTS[1:] + (0.0,), np.float32)[np.minimum(apart, REACH + 1)]
    high = weights.astype(jnp.bfloat16)
    low = (weights - high.astype(np.float32)).astype(jnp.bfloat16)
    return jnp.asarray(np.block([[high, low], [high, np.zeros_like(low)]]))


def z_product(lines, matrix):
    size_z = lines.shape[1]
    high = lines.astype(jnp.bfloat16)
    low = (lines - high.astype(F32)).astype(jnp.bfloat16)
    both = jnp.dot(jnp.concatenate([high, low], axis=1), matrix, preferred_element_type=F32)
    return both[:, :size_z] + both[:, size_z:]


def first_step(now, row, z_sums, before, before_row, scale, scale_row, after, field):
    size_y = before.shape[2]
    lines = size_y // KEEP_EVERY
    for phase in range(KEEP_EVERY):
        kept = lambda start: pl.ds(start, lines, stride=KEEP_EVERY)
        at = PAD + phase
        center = now[field, row, kept(at), :]
        total = (3.0 * WEIGHTS[0]) * center + z_sums[field, kept(phase), :]
        for d in range(1, REACH + 1):
            around = (
                now[field, row + d, kept(at), :]
                + now[field, row - d, kept(at), :]
                + now[field, row, kept(at + d), :]
                + now[field, row, kept(at - d), :]
            )
            total = total + WEIGHTS[d] * around
        after[field, row, kept(at), :] = (
            2.0 * center
            - before[field, before_row, kept(phase), :]
            + scale[scale_row, kept(phase), :] * total
        )


def second_step(now, row, scale, scale_row, after, field, z_sum):
    size_y = scale.shape[1]
    lines = size_y // KEEP_EVERY
    kept = lambda start: pl.ds(start, lines, stride=KEEP_EVERY)
    center = after[field, row, kept(PAD), :]
    total = (3.0 * WEIGHTS[0]) * center + z_sum
    for d in range(1, REACH + 1):
        around = (
            after[field, row + d, kept(PAD), :]
            + after[field, row - d, kept(PAD), :]
            + after[field, row, kept(PAD + d), :]
            + after[field, row, kept(PAD - d), :]
        )
        total = total + WEIGHTS[d] * around
    return 2.0 * center - now[field, row, kept(PAD), :] + scale[scale_row, kept(0), :] * total


def side_term(after, after_row, field, size_y, gy):
    lowest = WEIGHTS[REACH] * after[field, after_row, PAD : PAD + 1, :]
    highest = sum(
        WEIGHTS[d] * after[field, after_row, PAD + size_y - d : PAD + size_y - d + 1, :]
        for d in range(1, REACH + 1)
    )
    return jnp.where(gy == 0, highest, lowest)


def fill_sides(now, row, got, field, size_y, gy):
    blank = jnp.zeros_like(got)
    now[field, row, PAD - REACH : PAD, :] = jnp.where(gy == 0, blank, got)
    now[field, row, size_y + PAD : size_y + PAD + REACH, :] = jnp.where(gy == 0, got, blank)


def blank_sides(after, row, field, size_y):
    blank = jnp.zeros((REACH, after.shape[3]), F32)
    after[field, row, PAD - REACH : PAD, :] = blank
    after[field, row, size_y + PAD : size_y + PAD + REACH, :] = blank


def steps_kernel(
    source, receiver, source_before, receiver_before, courant, side, matrix,
    partial, kept_courant, edge_courant, edge, side_out, now, before, scale, after, z_sums, sems,
):
    gy = lax.axis_index("gy")
    rows, size_y, size_z = courant.shape
    lines = size_y // KEEP_EVERY
    piece = 2 * REACH
    middle = pl.ds(PAD, size_y)

    def copies(index):
        part = pl.ds(piece * index, piece)
        found = []
        for field in range(2):
            src = (source, receiver)[field].at[0, part]
            dst = now.at[field, pl.ds(REACH + piece * index, piece), middle]
            found.append(pltpu.make_async_copy(src, dst, sems.at[index, field]))
        for field in range(2):
            src = (source_before, receiver_before)[field].at[0, part]
            found.append(pltpu.make_async_copy(src, before.at[field, part], sems.at[index, 2 + field]))
        found.append(pltpu.make_async_copy(courant.at[part], scale.at[part], sems.at[index, 4]))
        return found

    for index in range(rows // piece):
        for one in copies(index):
            one.start()

    for field in range(2):
        for row in list(range(REACH)) + list(range(rows + REACH, rows + 2 * REACH)):
            now[field, row] = jnp.zeros((size_y + 2 * PAD, size_z), F32)
            after[field, row] = jnp.zeros((size_y + 2 * PAD, size_z), F32)

    def fill(row, carry):
        for field in range(2):
            got = side[row, field * REACH : (field + 1) * REACH, :]
            fill_sides(now, row + REACH, got, field, size_y, gy)
            blank_sides(after, row + REACH, field, size_y)
        return carry

    lax.fori_loop(0, rows, fill, 0)
    for one in copies(0)[:2]:
        one.wait()

    def z_next(row):
        found = z_product(
            jnp.concatenate([now[field, row + REACH, middle, :] for field in range(2)], axis=0), matrix[...]
        )
        for field in range(2):
            z_sums[row % 2, field] = found[field * size_y : (field + 1) * size_y]

    z_next(0)

    def first(row, carry):
        @pl.when(row % piece == 0)
        def _():
            index = row // piece
            for one in copies(index)[2:]:
                one.wait()

            @pl.when(index + 1 < rows // piece)
            def _():
                for one in copies(index + 1)[:2]:
                    one.wait()

        at = row + REACH
        for field in range(2):
            first_step(now, at, z_sums.at[row % 2], before, row, scale, row, after, field)
        z_next(row + 1)
        for field in range(2):
            side_out[field, pl.ds(row, 1), :] = side_term(after, at, field, size_y, gy)
        return carry

    lax.fori_loop(0, rows, first, 0)

    def second(row, carry):
        at = row + REACH
        kept_courant[row] = scale[row, pl.ds(0, lines, stride=KEEP_EVERY), :]
        centers = [after[field, at, pl.ds(PAD, lines, stride=KEEP_EVERY), :] for field in range(2)]
        z_sum = z_product(jnp.concatenate(centers, axis=0), matrix[...])
        for field in range(2):
            partial[field, row] = second_step(
                now, at, scale, row, after, field, z_sum[field * lines : (field + 1) * lines]
            )
        return carry

    lax.fori_loop(0, rows, second, 0, unroll=2)
    for end in range(2):
        for row in range(REACH):
            at = rows - 1 - row if end else row
            edge_courant[end, row] = scale[at]
            for field in range(2):
                edge[field, end, row] = after[field, REACH + at, pl.ds(PAD, lines, stride=KEEP_EVERY), :]


def steps(source, receiver, source_before, receiver_before, courant, side):
    rows, size_y, size_z = courant.shape
    lines = size_y // KEEP_EVERY
    return pl.pallas_call(
        steps_kernel,
        out_shape=(
            jax.ShapeDtypeStruct((2, rows, lines, size_z), F32),
            jax.ShapeDtypeStruct((rows, lines, size_z), F32),
            jax.ShapeDtypeStruct((2, REACH, size_y, size_z), F32),
            jax.ShapeDtypeStruct((2, 2, REACH, lines, size_z), F32),
            jax.ShapeDtypeStruct((2, rows, size_z), F32),
        ),
        in_specs=[HBM] * 5 + [VMEM] * 2,
        out_specs=(VMEM,) * 5,
        scratch_shapes=[
            pltpu.VMEM((2, rows + 2 * REACH, size_y + 2 * PAD, size_z), F32),
            pltpu.VMEM((2, rows, size_y, size_z), F32),
            pltpu.VMEM((rows, size_y, size_z), F32),
            pltpu.VMEM((2, rows + 2 * REACH, size_y + 2 * PAD, size_z), F32),
            pltpu.VMEM((2, 2, size_y, size_z), F32),
            pltpu.SemaphoreType.DMA((rows // (2 * REACH), 5)),
        ],
        compiler_params=params(STEPS_MIB),
        cost_estimate=cost(2 * 10**10, 2**20),
        name="steps",
    )(source, receiver, source_before, receiver_before, courant, side, z_matrix(size_z))


def mend_kernel(
    left, right, near, far, partial, kept_courant, edge_courant, edge, side_in,
    ends, up, down, side_out, keep, give, added,
):
    gy, shot = lax.axis_index("gy"), lax.axis_index("shot")
    even = lax.axis_index("gx") % 2 == 0
    rows, lines, size_z = kept_courant.shape
    size_y = KEEP_EVERY * lines
    masks = z_weights(size_z)
    kept = lambda start: pl.ds(start, lines, stride=KEEP_EVERY)
    side_out[...] = side_in[...]
    for end in range(2):
        for field in range(2):
            group = 2 * end + field
            for row in range(REACH):
                blank_sides(added, row, group, size_y)
                for phase in range(KEEP_EVERY):
                    total = None
                    for d in range(row + 1, REACH + 1):
                        beyond = d - row - 1
                        at = beyond if end else REACH - 1 - beyond
                        if phase:
                            halo = (right if end else left)[field, at, (phase - 1) * lines : phase * lines, :]
                        elif end:
                            halo = jnp.where(even, near[field, at], far[field, at])
                        else:
                            halo = jnp.where(even, far[field, REACH + at], near[field, REACH + at])
                        term = WEIGHTS[d] * halo
                        total = term if total is None else total + term
                    scaled = edge_courant[end, row, pl.ds(phase, lines, stride=KEEP_EVERY), :]
                    added[group, row, kept(PAD + phase), :] = scaled * total
            for row in range(2 * REACH):
                at = rows - 1 - row if end else row
                total = None
                for other in range(REACH):
                    if 0 < abs(row - other) <= REACH:
                        term = WEIGHTS[abs(row - other)] * added[group, other, kept(PAD), :]
                        total = term if total is None else total + term
                value = partial[field, at]
                if row < REACH:
                    center = added[group, row, kept(PAD), :]
                    total = total + (3.0 * WEIGHTS[0]) * center + z_terms(center, masks)
                    for d in range(1, REACH + 1):
                        around = added[group, row, kept(PAD + d), :] + added[group, row, kept(PAD - d), :]
                        total = total + WEIGHTS[d] * around
                    value = value + 2.0 * center
                    first = edge[field, end, row] + center
                    if end:
                        up[field, REACH - 1 - row] = first
                    else:
                        down[field, row] = first
                    side_out[field, at : at + 1, :] = side_in[field, at : at + 1, :] + side_term(
                        added, row, group, size_y, gy
                    )
                ends[field, end, row] = value + kept_courant[at] * total
    for kind, ref in enumerate((near, far)):
        for field in range(2):
            for row in range(2 * REACH):
                pack_row(ref[field, row], field, row, shot, keep.at[kind], give.at[kind])


def mend(left, right, near, far, partial, kept_courant, edge_courant, edge, side_in):
    rows, lines, size_z = kept_courant.shape
    halo = jax.ShapeDtypeStruct((2, REACH, lines, size_z), F32)
    half = jax.ShapeDtypeStruct((2, 2, 2 * REACH, lines // 2, size_z), F32)
    return pl.pallas_call(
        mend_kernel,
        out_shape=(
            jax.ShapeDtypeStruct((2, 2, 2 * REACH, lines, size_z), F32),
            halo,
            halo,
            jax.ShapeDtypeStruct((2, rows, size_z), F32),
            half,
            half,
        ),
        in_specs=[VMEM] * 9,
        out_specs=(VMEM,) * 6,
        scratch_shapes=[pltpu.VMEM((4, REACH, KEEP_EVERY * lines + 2 * PAD, size_z), F32)],
        compiler_params=params(24),
        cost_estimate=cost(10**6, 2**20),
        name="mend",
    )(left, right, near, far, partial, kept_courant, edge_courant, edge, side_in)


def pack_row(value, field, row, shot, keep, give):
    first, second = z_halves(value)
    keep[field, row] = jnp.where(shot == 0, first, second)
    give[field, row] = jnp.where(shot == 0, second, first)


def side_lines(side, field, row, gy, lines):
    line = lax.broadcasted_iota(jnp.int32, (lines, side.shape[2]), 0)
    meets = line == jnp.where(gy == 0, lines - 1, 0)
    return jnp.where(meets, side[field, pl.ds(row, 1), :], 0.0)


def middle_kernel(partial, ends, kept_courant, side, keep, give):
    shot, gy = lax.axis_index("shot"), lax.axis_index("gy")
    rows, lines, _ = kept_courant.shape

    def one_row(row, values):
        for field in range(2):
            total = side_lines(side, field, row, gy, lines)
            pack_row(values[field] + kept_courant[row] * total, field, row - REACH, shot, keep, give)

    def middle(row, carry):
        one_row(row, [partial[field, row] for field in range(2)])
        return carry

    lax.fori_loop(2 * REACH, rows - 2 * REACH, middle, 0)
    for row in range(REACH, 2 * REACH):
        one_row(row, [ends[field, 0, row] for field in range(2)])
        one_row(rows - 1 - row, [ends[field, 1, row] for field in range(2)])


def finish_middle(partial, ends, kept_courant, side):
    rows, lines, size_z = kept_courant.shape
    half = jax.ShapeDtypeStruct((2, rows - 2 * REACH, lines // 2, size_z), F32)
    return pl.pallas_call(
        middle_kernel,
        out_shape=(half, half),
        in_specs=[VMEM] * 4,
        out_specs=(VMEM,) * 2,
        compiler_params=params(24),
        cost_estimate=cost(1, 1),
        name="finish_middle",
    )(partial, ends, kept_courant, side)


def ends_kernel(ends, kept_courant, left, right, side, keep, give):
    shot, gy = lax.axis_index("shot"), lax.axis_index("gy")
    rows, lines, _ = kept_courant.shape
    for field in range(2):
        for row in range(REACH):
            below = above = None
            for d in range(row + 1, REACH + 1):
                term = WEIGHTS[d] * left[field, REACH + row - d]
                below = term if below is None else below + term
                term = WEIGHTS[d] * right[field, d - 1 - row]
                above = term if above is None else above + term
            far = rows - 1 - row
            below = below + side_lines(side, field, row, gy, lines)
            above = above + side_lines(side, field, far, gy, lines)
            pack_row(ends[field, 0, row] + kept_courant[row] * below, field, row, shot, keep, give)
            pack_row(
                ends[field, 1, row] + kept_courant[far] * above,
                field, 2 * REACH - 1 - row, shot, keep, give,
            )


def finish_ends(ends, kept_courant, left, right, side):
    _, lines, size_z = kept_courant.shape
    half = jax.ShapeDtypeStruct((2, 2 * REACH, lines // 2, size_z), F32)
    return pl.pallas_call(
        ends_kernel,
        out_shape=(half, half),
        in_specs=[VMEM] * 5,
        out_specs=(VMEM,) * 2,
        compiler_params=params(24),
        cost_estimate=cost(10**10, 3 * 2**20),
        name="finish_ends",
    )(ends, kept_courant, left, right, side)


def block_starts(rows):
    even = lax.axis_index("gx") % 2 == 0
    return HALF, jnp.where(even, HALF + rows, 0), jnp.where(even, 0, HALF + rows)


def products(rows_of, sample, shift, here):
    total = None
    for group in range(rows_of.shape[0]):
        term = (
            rows_of[group, 0, 2 * HALF + sample - shift, here, :]
            * rows_of[group, 1, sample + shift, here, :]
        )
        total = term if total is None else total + term
    return total


def layout_copies(middles, ends, middle_starts, end_starts, rows_of, sems):
    copies = []

    def copy(src, part, start, count):
        dst = rows_of.at[part, :, pl.ds(start, count)]
        copies.append(pltpu.make_async_copy(src, dst, sems.at[len(copies)]))

    count = middles[0][0].shape[1]
    for part in range(2):
        for src, start in zip(middles[part], middle_starts):
            copy(src, part, start + REACH, count)
        for src, start in zip(ends[part], end_starts):
            copy(src.at[:, pl.ds(0, REACH)], part, start, REACH)
            copy(src.at[:, pl.ds(REACH, REACH)], part, start + REACH + count, REACH)
    return copies


def first_image_kernel(*refs):
    blocks, (out, rows_of, sems) = refs[:10], refs[10:]
    rows = blocks[0].shape[1] + 2 * REACH

    @pl.when(pl.program_id(0) == 0)
    def _():
        starts = block_starts(rows)
        ends = [[blocks[6 + part], blocks[8 + part].at[0], blocks[8 + part].at[1]] for part in range(2)]
        run_copies(layout_copies([blocks[:3], blocks[3:6]], ends, starts, starts, rows_of, sems))

    sample = 4 * pl.program_id(0)
    for chunk in range(rows_of.shape[3] // 8):
        here = pl.ds(8 * chunk, 8)
        for shift in range(OFFSETS):
            out[0, shift, here, :] = products(rows_of, sample, shift, here)


def first_image(blocks):
    _, middle_rows, lines, size_z = blocks[0].shape
    rows = middle_rows + 2 * REACH
    samples = rows // 4
    return pl.pallas_call(
        first_image_kernel,
        grid=(samples,),
        out_shape=jax.ShapeDtypeStruct((samples, OFFSETS, lines, size_z), F32),
        in_specs=[ANY] * len(blocks),
        out_specs=pl.BlockSpec((1, OFFSETS, lines, size_z), lambda i: (i, 0, 0, 0)),
        scratch_shapes=[
            pltpu.VMEM((2, 2, rows + 2 * HALF, lines, size_z), F32),
            pltpu.SemaphoreType.DMA((18,)),
        ],
        compiler_params=params(16),
        cost_estimate=cost(10**10, 8 * 2**20),
        name="first_image",
    )(*blocks)


def image_kernel(token, first, *refs):
    blocks, (out, rows_of, turned, staged, sems, out_sems) = refs[:9], refs[9:]
    rows = blocks[0].shape[1] + 2 * REACH
    step, steps_in_all = pl.program_id(0), pl.num_programs(0)

    @pl.when(step == 0)
    def _():
        ends = [[ref.at[part] for ref in blocks[6:]] for part in range(2)]
        end_starts = (HALF, 0, HALF + rows)
        run_copies(
            layout_copies([blocks[:3], blocks[3:6]], ends, block_starts(rows), end_starts, rows_of, sems)
        )

    lines, size_z = rows_of.shape[3], rows_of.shape[4]
    chunks = lines // 8

    def leave(at_step, chunk, half):
        slot = at_step % 2
        here = pl.ds(half * lines + 8 * chunk, 8)
        return pltpu.make_async_copy(staged.at[slot, here], out.at[at_step, here], out_sems.at[slot, chunk, half])

    sample = 4 * step
    for chunk in range(chunks):
        here = pl.ds(8 * chunk, 8)
        for shift in range(OFFSETS):
            total = first[0, shift, here, :] + products(rows_of, sample, shift, here)
            turned[chunk, pl.ds(shift, 8, stride=OFFSET_ROWS), :] = total

        @pl.when(step >= 2)
        def _():
            for half in range(2):
                leave(step - 2, chunk, half).wait()

        for line in range(8):
            values = turned[chunk, line * OFFSET_ROWS : (line + 1) * OFFSET_ROWS, :].T
            at = 8 * chunk + line
            staged[step % 2, at] = values[: size_z // 2, :OFFSETS]
            staged[step % 2, lines + at] = values[size_z // 2 :, :OFFSETS]
        for half in range(2):
            leave(step, chunk, half).start()

    @pl.when(step == steps_in_all - 1)
    def _():
        for back in (1, 0):
            for chunk in range(chunks):
                for half in range(2):
                    leave(step - back, chunk, half).wait()


def image(token, first, blocks):
    samples, _, lines, size_z = first.shape
    rows = 4 * samples
    return pl.pallas_call(
        image_kernel,
        grid=(samples,),
        out_shape=jax.ShapeDtypeStruct((samples, 2 * lines, size_z // 2, OFFSETS), F32),
        in_specs=[SMEM, pl.BlockSpec((1, OFFSETS, lines, size_z), lambda i: (i, 0, 0, 0))] + [ANY] * len(blocks),
        out_specs=HBM,
        scratch_shapes=[
            pltpu.VMEM((2, 2, rows + 2 * HALF, lines, size_z), F32),
            pltpu.VMEM((lines // 8, 8 * OFFSET_ROWS, size_z), F32),
            pltpu.VMEM((2, 2 * lines, size_z // 2, OFFSETS), F32),
            pltpu.SemaphoreType.DMA((18,)),
            pltpu.SemaphoreType.DMA((2, lines // 8, 2)),
        ],
        compiler_params=params(20),
        cost_estimate=cost(10**10, 16 * 2**20),
        name="image",
    )(token, first, *blocks)


def in_order_kernel(*refs):
    refs[-1][0] = 0


def in_order(*arrays):
    return pl.pallas_call(
        in_order_kernel,
        out_shape=jax.ShapeDtypeStruct((1,), jnp.int32),
        in_specs=[ANY] * len(arrays),
        out_specs=SMEM,
        compiler_params=params(1),
        cost_estimate=cost(1, 1),
        name="in_order",
    )(*arrays)


def on_device(source_now, source_before, receiver_now, receiver_before, courant):
    size = lax.axis_size("gx")
    up_pairs = [(i, i + 1) for i in range(size - 1)]
    down_pairs = [(j, i) for i, j in up_pairs]
    partner = [(i, i ^ 1) for i in range(size)]
    onward = [(i, i + 2) for i in range(0, size - 2, 2)] + [(i, i - 2) for i in range(3, size, 2)]
    both = [(0, 1), (1, 0)]

    def exchange(array, axis, pairs):
        return lax.ppermute(array, axis, pairs)

    barrier = lax.optimization_barrier
    up, down, edge, keep, keep_ends, give, give_ends, side = pack(source_now, receiver_now)
    near_edge = exchange(edge, "gx", partner)
    left = exchange(up, "gx", up_pairs)
    right = exchange(down, "gx", down_pairs)
    side = exchange(side, "gy", both)
    other = exchange(give, "shot", both)
    other_ends = exchange(give_ends, "shot", both)
    side, keep, other = barrier((side, keep, other))
    near_keep = exchange(keep, "gx", partner)
    near_other = exchange(other, "gx", partner)
    blocks = [keep, near_keep, None, other, near_other, None, keep_ends, other_ends]
    partial, kept_courant, edge_courant, edge, side = steps(
        source_now, receiver_now, source_before, receiver_before, courant, side
    )
    near_edge, side = barrier((near_edge, side))
    far_edge = exchange(near_edge, "gx", onward)
    ends, up, down, side, keep_edges, give_edges = mend(
        left, right, near_edge, far_edge, partial, kept_courant, edge_courant, edge, side
    )
    blocks += [keep_edges, exchange(give_edges, "shot", both)]
    left = exchange(up, "gx", up_pairs)
    right = exchange(down, "gx", down_pairs)
    side = exchange(side, "gy", both)
    side, near_keep, blocks[7], blocks[9] = barrier((side, near_keep, blocks[7], blocks[9]))
    far_keep = exchange(near_keep, "gx", onward)

    keep, give = finish_middle(partial, ends, kept_courant, side)
    other = exchange(give, "shot", both)
    near_keep = exchange(keep, "gx", partner)

    left, right, blocks[2], blocks[4] = barrier((left, right, far_keep, near_other))
    blocks[5] = exchange(blocks[4], "gx", onward)
    keep_ends, give_ends = finish_ends(ends, kept_courant, left, right, side)
    other, keep_ends, give_ends = barrier((other, keep_ends, give_ends))
    near_other = exchange(other, "gx", partner)
    other_ends = exchange(give_ends, "shot", both)
    other_ends, near_keep = barrier((other_ends, near_keep))
    own = jnp.stack([keep_ends, other_ends])
    far_keep = exchange(near_keep, "gx", onward)
    left = exchange(own, "gx", up_pairs)
    right = exchange(own, "gx", down_pairs)
    far_other = exchange(near_other, "gx", onward)
    blocks[5], far_keep = lax.optimization_barrier((blocks[5], far_keep))
    first = first_image(blocks)
    token = in_order(left, right, first)
    blocks = [keep, near_keep, far_keep, other, near_other, far_other, own, left, right]
    return jnp.transpose(image(token, first, blocks), (3, 0, 1, 2))


def solution(mesh):
    in_specs = (
        P("shot", "gx", "gy", None),
        P("shot", "gx", "gy", None),
        P("shot", "gx", "gy", None),
        P("shot", "gx", "gy", None),
        P("gx", "gy", None),
    )
    out_specs = P(None, "gx", "gy", "shot")
    return jax.shard_map(
        on_device, mesh=mesh, in_specs=in_specs, out_specs=out_specs, check_vma=False
    )
```

```python
import functools

import jax
import jax.numpy as jnp
import numpy as np
from jax import lax
from jax.experimental import pallas as pl
from jax.experimental.pallas import tpu as pltpu
from jax.sharding import PartitionSpec as P

HALF = 32
REACH = 4
KEEP_EVERY = 4
OFFSETS = 2 * HALF + 1
OFFSET_ROWS = 72
LINES = 32
STEPS_MIB = 50
WEIGHTS = (-205.0 / 72.0, 8.0 / 5.0, -1.0 / 5.0, 8.0 / 315.0, -1.0 / 560.0)
PAD = 8
F32 = jnp.float32
HBM = pl.BlockSpec(memory_space=pltpu.HBM)
ANY = pl.BlockSpec(memory_space=pl.ANY)
VMEM = pl.BlockSpec(memory_space=pltpu.VMEM)
SMEM = pl.BlockSpec(memory_space=pltpu.SMEM)


def params(mib):
    return pltpu.CompilerParams(vmem_limit_bytes=mib * 2**20)


def cost(flops, nbytes):
    return pl.CostEstimate(flops=flops, bytes_accessed=nbytes, transcendentals=0)


def run_copies(copies):
    for copy in copies:
        copy.start()
    for copy in copies:
        copy.wait()


def z_halves(lines):
    count, size_z = lines.shape
    top, bottom = lines[: count // 2], lines[count // 2 :]
    low = lax.broadcasted_iota(jnp.int32, top.shape, 1) < size_z // 2
    first = jnp.where(low, top, pltpu.roll(bottom, size_z // 2, 1))
    second = jnp.where(low, pltpu.roll(top, size_z // 2, 1), bottom)
    return first, second


def pack_kernel(
    source, receiver, up, down, edge, keep, keep_ends, give, give_ends, side, fields, sems
):
    shot, gy = lax.axis_index("shot"), lax.axis_index("gy")
    _, rows, size_y, _ = fields.shape
    lines = size_y // KEEP_EVERY
    pieces = sems.shape[0]
    count = rows // pieces
    order = [0, pieces - 1] + list(range(1, pieces - 1))
    copies = {}
    for index in order:
        part = pl.ds(count * index, count)
        for field, ref in enumerate((source, receiver)):
            copies[index, field] = pltpu.make_async_copy(
                ref.at[0, part], fields.at[field, part], sems.at[index, field]
            )
            copies[index, field].start()

    def one_row(row, keep_ref, give_ref, to):
        parts = []
        for field in range(2):
            first, second = z_halves(fields[field, row, pl.ds(0, lines, stride=KEEP_EVERY), :])
            keep_ref[field, to] = jnp.where(shot == 0, first, second)
            give_ref[field, to] = jnp.where(shot == 0, second, first)
            low = fields[field, row, 0:REACH, :]
            high = fields[field, row, size_y - REACH : size_y, :]
            parts.append(jnp.where(gy == 0, high, low))
        side[row] = jnp.concatenate(parts, axis=0)

    def middle_row(row, carry):
        one_row(row, keep, give, row - REACH)
        return carry

    def end_rows(out, start, to):
        for row in range(REACH):
            for field in range(2):
                edge[field, to + row] = fields[field, start + row, pl.ds(0, lines, stride=KEEP_EVERY), :]
                for phase in range(1, KEEP_EVERY):
                    out[field, row, (phase - 1) * lines : phase * lines, :] = fields[
                        field, start + row, pl.ds(phase, lines, stride=KEEP_EVERY), :
                    ]
            one_row(start + row, keep_ends, give_ends, to + row)

    for index in order:
        for field in range(2):
            copies[index, field].wait()
        low, high = count * index, count * (index + 1)
        if index == 0:
            end_rows(down, 0, 0)
            low += REACH
        if index == pieces - 1:
            end_rows(up, rows - REACH, REACH)
            high -= REACH
        lax.fori_loop(low, high, middle_row, 0, unroll=4)


def pack(source, receiver):
    _, rows, size_y, size_z = source.shape
    lines = size_y // KEEP_EVERY
    apart = jax.ShapeDtypeStruct((2, REACH, size_y - lines, size_z), F32)
    middle = jax.ShapeDtypeStruct((2, rows - 2 * REACH, lines // 2, size_z), F32)
    ends = jax.ShapeDtypeStruct((2, 2 * REACH, lines // 2, size_z), F32)
    return pl.pallas_call(
        pack_kernel,
        out_shape=(
            apart,
            apart,
            jax.ShapeDtypeStruct((2, 2 * REACH, lines, size_z), F32),
            middle,
            ends,
            middle,
            ends,
            jax.ShapeDtypeStruct((rows, 2 * REACH, size_z), F32),
        ),
        in_specs=[HBM, HBM],
        out_specs=(VMEM,) * 8,
        scratch_shapes=[
            pltpu.VMEM((2, rows, size_y, size_z), F32),
            pltpu.SemaphoreType.DMA((4, 2)),
        ],
        compiler_params=params(56),
        cost_estimate=cost(10**10, 7 * 2**20),
        name="pack",
    )(source, receiver)


def z_weights(size_z):
    z = lax.broadcasted_iota(jnp.int32, (8, size_z), 1)
    return [
        (jnp.where(z >= d, WEIGHTS[d], 0.0), jnp.where(z < size_z - d, WEIGHTS[d], 0.0))
        for d in range(1, REACH + 1)
    ]


def z_terms(center, masks):
    size_z = center.shape[1]
    center = center.reshape(-1, 8, size_z)
    total = None
    for d, (below, above) in enumerate(masks, start=1):
        term = below * pltpu.roll(center, d, 2) + above * pltpu.roll(center, size_z - d, 2)
        total = term if total is None else total + term
    return total.reshape(-1, size_z)


def z_matrix(size_z):
    z = np.arange(size_z)
    apart = np.abs(z[:, None] - z[None, :])
    weights = np.array((0.0,) + WEIGHTS[1:] + (0.0,), np.float32)[np.minimum(apart, REACH + 1)]
    high = weights.astype(jnp.bfloat16)
    low = (weights - high.astype(np.float32)).astype(jnp.bfloat16)
    return jnp.asarray(np.block([[high, low], [high, np.zeros_like(low)]]))


def z_product(lines, matrix):
    size_z = lines.shape[1]
    high = lines.astype(jnp.bfloat16)
    low = (lines - high.astype(F32)).astype(jnp.bfloat16)
    both = jnp.dot(jnp.concatenate([high, low], axis=1), matrix, preferred_element_type=F32)
    return both[:, :size_z] + both[:, size_z:]


def first_step(now, row, z_sums, before, before_row, scale, scale_row, after, field):
    size_y = before.shape[2]
    lines = size_y // KEEP_EVERY
    for phase in range(KEEP_EVERY):
        kept = lambda start: pl.ds(start, lines, stride=KEEP_EVERY)
        at = PAD + phase
        center = now[field, row, kept(at), :]
        total = (3.0 * WEIGHTS[0]) * center + z_sums[field, kept(phase), :]
        for d in range(1, REACH + 1):
            around = (
                now[field, row + d, kept(at), :]
                + now[field, row - d, kept(at), :]
                + now[field, row, kept(at + d), :]
                + now[field, row, kept(at - d), :]
            )
            total = total + WEIGHTS[d] * around
        after[field, row, kept(at), :] = (
            2.0 * center
            - before[field, before_row, kept(phase), :]
            + scale[scale_row, kept(phase), :] * total
        )


def second_step(now, row, scale, scale_row, after, field, z_sum):
    size_y = scale.shape[1]
    lines = size_y // KEEP_EVERY
    kept = lambda start: pl.ds(start, lines, stride=KEEP_EVERY)
    center = after[field, row, kept(PAD), :]
    total = (3.0 * WEIGHTS[0]) * center + z_sum
    for d in range(1, REACH + 1):
        around = (
            after[field, row + d, kept(PAD), :]
            + after[field, row - d, kept(PAD), :]
            + after[field, row, kept(PAD + d), :]
            + after[field, row, kept(PAD - d), :]
        )
        total = total + WEIGHTS[d] * around
    return 2.0 * center - now[field, row, kept(PAD), :] + scale[scale_row, kept(0), :] * total


def side_term(after, after_row, field, size_y, gy):
    lowest = WEIGHTS[REACH] * after[field, after_row, PAD : PAD + 1, :]
    highest = sum(
        WEIGHTS[d] * after[field, after_row, PAD + size_y - d : PAD + size_y - d + 1, :]
        for d in range(1, REACH + 1)
    )
    return jnp.where(gy == 0, highest, lowest)


def fill_sides(now, row, got, field, size_y, gy):
    blank = jnp.zeros_like(got)
    now[field, row, PAD - REACH : PAD, :] = jnp.where(gy == 0, blank, got)
    now[field, row, size_y + PAD : size_y + PAD + REACH, :] = jnp.where(gy == 0, got, blank)


def blank_sides(after, row, field, size_y):
    blank = jnp.zeros((REACH, after.shape[3]), F32)
    after[field, row, PAD - REACH : PAD, :] = blank
    after[field, row, size_y + PAD : size_y + PAD + REACH, :] = blank


def steps_kernel(
    source, receiver, source_before, receiver_before, courant, side, matrix,
    partial, kept_courant, edge_courant, edge, side_out, now, before, scale, after, z_sums, sems,
):
    gy = lax.axis_index("gy")
    rows, size_y, size_z = courant.shape
    lines = size_y // KEEP_EVERY
    piece = 2 * REACH
    middle = pl.ds(PAD, size_y)

    def copies(index):
        part = pl.ds(piece * index, piece)
        found = []
        for field in range(2):
            src = (source, receiver)[field].at[0, part]
            dst = now.at[field, pl.ds(REACH + piece * index, piece), middle]
            found.append(pltpu.make_async_copy(src, dst, sems.at[index, field]))
        for field in range(2):
            src = (source_before, receiver_before)[field].at[0, part]
            found.append(pltpu.make_async_copy(src, before.at[field, part], sems.at[index, 2 + field]))
        found.append(pltpu.make_async_copy(courant.at[part], scale.at[part], sems.at[index, 4]))
        return found

    for index in range(rows // piece):
        for one in copies(index):
            one.start()

    for field in range(2):
        for row in list(range(REACH)) + list(range(rows + REACH, rows + 2 * REACH)):
            now[field, row] = jnp.zeros((size_y + 2 * PAD, size_z), F32)
            after[field, row] = jnp.zeros((size_y + 2 * PAD, size_z), F32)

    def fill(row, carry):
        for field in range(2):
            got = side[row, field * REACH : (field + 1) * REACH, :]
            fill_sides(now, row + REACH, got, field, size_y, gy)
            blank_sides(after, row + REACH, field, size_y)
        return carry

    lax.fori_loop(0, rows, fill, 0)
    for one in copies(0)[:2]:
        one.wait()

    def z_next(row):
        found = z_product(
            jnp.concatenate([now[field, row + REACH, middle, :] for field in range(2)], axis=0), matrix[...]
        )
        for field in range(2):
            z_sums[row % 2, field] = found[field * size_y : (field + 1) * size_y]

    z_next(0)

    def first(row, carry):
        @pl.when(row % piece == 0)
        def _():
            index = row // piece
            for one in copies(index)[2:]:
                one.wait()

            @pl.when(index + 1 < rows // piece)
            def _():
                for one in copies(index + 1)[:2]:
                    one.wait()

        at = row + REACH
        for field in range(2):
            first_step(now, at, z_sums.at[row % 2], before, row, scale, row, after, field)
        z_next(row + 1)
        for field in range(2):
            side_out[field, pl.ds(row, 1), :] = side_term(after, at, field, size_y, gy)
        return carry

    lax.fori_loop(0, rows, first, 0)

    def second(row, carry):
        at = row + REACH
        kept_courant[row] = scale[row, pl.ds(0, lines, stride=KEEP_EVERY), :]
        centers = [after[field, at, pl.ds(PAD, lines, stride=KEEP_EVERY), :] for field in range(2)]
        z_sum = z_product(jnp.concatenate(centers, axis=0), matrix[...])
        for field in range(2):
            partial[field, row] = second_step(
                now, at, scale, row, after, field, z_sum[field * lines : (field + 1) * lines]
            )
        return carry

    lax.fori_loop(0, rows, second, 0, unroll=2)
    for end in range(2):
        for row in range(REACH):
            at = rows - 1 - row if end else row
            edge_courant[end, row] = scale[at]
            for field in range(2):
                edge[field, end, row] = after[field, REACH + at, pl.ds(PAD, lines, stride=KEEP_EVERY), :]


def steps(source, receiver, source_before, receiver_before, courant, side):
    rows, size_y, size_z = courant.shape
    lines = size_y // KEEP_EVERY
    return pl.pallas_call(
        steps_kernel,
        out_shape=(
            jax.ShapeDtypeStruct((2, rows, lines, size_z), F32),
            jax.ShapeDtypeStruct((rows, lines, size_z), F32),
            jax.ShapeDtypeStruct((2, REACH, size_y, size_z), F32),
            jax.ShapeDtypeStruct((2, 2, REACH, lines, size_z), F32),
            jax.ShapeDtypeStruct((2, rows, size_z), F32),
        ),
        in_specs=[HBM] * 5 + [VMEM] * 2,
        out_specs=(VMEM,) * 5,
        scratch_shapes=[
            pltpu.VMEM((2, rows + 2 * REACH, size_y + 2 * PAD, size_z), F32),
            pltpu.VMEM((2, rows, size_y, size_z), F32),
            pltpu.VMEM((rows, size_y, size_z), F32),
            pltpu.VMEM((2, rows + 2 * REACH, size_y + 2 * PAD, size_z), F32),
            pltpu.VMEM((2, 2, size_y, size_z), F32),
            pltpu.SemaphoreType.DMA((rows // (2 * REACH), 5)),
        ],
        compiler_params=params(STEPS_MIB),
        cost_estimate=cost(2 * 10**10, 2**20),
        name="steps",
    )(source, receiver, source_before, receiver_before, courant, side, z_matrix(size_z))


def mend_kernel(
    left, right, near, far, partial, kept_courant, edge_courant, edge, side_in,
    ends, up, down, side_out, keep, give, added,
):
    gy, shot = lax.axis_index("gy"), lax.axis_index("shot")
    even = lax.axis_index("gx") % 2 == 0
    rows, lines, size_z = kept_courant.shape
    size_y = KEEP_EVERY * lines
    masks = z_weights(size_z)
    kept = lambda start: pl.ds(start, lines, stride=KEEP_EVERY)
    side_out[...] = side_in[...]
    for end in range(2):
        for field in range(2):
            group = 2 * end + field
            for row in range(REACH):
                blank_sides(added, row, group, size_y)
                for phase in range(KEEP_EVERY):
                    total = None
                    for d in range(row + 1, REACH + 1):
                        beyond = d - row - 1
                        at = beyond if end else REACH - 1 - beyond
                        if phase:
                            halo = (right if end else left)[field, at, (phase - 1) * lines : phase * lines, :]
                        elif end:
                            halo = jnp.where(even, near[field, at], far[field, at])
                        else:
                            halo = jnp.where(even, far[field, REACH + at], near[field, REACH + at])
                        term = WEIGHTS[d] * halo
                        total = term if total is None else total + term
                    scaled = edge_courant[end, row, pl.ds(phase, lines, stride=KEEP_EVERY), :]
                    added[group, row, kept(PAD + phase), :] = scaled * total
            for row in range(2 * REACH):
                at = rows - 1 - row if end else row
                total = None
                for other in range(REACH):
                    if 0 < abs(row - other) <= REACH:
                        term = WEIGHTS[abs(row - other)] * added[group, other, kept(PAD), :]
                        total = term if total is None else total + term
                value = partial[field, at]
                if row < REACH:
                    center = added[group, row, kept(PAD), :]
                    total = total + (3.0 * WEIGHTS[0]) * center + z_terms(center, masks)
                    for d in range(1, REACH + 1):
                        around = added[group, row, kept(PAD + d), :] + added[group, row, kept(PAD - d), :]
                        total = total + WEIGHTS[d] * around
                    value = value + 2.0 * center
                    first = edge[field, end, row] + center
                    if end:
                        up[field, REACH - 1 - row] = first
                    else:
                        down[field, row] = first
                    side_out[field, at : at + 1, :] = side_in[field, at : at + 1, :] + side_term(
                        added, row, group, size_y, gy
                    )
                ends[field, end, row] = value + kept_courant[at] * total
    for kind, ref in enumerate((near, far)):
        for field in range(2):
            for row in range(2 * REACH):
                pack_row(ref[field, row], field, row, shot, keep.at[kind], give.at[kind])


def mend(left, right, near, far, partial, kept_courant, edge_courant, edge, side_in):
    rows, lines, size_z = kept_courant.shape
    halo = jax.ShapeDtypeStruct((2, REACH, lines, size_z), F32)
    half = jax.ShapeDtypeStruct((2, 2, 2 * REACH, lines // 2, size_z), F32)
    return pl.pallas_call(
        mend_kernel,
        out_shape=(
            jax.ShapeDtypeStruct((2, 2, 2 * REACH, lines, size_z), F32),
            halo,
            halo,
            jax.ShapeDtypeStruct((2, rows, size_z), F32),
            half,
            half,
        ),
        in_specs=[VMEM] * 9,
        out_specs=(VMEM,) * 6,
        scratch_shapes=[pltpu.VMEM((4, REACH, KEEP_EVERY * lines + 2 * PAD, size_z), F32)],
        compiler_params=params(24),
        cost_estimate=cost(10**6, 2**20),
        name="mend",
    )(left, right, near, far, partial, kept_courant, edge_courant, edge, side_in)


def pack_row(value, field, row, shot, keep, give):
    first, second = z_halves(value)
    keep[field, row] = jnp.where(shot == 0, first, second)
    give[field, row] = jnp.where(shot == 0, second, first)


def side_lines(side, field, row, gy, lines):
    line = lax.broadcasted_iota(jnp.int32, (lines, side.shape[2]), 0)
    meets = line == jnp.where(gy == 0, lines - 1, 0)
    return jnp.where(meets, side[field, pl.ds(row, 1), :], 0.0)


def middle_kernel(partial, ends, kept_courant, side, keep, give):
    shot, gy = lax.axis_index("shot"), lax.axis_index("gy")
    rows, lines, _ = kept_courant.shape

    def one_row(row, values):
        for field in range(2):
            total = side_lines(side, field, row, gy, lines)
            pack_row(values[field] + kept_courant[row] * total, field, row - REACH, shot, keep, give)

    def middle(row, carry):
        one_row(row, [partial[field, row] for field in range(2)])
        return carry

    lax.fori_loop(2 * REACH, rows - 2 * REACH, middle, 0)
    for row in range(REACH, 2 * REACH):
        one_row(row, [ends[field, 0, row] for field in range(2)])
        one_row(rows - 1 - row, [ends[field, 1, row] for field in range(2)])


def finish_middle(partial, ends, kept_courant, side):
    rows, lines, size_z = kept_courant.shape
    half = jax.ShapeDtypeStruct((2, rows - 2 * REACH, lines // 2, size_z), F32)
    return pl.pallas_call(
        middle_kernel,
        out_shape=(half, half),
        in_specs=[VMEM] * 4,
        out_specs=(VMEM,) * 2,
        compiler_params=params(24),
        cost_estimate=cost(1, 1),
        name="finish_middle",
    )(partial, ends, kept_courant, side)


def ends_kernel(ends, kept_courant, left, right, side, keep, give):
    shot, gy = lax.axis_index("shot"), lax.axis_index("gy")
    rows, lines, _ = kept_courant.shape
    for field in range(2):
        for row in range(REACH):
            below = above = None
            for d in range(row + 1, REACH + 1):
                term = WEIGHTS[d] * left[field, REACH + row - d]
                below = term if below is None else below + term
                term = WEIGHTS[d] * right[field, d - 1 - row]
                above = term if above is None else above + term
            far = rows - 1 - row
            below = below + side_lines(side, field, row, gy, lines)
            above = above + side_lines(side, field, far, gy, lines)
            pack_row(ends[field, 0, row] + kept_courant[row] * below, field, row, shot, keep, give)
            pack_row(
                ends[field, 1, row] + kept_courant[far] * above,
                field, 2 * REACH - 1 - row, shot, keep, give,
            )


def finish_ends(ends, kept_courant, left, right, side):
    _, lines, size_z = kept_courant.shape
    half = jax.ShapeDtypeStruct((2, 2 * REACH, lines // 2, size_z), F32)
    return pl.pallas_call(
        ends_kernel,
        out_shape=(half, half),
        in_specs=[VMEM] * 5,
        out_specs=(VMEM,) * 2,
        compiler_params=params(24),
        cost_estimate=cost(10**10, 3 * 2**20),
        name="finish_ends",
    )(ends, kept_courant, left, right, side)


def block_starts(rows):
    even = lax.axis_index("gx") % 2 == 0
    return HALF, jnp.where(even, HALF + rows, 0), jnp.where(even, 0, HALF + rows)


def products(rows_of, sample, shift, here):
    total = None
    for group in range(rows_of.shape[0]):
        term = (
            rows_of[group, 0, 2 * HALF + sample - shift, here, :]
            * rows_of[group, 1, sample + shift, here, :]
        )
        total = term if total is None else total + term
    return total


def layout_copies(middles, ends, middle_starts, end_starts, rows_of, sems):
    copies = []

    def copy(src, part, start, count):
        dst = rows_of.at[part, :, pl.ds(start, count)]
        copies.append(pltpu.make_async_copy(src, dst, sems.at[len(copies)]))

    count = middles[0][0].shape[1]
    for part in range(2):
        for src, start in zip(middles[part], middle_starts):
            copy(src, part, start + REACH, count)
        for src, start in zip(ends[part], end_starts):
            copy(src.at[:, pl.ds(0, REACH)], part, start, REACH)
            copy(src.at[:, pl.ds(REACH, REACH)], part, start + REACH + count, REACH)
    return copies


def first_image_kernel(*refs):
    blocks, (out, rows_of, sems) = refs[:10], refs[10:]
    rows = blocks[0].shape[1] + 2 * REACH

    @pl.when(pl.program_id(0) == 0)
    def _():
        starts = block_starts(rows)
        ends = [[blocks[6 + part], blocks[8 + part].at[0], blocks[8 + part].at[1]] for part in range(2)]
        run_copies(layout_copies([blocks[:3], blocks[3:6]], ends, starts, starts, rows_of, sems))

    sample = 4 * pl.program_id(0)
    for chunk in range(rows_of.shape[3] // 8):
        here = pl.ds(8 * chunk, 8)
        for shift in range(OFFSETS):
            out[0, shift, here, :] = products(rows_of, sample, shift, here)


def first_image(blocks):
    _, middle_rows, lines, size_z = blocks[0].shape
    rows = middle_rows + 2 * REACH
    samples = rows // 4
    return pl.pallas_call(
        first_image_kernel,
        grid=(samples,),
        out_shape=jax.ShapeDtypeStruct((samples, OFFSETS, lines, size_z), F32),
        in_specs=[ANY] * len(blocks),
        out_specs=pl.BlockSpec((1, OFFSETS, lines, size_z), lambda i: (i, 0, 0, 0)),
        scratch_shapes=[
            pltpu.VMEM((2, 2, rows + 2 * HALF, lines, size_z), F32),
            pltpu.SemaphoreType.DMA((18,)),
        ],
        compiler_params=params(16),
        cost_estimate=cost(10**10, 8 * 2**20),
        name="first_image",
    )(*blocks)


def image_kernel(token, first, *refs):
    blocks, (out, rows_of, turned, staged, sems, out_sems) = refs[:9], refs[9:]
    rows = blocks[0].shape[1] + 2 * REACH
    step, steps_in_all = pl.program_id(0), pl.num_programs(0)

    @pl.when(step == 0)
    def _():
        ends = [[ref.at[part] for ref in blocks[6:]] for part in range(2)]
        end_starts = (HALF, 0, HALF + rows)
        run_copies(
            layout_copies([blocks[:3], blocks[3:6]], ends, block_starts(rows), end_starts, rows_of, sems)
        )

    lines, size_z = rows_of.shape[3], rows_of.shape[4]
    chunks = lines // 8

    def leave(at_step, chunk, half):
        slot = at_step % 2
        here = pl.ds(half * lines + 8 * chunk, 8)
        return pltpu.make_async_copy(staged.at[slot, here], out.at[at_step, here], out_sems.at[slot, chunk, half])

    @pl.when(step >= 2)
    def _():
        for chunk in range(chunks):
            for half in range(2):
                leave(step - 2, chunk, half).wait()

    sample = 4 * step
    for chunk in range(chunks):
        here = pl.ds(8 * chunk, 8)
        for shift in range(OFFSETS):
            total = first[0, shift, here, :] + products(rows_of, sample, shift, here)
            turned[chunk, pl.ds(shift, 8, stride=OFFSET_ROWS), :] = total

        for line in range(8):
            values = turned[chunk, line * OFFSET_ROWS : (line + 1) * OFFSET_ROWS, :].T
            at = 8 * chunk + line
            staged[step % 2, at] = values[: size_z // 2, :OFFSETS]
            staged[step % 2, lines + at] = values[size_z // 2 :, :OFFSETS]
    for chunk in range(chunks):
        for half in range(2):
            leave(step, chunk, half).start()

    @pl.when(step == steps_in_all - 1)
    def _():
        for back in (1, 0):
            for chunk in range(chunks):
                for half in range(2):
                    leave(step - back, chunk, half).wait()


def image(token, first, blocks):
    samples, _, lines, size_z = first.shape
    rows = 4 * samples
    return pl.pallas_call(
        image_kernel,
        grid=(samples,),
        out_shape=jax.ShapeDtypeStruct((samples, 2 * lines, size_z // 2, OFFSETS), F32),
        in_specs=[SMEM, pl.BlockSpec((1, OFFSETS, lines, size_z), lambda i: (i, 0, 0, 0))] + [ANY] * len(blocks),
        out_specs=HBM,
        scratch_shapes=[
            pltpu.VMEM((2, 2, rows + 2 * HALF, lines, size_z), F32),
            pltpu.VMEM((lines // 8, 8 * OFFSET_ROWS, size_z), F32),
            pltpu.VMEM((2, 2 * lines, size_z // 2, OFFSETS), F32),
            pltpu.SemaphoreType.DMA((18,)),
            pltpu.SemaphoreType.DMA((2, lines // 8, 2)),
        ],
        compiler_params=params(20),
        cost_estimate=cost(10**10, 16 * 2**20),
        name="image",
    )(token, first, *blocks)


def in_order_kernel(*refs):
    refs[-1][0] = 0


def in_order(*arrays):
    return pl.pallas_call(
        in_order_kernel,
        out_shape=jax.ShapeDtypeStruct((1,), jnp.int32),
        in_specs=[ANY] * len(arrays),
        out_specs=SMEM,
        compiler_params=params(1),
        cost_estimate=cost(1, 1),
        name="in_order",
    )(*arrays)


def on_device(source_now, source_before, receiver_now, receiver_before, courant):
    size = lax.axis_size("gx")
    up_pairs = [(i, i + 1) for i in range(size - 1)]
    down_pairs = [(j, i) for i, j in up_pairs]
    partner = [(i, i ^ 1) for i in range(size)]
    onward = [(i, i + 2) for i in range(0, size - 2, 2)] + [(i, i - 2) for i in range(3, size, 2)]
    both = [(0, 1), (1, 0)]

    def exchange(array, axis, pairs):
        return lax.ppermute(array, axis, pairs)

    barrier = lax.optimization_barrier
    up, down, edge, keep, keep_ends, give, give_ends, side = pack(source_now, receiver_now)
    near_edge = exchange(edge, "gx", partner)
    left = exchange(up, "gx", up_pairs)
    right = exchange(down, "gx", down_pairs)
    side = exchange(side, "gy", both)
    other = exchange(give, "shot", both)
    other_ends = exchange(give_ends, "shot", both)
    side, keep, other = barrier((side, keep, other))
    near_keep = exchange(keep, "gx", partner)
    near_other = exchange(other, "gx", partner)
    blocks = [keep, near_keep, None, other, near_other, None, keep_ends, other_ends]
    partial, kept_courant, edge_courant, edge, side = steps(
        source_now, receiver_now, source_before, receiver_before, courant, side
    )
    near_edge, side = barrier((near_edge, side))
    far_edge = exchange(near_edge, "gx", onward)
    ends, up, down, side, keep_edges, give_edges = mend(
        left, right, near_edge, far_edge, partial, kept_courant, edge_courant, edge, side
    )
    blocks += [keep_edges, exchange(give_edges, "shot", both)]
    left = exchange(up, "gx", up_pairs)
    right = exchange(down, "gx", down_pairs)
    side = exchange(side, "gy", both)
    side, near_keep, blocks[7], blocks[9] = barrier((side, near_keep, blocks[7], blocks[9]))
    far_keep = exchange(near_keep, "gx", onward)

    keep, give = finish_middle(partial, ends, kept_courant, side)
    other = exchange(give, "shot", both)
    near_keep = exchange(keep, "gx", partner)

    left, right, blocks[2], blocks[4] = barrier((left, right, far_keep, near_other))
    blocks[5] = exchange(blocks[4], "gx", onward)
    keep_ends, give_ends = finish_ends(ends, kept_courant, left, right, side)
    other, keep_ends, give_ends = barrier((other, keep_ends, give_ends))
    near_other = exchange(other, "gx", partner)
    other_ends = exchange(give_ends, "shot", both)
    other_ends, near_keep = barrier((other_ends, near_keep))
    own = jnp.stack([keep_ends, other_ends])
    far_keep = exchange(near_keep, "gx", onward)
    right = exchange(own, "gx", down_pairs)
    late, near_other = barrier((keep_ends, near_other))
    far_other = exchange(near_other, "gx", onward)
    left = exchange(jnp.stack([late, other_ends]), "gx", up_pairs)
    blocks[5], far_keep = lax.optimization_barrier((blocks[5], far_keep))
    first = first_image(blocks)
    token = in_order(right, first)
    blocks = [keep, near_keep, far_keep, other, near_other, far_other, own, left, right]
    return jnp.transpose(image(token, first, blocks), (3, 0, 1, 2))


def solution(mesh):
    in_specs = (
        P("shot", "gx", "gy", None),
        P("shot", "gx", "gy", None),
        P("shot", "gx", "gy", None),
        P("shot", "gx", "gy", None),
        P("gx", "gy", None),
    )
    out_specs = P(None, "gx", "gy", "shot")
    return jax.shard_map(
        on_device, mesh=mesh, in_specs=in_specs, out_specs=out_specs, check_vma=False
    )
```

```python
import functools

import jax
import jax.numpy as jnp
import numpy as np
from jax import lax
from jax.experimental import pallas as pl
from jax.experimental.pallas import tpu as pltpu
from jax.sharding import PartitionSpec as P

HALF = 32
REACH = 4
KEEP_EVERY = 4
OFFSETS = 2 * HALF + 1
OFFSET_ROWS = 72
LINES = 32
STEPS_MIB = 50
WEIGHTS = (-205.0 / 72.0, 8.0 / 5.0, -1.0 / 5.0, 8.0 / 315.0, -1.0 / 560.0)
PAD = 8
F32 = jnp.float32
HBM = pl.BlockSpec(memory_space=pltpu.HBM)
ANY = pl.BlockSpec(memory_space=pl.ANY)
VMEM = pl.BlockSpec(memory_space=pltpu.VMEM)
SMEM = pl.BlockSpec(memory_space=pltpu.SMEM)


def params(mib):
    return pltpu.CompilerParams(vmem_limit_bytes=mib * 2**20)


def cost(flops, nbytes):
    return pl.CostEstimate(flops=flops, bytes_accessed=nbytes, transcendentals=0)


def run_copies(copies):
    for copy in copies:
        copy.start()
    for copy in copies:
        copy.wait()


def z_halves(lines):
    count, size_z = lines.shape
    top, bottom = lines[: count // 2], lines[count // 2 :]
    low = lax.broadcasted_iota(jnp.int32, top.shape, 1) < size_z // 2
    first = jnp.where(low, top, pltpu.roll(bottom, size_z // 2, 1))
    second = jnp.where(low, pltpu.roll(top, size_z // 2, 1), bottom)
    return first, second


def pack_kernel(
    source, receiver, up, down, edge, keep, keep_ends, give, give_ends, side, fields, sems
):
    shot, gy = lax.axis_index("shot"), lax.axis_index("gy")
    _, rows, size_y, _ = fields.shape
    lines = size_y // KEEP_EVERY
    pieces = sems.shape[0]
    count = rows // pieces
    order = [0, pieces - 1] + list(range(1, pieces - 1))
    copies = {}
    for index in order:
        part = pl.ds(count * index, count)
        for field, ref in enumerate((source, receiver)):
            copies[index, field] = pltpu.make_async_copy(
                ref.at[0, part], fields.at[field, part], sems.at[index, field]
            )
            copies[index, field].start()

    def one_row(row, keep_ref, give_ref, to):
        parts = []
        for field in range(2):
            first, second = z_halves(fields[field, row, pl.ds(0, lines, stride=KEEP_EVERY), :])
            keep_ref[field, to] = jnp.where(shot == 0, first, second)
            give_ref[field, to] = jnp.where(shot == 0, second, first)
            low = fields[field, row, 0:REACH, :]
            high = fields[field, row, size_y - REACH : size_y, :]
            parts.append(jnp.where(gy == 0, high, low))
        side[row] = jnp.concatenate(parts, axis=0)

    def middle_row(row, carry):
        one_row(row, keep, give, row - REACH)
        return carry

    def end_rows(out, start, to):
        for row in range(REACH):
            for field in range(2):
                edge[field, to + row] = fields[field, start + row, pl.ds(0, lines, stride=KEEP_EVERY), :]
                for phase in range(1, KEEP_EVERY):
                    out[field, row, (phase - 1) * lines : phase * lines, :] = fields[
                        field, start + row, pl.ds(phase, lines, stride=KEEP_EVERY), :
                    ]
            one_row(start + row, keep_ends, give_ends, to + row)

    for index in order:
        for field in range(2):
            copies[index, field].wait()
        low, high = count * index, count * (index + 1)
        if index == 0:
            end_rows(down, 0, 0)
            low += REACH
        if index == pieces - 1:
            end_rows(up, rows - REACH, REACH)
            high -= REACH
        lax.fori_loop(low, high, middle_row, 0, unroll=4)


def pack(source, receiver):
    _, rows, size_y, size_z = source.shape
    lines = size_y // KEEP_EVERY
    apart = jax.ShapeDtypeStruct((2, REACH, size_y - lines, size_z), F32)
    middle = jax.ShapeDtypeStruct((2, rows - 2 * REACH, lines // 2, size_z), F32)
    ends = jax.ShapeDtypeStruct((2, 2 * REACH, lines // 2, size_z), F32)
    return pl.pallas_call(
        pack_kernel,
        out_shape=(
            apart,
            apart,
            jax.ShapeDtypeStruct((2, 2 * REACH, lines, size_z), F32),
            middle,
            ends,
            middle,
            ends,
            jax.ShapeDtypeStruct((rows, 2 * REACH, size_z), F32),
        ),
        in_specs=[HBM, HBM],
        out_specs=(VMEM,) * 8,
        scratch_shapes=[
            pltpu.VMEM((2, rows, size_y, size_z), F32),
            pltpu.SemaphoreType.DMA((4, 2)),
        ],
        compiler_params=params(56),
        cost_estimate=cost(10**10, 7 * 2**20),
        name="pack",
    )(source, receiver)


def z_weights(size_z):
    z = lax.broadcasted_iota(jnp.int32, (8, size_z), 1)
    return [
        (jnp.where(z >= d, WEIGHTS[d], 0.0), jnp.where(z < size_z - d, WEIGHTS[d], 0.0))
        for d in range(1, REACH + 1)
    ]


def z_terms(center, masks):
    size_z = center.shape[1]
    center = center.reshape(-1, 8, size_z)
    total = None
    for d, (below, above) in enumerate(masks, start=1):
        term = below * pltpu.roll(center, d, 2) + above * pltpu.roll(center, size_z - d, 2)
        total = term if total is None else total + term
    return total.reshape(-1, size_z)


def z_matrix(size_z):
    z = np.arange(size_z)
    apart = np.abs(z[:, None] - z[None, :])
    weights = np.array((0.0,) + WEIGHTS[1:] + (0.0,), np.float32)[np.minimum(apart, REACH + 1)]
    high = weights.astype(jnp.bfloat16)
    low = (weights - high.astype(np.float32)).astype(jnp.bfloat16)
    return jnp.asarray(np.block([[high, low], [high, np.zeros_like(low)]]))


def z_product(lines, matrix):
    size_z = lines.shape[1]
    high = lines.astype(jnp.bfloat16)
    low = (lines - high.astype(F32)).astype(jnp.bfloat16)
    both = jnp.dot(jnp.concatenate([high, low], axis=1), matrix, preferred_element_type=F32)
    return both[:, :size_z] + both[:, size_z:]


def first_step(now, row, z_sums, before, before_row, scale, scale_row, after, field):
    size_y = before.shape[2]
    lines = size_y // KEEP_EVERY
    for phase in range(KEEP_EVERY):
        kept = lambda start: pl.ds(start, lines, stride=KEEP_EVERY)
        at = PAD + phase
        center = now[field, row, kept(at), :]
        total = (3.0 * WEIGHTS[0]) * center + z_sums[field, kept(phase), :]
        for d in range(1, REACH + 1):
            around = (
                now[field, row + d, kept(at), :]
                + now[field, row - d, kept(at), :]
                + now[field, row, kept(at + d), :]
                + now[field, row, kept(at - d), :]
            )
            total = total + WEIGHTS[d] * around
        after[field, row, kept(at), :] = (
            2.0 * center
            - before[field, before_row, kept(phase), :]
            + scale[scale_row, kept(phase), :] * total
        )


def second_step(now, row, scale, scale_row, after, field, z_sum):
    size_y = scale.shape[1]
    lines = size_y // KEEP_EVERY
    kept = lambda start: pl.ds(start, lines, stride=KEEP_EVERY)
    center = after[field, row, kept(PAD), :]
    total = (3.0 * WEIGHTS[0]) * center + z_sum
    for d in range(1, REACH + 1):
        around = (
            after[field, row + d, kept(PAD), :]
            + after[field, row - d, kept(PAD), :]
            + after[field, row, kept(PAD + d), :]
            + after[field, row, kept(PAD - d), :]
        )
        total = total + WEIGHTS[d] * around
    return 2.0 * center - now[field, row, kept(PAD), :] + scale[scale_row, kept(0), :] * total


def side_term(after, after_row, field, size_y, gy):
    lowest = WEIGHTS[REACH] * after[field, after_row, PAD : PAD + 1, :]
    highest = sum(
        WEIGHTS[d] * after[field, after_row, PAD + size_y - d : PAD + size_y - d + 1, :]
        for d in range(1, REACH + 1)
    )
    return jnp.where(gy == 0, highest, lowest)


def fill_sides(now, row, got, field, size_y, gy):
    blank = jnp.zeros_like(got)
    now[field, row, PAD - REACH : PAD, :] = jnp.where(gy == 0, blank, got)
    now[field, row, size_y + PAD : size_y + PAD + REACH, :] = jnp.where(gy == 0, got, blank)


def blank_sides(after, row, field, size_y):
    blank = jnp.zeros((REACH, after.shape[3]), F32)
    after[field, row, PAD - REACH : PAD, :] = blank
    after[field, row, size_y + PAD : size_y + PAD + REACH, :] = blank


def steps_kernel(
    source, receiver, source_before, receiver_before, courant, side, matrix,
    partial, kept_courant, edge_courant, edge, side_out, now, before, scale, after, z_sums, sems,
):
    gy = lax.axis_index("gy")
    rows, size_y, size_z = courant.shape
    lines = size_y // KEEP_EVERY
    piece = 2 * REACH
    middle = pl.ds(PAD, size_y)

    def copies(index):
        part = pl.ds(piece * index, piece)
        found = []
        for field in range(2):
            src = (source, receiver)[field].at[0, part]
            dst = now.at[field, pl.ds(REACH + piece * index, piece), middle]
            found.append(pltpu.make_async_copy(src, dst, sems.at[index, field]))
        for field in range(2):
            src = (source_before, receiver_before)[field].at[0, part]
            found.append(pltpu.make_async_copy(src, before.at[field, part], sems.at[index, 2 + field]))
        found.append(pltpu.make_async_copy(courant.at[part], scale.at[part], sems.at[index, 4]))
        return found

    for index in range(rows // piece):
        for one in copies(index):
            one.start()

    for field in range(2):
        for row in list(range(REACH)) + list(range(rows + REACH, rows + 2 * REACH)):
            now[field, row] = jnp.zeros((size_y + 2 * PAD, size_z), F32)
            after[field, row] = jnp.zeros((size_y + 2 * PAD, size_z), F32)

    def fill(row, carry):
        for field in range(2):
            got = side[row, field * REACH : (field + 1) * REACH, :]
            fill_sides(now, row + REACH, got, field, size_y, gy)
            blank_sides(after, row + REACH, field, size_y)
        return carry

    lax.fori_loop(0, rows, fill, 0)
    for one in copies(0)[:2]:
        one.wait()

    def z_next(row):
        found = z_product(
            jnp.concatenate([now[field, row + REACH, middle, :] for field in range(2)], axis=0), matrix[...]
        )
        for field in range(2):
            z_sums[row % 2, field] = found[field * size_y : (field + 1) * size_y]

    z_next(0)

    def first(row, carry):
        @pl.when(row % piece == 0)
        def _():
            index = row // piece
            for one in copies(index)[2:]:
                one.wait()

            @pl.when(index + 1 < rows // piece)
            def _():
                for one in copies(index + 1)[:2]:
                    one.wait()

        at = row + REACH
        for field in range(2):
            first_step(now, at, z_sums.at[row % 2], before, row, scale, row, after, field)
        z_next(row + 1)
        for field in range(2):
            side_out[field, pl.ds(row, 1), :] = side_term(after, at, field, size_y, gy)
        return carry

    lax.fori_loop(0, rows, first, 0)

    def second(row, carry):
        at = row + REACH
        kept_courant[row] = scale[row, pl.ds(0, lines, stride=KEEP_EVERY), :]
        centers = [after[field, at, pl.ds(PAD, lines, stride=KEEP_EVERY), :] for field in range(2)]
        z_sum = z_product(jnp.concatenate(centers, axis=0), matrix[...])
        for field in range(2):
            partial[field, row] = second_step(
                now, at, scale, row, after, field, z_sum[field * lines : (field + 1) * lines]
            )
        return carry

    lax.fori_loop(0, rows, second, 0, unroll=2)
    for end in range(2):
        for row in range(REACH):
            at = rows - 1 - row if end else row
            edge_courant[end, row] = scale[at]
            for field in range(2):
                edge[field, end, row] = after[field, REACH + at, pl.ds(PAD, lines, stride=KEEP_EVERY), :]


def steps(source, receiver, source_before, receiver_before, courant, side):
    rows, size_y, size_z = courant.shape
    lines = size_y // KEEP_EVERY
    return pl.pallas_call(
        steps_kernel,
        out_shape=(
            jax.ShapeDtypeStruct((2, rows, lines, size_z), F32),
            jax.ShapeDtypeStruct((rows, lines, size_z), F32),
            jax.ShapeDtypeStruct((2, REACH, size_y, size_z), F32),
            jax.ShapeDtypeStruct((2, 2, REACH, lines, size_z), F32),
            jax.ShapeDtypeStruct((2, rows, size_z), F32),
        ),
        in_specs=[HBM] * 5 + [VMEM] * 2,
        out_specs=(VMEM,) * 5,
        scratch_shapes=[
            pltpu.VMEM((2, rows + 2 * REACH, size_y + 2 * PAD, size_z), F32),
            pltpu.VMEM((2, rows, size_y, size_z), F32),
            pltpu.VMEM((rows, size_y, size_z), F32),
            pltpu.VMEM((2, rows + 2 * REACH, size_y + 2 * PAD, size_z), F32),
            pltpu.VMEM((2, 2, size_y, size_z), F32),
            pltpu.SemaphoreType.DMA((rows // (2 * REACH), 5)),
        ],
        compiler_params=params(STEPS_MIB),
        cost_estimate=cost(2 * 10**10, 2**20),
        name="steps",
    )(source, receiver, source_before, receiver_before, courant, side, z_matrix(size_z))


def mend_kernel(
    left, right, near, far, partial, kept_courant, edge_courant, edge, side_in,
    ends, up, down, side_out, keep, give, added,
):
    gy, shot = lax.axis_index("gy"), lax.axis_index("shot")
    even = lax.axis_index("gx") % 2 == 0
    rows, lines, size_z = kept_courant.shape
    size_y = KEEP_EVERY * lines
    masks = z_weights(size_z)
    kept = lambda start: pl.ds(start, lines, stride=KEEP_EVERY)
    side_out[...] = side_in[...]
    for end in range(2):
        for field in range(2):
            group = 2 * end + field
            for row in range(REACH):
                blank_sides(added, row, group, size_y)
                for phase in range(KEEP_EVERY):
                    total = None
                    for d in range(row + 1, REACH + 1):
                        beyond = d - row - 1
                        at = beyond if end else REACH - 1 - beyond
                        if phase:
                            halo = (right if end else left)[field, at, (phase - 1) * lines : phase * lines, :]
                        elif end:
                            halo = jnp.where(even, near[field, at], far[field, at])
                        else:
                            halo = jnp.where(even, far[field, REACH + at], near[field, REACH + at])
                        term = WEIGHTS[d] * halo
                        total = term if total is None else total + term
                    scaled = edge_courant[end, row, pl.ds(phase, lines, stride=KEEP_EVERY), :]
                    added[group, row, kept(PAD + phase), :] = scaled * total
            for row in range(2 * REACH):
                at = rows - 1 - row if end else row
                total = None
                for other in range(REACH):
                    if 0 < abs(row - other) <= REACH:
                        term = WEIGHTS[abs(row - other)] * added[group, other, kept(PAD), :]
                        total = term if total is None else total + term
                value = partial[field, at]
                if row < REACH:
                    center = added[group, row, kept(PAD), :]
                    total = total + (3.0 * WEIGHTS[0]) * center + z_terms(center, masks)
                    for d in range(1, REACH + 1):
                        around = added[group, row, kept(PAD + d), :] + added[group, row, kept(PAD - d), :]
                        total = total + WEIGHTS[d] * around
                    value = value + 2.0 * center
                    first = edge[field, end, row] + center
                    if end:
                        up[field, REACH - 1 - row] = first
                    else:
                        down[field, row] = first
                    side_out[field, at : at + 1, :] = side_in[field, at : at + 1, :] + side_term(
                        added, row, group, size_y, gy
                    )
                ends[field, end, row] = value + kept_courant[at] * total
    for kind, ref in enumerate((near, far)):
        for field in range(2):
            for row in range(2 * REACH):
                pack_row(ref[field, row], field, row, shot, keep.at[kind], give.at[kind])


def mend(left, right, near, far, partial, kept_courant, edge_courant, edge, side_in):
    rows, lines, size_z = kept_courant.shape
    halo = jax.ShapeDtypeStruct((2, REACH, lines, size_z), F32)
    half = jax.ShapeDtypeStruct((2, 2, 2 * REACH, lines // 2, size_z), F32)
    return pl.pallas_call(
        mend_kernel,
        out_shape=(
            jax.ShapeDtypeStruct((2, 2, 2 * REACH, lines, size_z), F32),
            halo,
            halo,
            jax.ShapeDtypeStruct((2, rows, size_z), F32),
            half,
            half,
        ),
        in_specs=[VMEM] * 9,
        out_specs=(VMEM,) * 6,
        scratch_shapes=[pltpu.VMEM((4, REACH, KEEP_EVERY * lines + 2 * PAD, size_z), F32)],
        compiler_params=params(24),
        cost_estimate=cost(10**6, 2**20),
        name="mend",
    )(left, right, near, far, partial, kept_courant, edge_courant, edge, side_in)


def pack_row(value, field, row, shot, keep, give):
    first, second = z_halves(value)
    keep[field, row] = jnp.where(shot == 0, first, second)
    give[field, row] = jnp.where(shot == 0, second, first)


def side_lines(side, field, row, gy, lines):
    line = lax.broadcasted_iota(jnp.int32, (lines, side.shape[2]), 0)
    meets = line == jnp.where(gy == 0, lines - 1, 0)
    return jnp.where(meets, side[field, pl.ds(row, 1), :], 0.0)


def middle_kernel(partial, ends, kept_courant, side, keep, give):
    shot, gy = lax.axis_index("shot"), lax.axis_index("gy")
    rows, lines, _ = kept_courant.shape

    def one_row(row, values):
        for field in range(2):
            total = side_lines(side, field, row, gy, lines)
            pack_row(values[field] + kept_courant[row] * total, field, row - REACH, shot, keep, give)

    def middle(row, carry):
        one_row(row, [partial[field, row] for field in range(2)])
        return carry

    lax.fori_loop(2 * REACH, rows - 2 * REACH, middle, 0)
    for row in range(REACH, 2 * REACH):
        one_row(row, [ends[field, 0, row] for field in range(2)])
        one_row(rows - 1 - row, [ends[field, 1, row] for field in range(2)])


def finish_middle(partial, ends, kept_courant, side):
    rows, lines, size_z = kept_courant.shape
    half = jax.ShapeDtypeStruct((2, rows - 2 * REACH, lines // 2, size_z), F32)
    return pl.pallas_call(
        middle_kernel,
        out_shape=(half, half),
        in_specs=[VMEM] * 4,
        out_specs=(VMEM,) * 2,
        compiler_params=params(24),
        cost_estimate=cost(1, 1),
        name="finish_middle",
    )(partial, ends, kept_courant, side)


def ends_kernel(ends, kept_courant, left, right, side, keep, give):
    shot, gy = lax.axis_index("shot"), lax.axis_index("gy")
    rows, lines, _ = kept_courant.shape
    for field in range(2):
        for row in range(REACH):
            below = above = None
            for d in range(row + 1, REACH + 1):
                term = WEIGHTS[d] * left[field, REACH + row - d]
                below = term if below is None else below + term
                term = WEIGHTS[d] * right[field, d - 1 - row]
                above = term if above is None else above + term
            far = rows - 1 - row
            below = below + side_lines(side, field, row, gy, lines)
            above = above + side_lines(side, field, far, gy, lines)
            pack_row(ends[field, 0, row] + kept_courant[row] * below, field, row, shot, keep, give)
            pack_row(
                ends[field, 1, row] + kept_courant[far] * above,
                field, 2 * REACH - 1 - row, shot, keep, give,
            )


def finish_ends(ends, kept_courant, left, right, side):
    _, lines, size_z = kept_courant.shape
    half = jax.ShapeDtypeStruct((2, 2 * REACH, lines // 2, size_z), F32)
    return pl.pallas_call(
        ends_kernel,
        out_shape=(half, half),
        in_specs=[VMEM] * 5,
        out_specs=(VMEM,) * 2,
        compiler_params=params(24),
        cost_estimate=cost(10**10, 3 * 2**20),
        name="finish_ends",
    )(ends, kept_courant, left, right, side)


def block_starts(rows):
    even = lax.axis_index("gx") % 2 == 0
    return HALF, jnp.where(even, HALF + rows, 0), jnp.where(even, 0, HALF + rows)


def products(rows_of, sample, shift, here):
    total = None
    for group in range(rows_of.shape[0]):
        term = (
            rows_of[group, 0, 2 * HALF + sample - shift, here, :]
            * rows_of[group, 1, sample + shift, here, :]
        )
        total = term if total is None else total + term
    return total


def layout_copies(middles, ends, middle_starts, end_starts, rows_of, sems):
    copies = []

    def copy(src, part, start, count):
        dst = rows_of.at[part, :, pl.ds(start, count)]
        copies.append(pltpu.make_async_copy(src, dst, sems.at[len(copies)]))

    count = middles[0][0].shape[1]
    for part in range(2):
        for src, start in zip(middles[part], middle_starts):
            copy(src, part, start + REACH, count)
        for src, start in zip(ends[part], end_starts):
            copy(src.at[:, pl.ds(0, REACH)], part, start, REACH)
            copy(src.at[:, pl.ds(REACH, REACH)], part, start + REACH + count, REACH)
    return copies


def first_image_kernel(*refs):
    blocks, (out, rows_of, sems) = refs[:10], refs[10:]
    rows = blocks[0].shape[1] + 2 * REACH

    @pl.when(pl.program_id(0) == 0)
    def _():
        starts = block_starts(rows)
        ends = [[blocks[6 + part], blocks[8 + part].at[0], blocks[8 + part].at[1]] for part in range(2)]
        run_copies(layout_copies([blocks[:3], blocks[3:6]], ends, starts, starts, rows_of, sems))

    sample = 4 * pl.program_id(0)
    for chunk in range(rows_of.shape[3] // 8):
        here = pl.ds(8 * chunk, 8)
        for shift in range(OFFSETS):
            out[0, shift, here, :] = products(rows_of, sample, shift, here)


def first_image(blocks):
    _, middle_rows, lines, size_z = blocks[0].shape
    rows = middle_rows + 2 * REACH
    samples = rows // 4
    return pl.pallas_call(
        first_image_kernel,
        grid=(samples,),
        out_shape=jax.ShapeDtypeStruct((samples, OFFSETS, lines, size_z), F32),
        in_specs=[ANY] * len(blocks),
        out_specs=pl.BlockSpec((1, OFFSETS, lines, size_z), lambda i: (i, 0, 0, 0)),
        scratch_shapes=[
            pltpu.VMEM((2, 2, rows + 2 * HALF, lines, size_z), F32),
            pltpu.SemaphoreType.DMA((18,)),
        ],
        compiler_params=params(16),
        cost_estimate=cost(10**10, 8 * 2**20),
        name="first_image",
    )(*blocks)


def image_kernel(token, first, *refs):
    blocks, (out, rows_of, turned, staged, sems, out_sems) = refs[:9], refs[9:]
    rows = blocks[0].shape[1] + 2 * REACH
    step, steps_in_all = pl.program_id(0), pl.num_programs(0)

    @pl.when(step == 0)
    def _():
        ends = [[ref.at[part] for ref in blocks[6:]] for part in range(2)]
        end_starts = (HALF, 0, HALF + rows)
        run_copies(
            layout_copies([blocks[:3], blocks[3:6]], ends, block_starts(rows), end_starts, rows_of, sems)
        )

    lines, size_z = rows_of.shape[3], rows_of.shape[4]
    chunks = lines // 8

    def leave(at_step, chunk, half):
        slot = at_step % 2
        here = pl.ds(half * lines + 8 * chunk, 8)
        return pltpu.make_async_copy(staged.at[slot, here], out.at[at_step, here], out_sems.at[slot, chunk, half])

    sample = 4 * step
    for chunk in range(chunks):
        here = pl.ds(8 * chunk, 8)
        for shift in range(OFFSETS):
            total = first[0, shift, here, :] + products(rows_of, sample, shift, here)
            turned[chunk, pl.ds(shift, 8, stride=OFFSET_ROWS), :] = total

        @pl.when(step >= 2)
        def _():
            for half in range(2):
                leave(step - 2, chunk, half).wait()

        for line in range(8):
            values = turned[chunk, line * OFFSET_ROWS : (line + 1) * OFFSET_ROWS, :].T
            at = 8 * chunk + line
            staged[step % 2, at] = values[: size_z // 2, :OFFSETS]
            staged[step % 2, lines + at] = values[size_z // 2 :, :OFFSETS]
        for half in range(2):
            leave(step, chunk, half).start()

    @pl.when(step == steps_in_all - 1)
    def _():
        for back in (1, 0):
            for chunk in range(chunks):
                for half in range(2):
                    leave(step - back, chunk, half).wait()


def image(token, first, blocks):
    samples, _, lines, size_z = first.shape
    rows = 4 * samples
    return pl.pallas_call(
        image_kernel,
        grid=(samples,),
        out_shape=jax.ShapeDtypeStruct((samples, 2 * lines, size_z // 2, OFFSETS), F32),
        in_specs=[SMEM, pl.BlockSpec((1, OFFSETS, lines, size_z), lambda i: (i, 0, 0, 0))] + [ANY] * len(blocks),
        out_specs=HBM,
        scratch_shapes=[
            pltpu.VMEM((2, 2, rows + 2 * HALF, lines, size_z), F32),
            pltpu.VMEM((lines // 8, 8 * OFFSET_ROWS, size_z), F32),
            pltpu.VMEM((2, 2 * lines, size_z // 2, OFFSETS), F32),
            pltpu.SemaphoreType.DMA((18,)),
            pltpu.SemaphoreType.DMA((2, lines // 8, 2)),
        ],
        compiler_params=params(20),
        cost_estimate=cost(10**10, 16 * 2**20),
        name="image",
    )(token, first, *blocks)


def in_order_kernel(*refs):
    refs[-1][0] = 0


def in_order(*arrays):
    return pl.pallas_call(
        in_order_kernel,
        out_shape=jax.ShapeDtypeStruct((1,), jnp.int32),
        in_specs=[ANY] * len(arrays),
        out_specs=SMEM,
        compiler_params=params(1),
        cost_estimate=cost(1, 1),
        name="in_order",
    )(*arrays)


def on_device(source_now, source_before, receiver_now, receiver_before, courant):
    size = lax.axis_size("gx")
    up_pairs = [(i, i + 1) for i in range(size - 1)]
    down_pairs = [(j, i) for i, j in up_pairs]
    partner = [(i, i ^ 1) for i in range(size)]
    onward = [(i, i + 2) for i in range(0, size - 2, 2)] + [(i, i - 2) for i in range(3, size, 2)]
    both = [(0, 1), (1, 0)]

    def exchange(array, axis, pairs):
        return lax.ppermute(array, axis, pairs)

    barrier = lax.optimization_barrier
    up, down, edge, keep, keep_ends, give, give_ends, side = pack(source_now, receiver_now)
    near_edge = exchange(edge, "gx", partner)
    left = exchange(up, "gx", up_pairs)
    right = exchange(down, "gx", down_pairs)
    side = exchange(side, "gy", both)
    other = exchange(give, "shot", both)
    other_ends = exchange(give_ends, "shot", both)
    side, keep, other = barrier((side, keep, other))
    near_keep = exchange(keep, "gx", partner)
    near_other = exchange(other, "gx", partner)
    blocks = [keep, near_keep, None, other, near_other, None, keep_ends, other_ends]
    partial, kept_courant, edge_courant, edge, side = steps(
        source_now, receiver_now, source_before, receiver_before, courant, side
    )
    near_edge, side = barrier((near_edge, side))
    far_edge = exchange(near_edge, "gx", onward)
    ends, up, down, side, keep_edges, give_edges = mend(
        left, right, near_edge, far_edge, partial, kept_courant, edge_courant, edge, side
    )
    blocks += [keep_edges, exchange(give_edges, "shot", both)]
    left = exchange(up, "gx", up_pairs)
    right = exchange(down, "gx", down_pairs)
    side = exchange(side, "gy", both)
    side, near_keep, blocks[7], blocks[9] = barrier((side, near_keep, blocks[7], blocks[9]))
    far_keep = exchange(near_keep, "gx", onward)

    keep, give = finish_middle(partial, ends, kept_courant, side)
    other = exchange(give, "shot", both)
    near_keep = exchange(keep, "gx", partner)

    left, right, blocks[2], blocks[4] = barrier((left, right, far_keep, near_other))
    blocks[5] = exchange(blocks[4], "gx", onward)
    keep_ends, give_ends = finish_ends(ends, kept_courant, left, right, side)
    other, keep_ends, give_ends = barrier((other, keep_ends, give_ends))
    near_other = exchange(other, "gx", partner)
    other_ends = exchange(give_ends, "shot", both)
    other_ends, near_keep = barrier((other_ends, near_keep))
    own = jnp.stack([keep_ends, other_ends])
    far_keep = exchange(near_keep, "gx", onward)
    right = exchange(own, "gx", down_pairs)
    late, near_other = barrier((own, near_other))
    left = exchange(late, "gx", up_pairs)
    far_other = exchange(near_other, "gx", onward)
    blocks[5], far_keep = lax.optimization_barrier((blocks[5], far_keep))
    first = first_image(blocks)
    token = in_order(right, first)
    blocks = [keep, near_keep, far_keep, other, near_other, far_other, own, left, right]
    return jnp.transpose(image(token, first, blocks), (3, 0, 1, 2))


def solution(mesh):
    in_specs = (
        P("shot", "gx", "gy", None),
        P("shot", "gx", "gy", None),
        P("shot", "gx", "gy", None),
        P("shot", "gx", "gy", None),
        P("gx", "gy", None),
    )
    out_specs = P(None, "gx", "gy", "shot")
    return jax.shard_map(
        on_device, mesh=mesh, in_specs=in_specs, out_specs=out_specs, check_vma=False
    )
```

```python
import functools

import jax
import jax.numpy as jnp
import numpy as np
from jax import lax
from jax.experimental import pallas as pl
from jax.experimental.pallas import tpu as pltpu
from jax.sharding import PartitionSpec as P

HALF = 32
REACH = 4
KEEP_EVERY = 4
OFFSETS = 2 * HALF + 1
OFFSET_ROWS = 72
LINES = 32
STEPS_MIB = 50
WEIGHTS = (-205.0 / 72.0, 8.0 / 5.0, -1.0 / 5.0, 8.0 / 315.0, -1.0 / 560.0)
PAD = 8
F32 = jnp.float32
HBM = pl.BlockSpec(memory_space=pltpu.HBM)
ANY = pl.BlockSpec(memory_space=pl.ANY)
VMEM = pl.BlockSpec(memory_space=pltpu.VMEM)
SMEM = pl.BlockSpec(memory_space=pltpu.SMEM)


def params(mib):
    return pltpu.CompilerParams(vmem_limit_bytes=mib * 2**20)


def cost(flops, nbytes):
    return pl.CostEstimate(flops=flops, bytes_accessed=nbytes, transcendentals=0)


def run_copies(copies):
    for copy in copies:
        copy.start()
    for copy in copies:
        copy.wait()


def z_halves(lines):
    count, size_z = lines.shape
    top, bottom = lines[: count // 2], lines[count // 2 :]
    low = lax.broadcasted_iota(jnp.int32, top.shape, 1) < size_z // 2
    first = jnp.where(low, top, pltpu.roll(bottom, size_z // 2, 1))
    second = jnp.where(low, pltpu.roll(top, size_z // 2, 1), bottom)
    return first, second


def pack_kernel(
    source, receiver, up, down, edge, keep, keep_ends, give, give_ends, side, fields, sems
):
    shot, gy = lax.axis_index("shot"), lax.axis_index("gy")
    _, rows, size_y, _ = fields.shape
    lines = size_y // KEEP_EVERY
    pieces = sems.shape[0]
    count = rows // pieces
    order = [0, pieces - 1] + list(range(1, pieces - 1))
    copies = {}
    for index in order:
        part = pl.ds(count * index, count)
        for field, ref in enumerate((source, receiver)):
            copies[index, field] = pltpu.make_async_copy(
                ref.at[0, part], fields.at[field, part], sems.at[index, field]
            )
            copies[index, field].start()

    def one_row(row, keep_ref, give_ref, to):
        parts = []
        for field in range(2):
            first, second = z_halves(fields[field, row, pl.ds(0, lines, stride=KEEP_EVERY), :])
            keep_ref[field, to] = jnp.where(shot == 0, first, second)
            give_ref[field, to] = jnp.where(shot == 0, second, first)
            low = fields[field, row, 0:REACH, :]
            high = fields[field, row, size_y - REACH : size_y, :]
            parts.append(jnp.where(gy == 0, high, low))
        side[row] = jnp.concatenate(parts, axis=0)

    def middle_row(row, carry):
        one_row(row, keep, give, row - REACH)
        return carry

    def end_rows(out, start, to):
        for row in range(REACH):
            for field in range(2):
                edge[field, to + row] = fields[field, start + row, pl.ds(0, lines, stride=KEEP_EVERY), :]
                for phase in range(1, KEEP_EVERY):
                    out[field, row, (phase - 1) * lines : phase * lines, :] = fields[
                        field, start + row, pl.ds(phase, lines, stride=KEEP_EVERY), :
                    ]
            one_row(start + row, keep_ends, give_ends, to + row)

    for index in order:
        for field in range(2):
            copies[index, field].wait()
        low, high = count * index, count * (index + 1)
        if index == 0:
            end_rows(down, 0, 0)
            low += REACH
        if index == pieces - 1:
            end_rows(up, rows - REACH, REACH)
            high -= REACH
        if low < high:
            lax.fori_loop(low, high, middle_row, 0, unroll=4)


def pack(source, receiver):
    _, rows, size_y, size_z = source.shape
    lines = size_y // KEEP_EVERY
    apart = jax.ShapeDtypeStruct((2, REACH, size_y - lines, size_z), F32)
    middle = jax.ShapeDtypeStruct((2, rows - 2 * REACH, lines // 2, size_z), F32)
    ends = jax.ShapeDtypeStruct((2, 2 * REACH, lines // 2, size_z), F32)
    return pl.pallas_call(
        pack_kernel,
        out_shape=(
            apart,
            apart,
            jax.ShapeDtypeStruct((2, 2 * REACH, lines, size_z), F32),
            middle,
            ends,
            middle,
            ends,
            jax.ShapeDtypeStruct((rows, 2 * REACH, size_z), F32),
        ),
        in_specs=[HBM, HBM],
        out_specs=(VMEM,) * 8,
        scratch_shapes=[
            pltpu.VMEM((2, rows, size_y, size_z), F32),
            pltpu.SemaphoreType.DMA((8, 2)),
        ],
        compiler_params=params(56),
        cost_estimate=cost(10**10, 7 * 2**20),
        name="pack",
    )(source, receiver)


def z_weights(size_z):
    z = lax.broadcasted_iota(jnp.int32, (8, size_z), 1)
    return [
        (jnp.where(z >= d, WEIGHTS[d], 0.0), jnp.where(z < size_z - d, WEIGHTS[d], 0.0))
        for d in range(1, REACH + 1)
    ]


def z_terms(center, masks):
    size_z = center.shape[1]
    center = center.reshape(-1, 8, size_z)
    total = None
    for d, (below, above) in enumerate(masks, start=1):
        term = below * pltpu.roll(center, d, 2) + above * pltpu.roll(center, size_z - d, 2)
        total = term if total is None else total + term
    return total.reshape(-1, size_z)


def z_matrix(size_z):
    z = np.arange(size_z)
    apart = np.abs(z[:, None] - z[None, :])
    weights = np.array((0.0,) + WEIGHTS[1:] + (0.0,), np.float32)[np.minimum(apart, REACH + 1)]
    high = weights.astype(jnp.bfloat16)
    low = (weights - high.astype(np.float32)).astype(jnp.bfloat16)
    return jnp.asarray(np.block([[high, low], [high, np.zeros_like(low)]]))


def z_product(lines, matrix):
    size_z = lines.shape[1]
    high = lines.astype(jnp.bfloat16)
    low = (lines - high.astype(F32)).astype(jnp.bfloat16)
    both = jnp.dot(jnp.concatenate([high, low], axis=1), matrix, preferred_element_type=F32)
    return both[:, :size_z] + both[:, size_z:]


def first_step(now, row, z_sums, before, before_row, scale, scale_row, after, field):
    size_y = before.shape[2]
    lines = size_y // KEEP_EVERY
    for phase in range(KEEP_EVERY):
        kept = lambda start: pl.ds(start, lines, stride=KEEP_EVERY)
        at = PAD + phase
        center = now[field, row, kept(at), :]
        total = (3.0 * WEIGHTS[0]) * center + z_sums[field, kept(phase), :]
        for d in range(1, REACH + 1):
            around = (
                now[field, row + d, kept(at), :]
                + now[field, row - d, kept(at), :]
                + now[field, row, kept(at + d), :]
                + now[field, row, kept(at - d), :]
            )
            total = total + WEIGHTS[d] * around
        after[field, row, kept(at), :] = (
            2.0 * center
            - before[field, before_row, kept(phase), :]
            + scale[scale_row, kept(phase), :] * total
        )


def second_step(now, row, scale, scale_row, after, field, z_sum):
    size_y = scale.shape[1]
    lines = size_y // KEEP_EVERY
    kept = lambda start: pl.ds(start, lines, stride=KEEP_EVERY)
    center = after[field, row, kept(PAD), :]
    total = (3.0 * WEIGHTS[0]) * center + z_sum
    for d in range(1, REACH + 1):
        around = (
            after[field, row + d, kept(PAD), :]
            + after[field, row - d, kept(PAD), :]
            + after[field, row, kept(PAD + d), :]
            + after[field, row, kept(PAD - d), :]
        )
        total = total + WEIGHTS[d] * around
    return 2.0 * center - now[field, row, kept(PAD), :] + scale[scale_row, kept(0), :] * total


def side_term(after, after_row, field, size_y, gy):
    lowest = WEIGHTS[REACH] * after[field, after_row, PAD : PAD + 1, :]
    highest = sum(
        WEIGHTS[d] * after[field, after_row, PAD + size_y - d : PAD + size_y - d + 1, :]
        for d in range(1, REACH + 1)
    )
    return jnp.where(gy == 0, highest, lowest)


def fill_sides(now, row, got, field, size_y, gy):
    blank = jnp.zeros_like(got)
    now[field, row, PAD - REACH : PAD, :] = jnp.where(gy == 0, blank, got)
    now[field, row, size_y + PAD : size_y + PAD + REACH, :] = jnp.where(gy == 0, got, blank)


def blank_sides(after, row, field, size_y):
    blank = jnp.zeros((REACH, after.shape[3]), F32)
    after[field, row, PAD - REACH : PAD, :] = blank
    after[field, row, size_y + PAD : size_y + PAD + REACH, :] = blank


def steps_kernel(
    source, receiver, source_before, receiver_before, courant, side, matrix,
    partial, kept_courant, edge_courant, edge, side_out, now, before, scale, after, z_sums, sems,
):
    gy = lax.axis_index("gy")
    rows, size_y, size_z = courant.shape
    lines = size_y // KEEP_EVERY
    piece = 2 * REACH
    middle = pl.ds(PAD, size_y)

    def copies(index):
        part = pl.ds(piece * index, piece)
        found = []
        for field in range(2):
            src = (source, receiver)[field].at[0, part]
            dst = now.at[field, pl.ds(REACH + piece * index, piece), middle]
            found.append(pltpu.make_async_copy(src, dst, sems.at[index, field]))
        for field in range(2):
            src = (source_before, receiver_before)[field].at[0, part]
            found.append(pltpu.make_async_copy(src, before.at[field, part], sems.at[index, 2 + field]))
        found.append(pltpu.make_async_copy(courant.at[part], scale.at[part], sems.at[index, 4]))
        return found

    for index in range(rows // piece):
        for one in copies(index):
            one.start()

    for field in range(2):
        for row in list(range(REACH)) + list(range(rows + REACH, rows + 2 * REACH)):
            now[field, row] = jnp.zeros((size_y + 2 * PAD, size_z), F32)
            after[field, row] = jnp.zeros((size_y + 2 * PAD, size_z), F32)

    def fill(row, carry):
        for field in range(2):
            got = side[row, field * REACH : (field + 1) * REACH, :]
            fill_sides(now, row + REACH, got, field, size_y, gy)
            blank_sides(after, row + REACH, field, size_y)
        return carry

    lax.fori_loop(0, rows, fill, 0)
    for one in copies(0)[:2]:
        one.wait()

    def z_next(row):
        found = z_product(
            jnp.concatenate([now[field, row + REACH, middle, :] for field in range(2)], axis=0), matrix[...]
        )
        for field in range(2):
            z_sums[row % 2, field] = found[field * size_y : (field + 1) * size_y]

    z_next(0)

    def first(row, carry):
        @pl.when(row % piece == 0)
        def _():
            index = row // piece
            for one in copies(index)[2:]:
                one.wait()

            @pl.when(index + 1 < rows // piece)
            def _():
                for one in copies(index + 1)[:2]:
                    one.wait()

        at = row + REACH
        for field in range(2):
            first_step(now, at, z_sums.at[row % 2], before, row, scale, row, after, field)
        z_next(row + 1)
        for field in range(2):
            side_out[field, pl.ds(row, 1), :] = side_term(after, at, field, size_y, gy)
        return carry

    lax.fori_loop(0, rows, first, 0)

    def second(row, carry):
        at = row + REACH
        kept_courant[row] = scale[row, pl.ds(0, lines, stride=KEEP_EVERY), :]
        centers = [after[field, at, pl.ds(PAD, lines, stride=KEEP_EVERY), :] for field in range(2)]
        z_sum = z_product(jnp.concatenate(centers, axis=0), matrix[...])
        for field in range(2):
            partial[field, row] = second_step(
                now, at, scale, row, after, field, z_sum[field * lines : (field + 1) * lines]
            )
        return carry

    lax.fori_loop(0, rows, second, 0, unroll=2)
    for end in range(2):
        for row in range(REACH):
            at = rows - 1 - row if end else row
            edge_courant[end, row] = scale[at]
            for field in range(2):
                edge[field, end, row] = after[field, REACH + at, pl.ds(PAD, lines, stride=KEEP_EVERY), :]


def steps(source, receiver, source_before, receiver_before, courant, side):
    rows, size_y, size_z = courant.shape
    lines = size_y // KEEP_EVERY
    return pl.pallas_call(
        steps_kernel,
        out_shape=(
            jax.ShapeDtypeStruct((2, rows, lines, size_z), F32),
            jax.ShapeDtypeStruct((rows, lines, size_z), F32),
            jax.ShapeDtypeStruct((2, REACH, size_y, size_z), F32),
            jax.ShapeDtypeStruct((2, 2, REACH, lines, size_z), F32),
            jax.ShapeDtypeStruct((2, rows, size_z), F32),
        ),
        in_specs=[HBM] * 5 + [VMEM] * 2,
        out_specs=(VMEM,) * 5,
        scratch_shapes=[
            pltpu.VMEM((2, rows + 2 * REACH, size_y + 2 * PAD, size_z), F32),
            pltpu.VMEM((2, rows, size_y, size_z), F32),
            pltpu.VMEM((rows, size_y, size_z), F32),
            pltpu.VMEM((2, rows + 2 * REACH, size_y + 2 * PAD, size_z), F32),
            pltpu.VMEM((2, 2, size_y, size_z), F32),
            pltpu.SemaphoreType.DMA((rows // (2 * REACH), 5)),
        ],
        compiler_params=params(STEPS_MIB),
        cost_estimate=cost(2 * 10**10, 2**20),
        name="steps",
    )(source, receiver, source_before, receiver_before, courant, side, z_matrix(size_z))


def mend_kernel(
    left, right, near, far, partial, kept_courant, edge_courant, edge, side_in,
    ends, up, down, side_out, keep, give, added,
):
    gy, shot = lax.axis_index("gy"), lax.axis_index("shot")
    even = lax.axis_index("gx") % 2 == 0
    rows, lines, size_z = kept_courant.shape
    size_y = KEEP_EVERY * lines
    masks = z_weights(size_z)
    kept = lambda start: pl.ds(start, lines, stride=KEEP_EVERY)
    side_out[...] = side_in[...]
    for end in range(2):
        for field in range(2):
            group = 2 * end + field
            for row in range(REACH):
                blank_sides(added, row, group, size_y)
                for phase in range(KEEP_EVERY):
                    total = None
                    for d in range(row + 1, REACH + 1):
                        beyond = d - row - 1
                        at = beyond if end else REACH - 1 - beyond
                        if phase:
                            halo = (right if end else left)[field, at, (phase - 1) * lines : phase * lines, :]
                        elif end:
                            halo = jnp.where(even, near[field, at], far[field, at])
                        else:
                            halo = jnp.where(even, far[field, REACH + at], near[field, REACH + at])
                        term = WEIGHTS[d] * halo
                        total = term if total is None else total + term
                    scaled = edge_courant[end, row, pl.ds(phase, lines, stride=KEEP_EVERY), :]
                    added[group, row, kept(PAD + phase), :] = scaled * total
            for row in range(2 * REACH):
                at = rows - 1 - row if end else row
                total = None
                for other in range(REACH):
                    if 0 < abs(row - other) <= REACH:
                        term = WEIGHTS[abs(row - other)] * added[group, other, kept(PAD), :]
                        total = term if total is None else total + term
                value = partial[field, at]
                if row < REACH:
                    center = added[group, row, kept(PAD), :]
                    total = total + (3.0 * WEIGHTS[0]) * center + z_terms(center, masks)
                    for d in range(1, REACH + 1):
                        around = added[group, row, kept(PAD + d), :] + added[group, row, kept(PAD - d), :]
                        total = total + WEIGHTS[d] * around
                    value = value + 2.0 * center
                    first = edge[field, end, row] + center
                    if end:
                        up[field, REACH - 1 - row] = first
                    else:
                        down[field, row] = first
                    side_out[field, at : at + 1, :] = side_in[field, at : at + 1, :] + side_term(
                        added, row, group, size_y, gy
                    )
                ends[field, end, row] = value + kept_courant[at] * total
    for kind, ref in enumerate((near, far)):
        for field in range(2):
            for row in range(2 * REACH):
                pack_row(ref[field, row], field, row, shot, keep.at[kind], give.at[kind])


def mend(left, right, near, far, partial, kept_courant, edge_courant, edge, side_in):
    rows, lines, size_z = kept_courant.shape
    halo = jax.ShapeDtypeStruct((2, REACH, lines, size_z), F32)
    half = jax.ShapeDtypeStruct((2, 2, 2 * REACH, lines // 2, size_z), F32)
    return pl.pallas_call(
        mend_kernel,
        out_shape=(
            jax.ShapeDtypeStruct((2, 2, 2 * REACH, lines, size_z), F32),
            halo,
            halo,
            jax.ShapeDtypeStruct((2, rows, size_z), F32),
            half,
            half,
        ),
        in_specs=[VMEM] * 9,
        out_specs=(VMEM,) * 6,
        scratch_shapes=[pltpu.VMEM((4, REACH, KEEP_EVERY * lines + 2 * PAD, size_z), F32)],
        compiler_params=params(24),
        cost_estimate=cost(10**6, 2**20),
        name="mend",
    )(left, right, near, far, partial, kept_courant, edge_courant, edge, side_in)


def pack_row(value, field, row, shot, keep, give):
    first, second = z_halves(value)
    keep[field, row] = jnp.where(shot == 0, first, second)
    give[field, row] = jnp.where(shot == 0, second, first)


def side_lines(side, field, row, gy, lines):
    line = lax.broadcasted_iota(jnp.int32, (lines, side.shape[2]), 0)
    meets = line == jnp.where(gy == 0, lines - 1, 0)
    return jnp.where(meets, side[field, pl.ds(row, 1), :], 0.0)


def middle_kernel(partial, ends, kept_courant, side, keep, give):
    shot, gy = lax.axis_index("shot"), lax.axis_index("gy")
    rows, lines, _ = kept_courant.shape

    def one_row(row, values):
        for field in range(2):
            total = side_lines(side, field, row, gy, lines)
            pack_row(values[field] + kept_courant[row] * total, field, row - REACH, shot, keep, give)

    def middle(row, carry):
        one_row(row, [partial[field, row] for field in range(2)])
        return carry

    lax.fori_loop(2 * REACH, rows - 2 * REACH, middle, 0)
    for row in range(REACH, 2 * REACH):
        one_row(row, [ends[field, 0, row] for field in range(2)])
        one_row(rows - 1 - row, [ends[field, 1, row] for field in range(2)])


def finish_middle(partial, ends, kept_courant, side):
    rows, lines, size_z = kept_courant.shape
    half = jax.ShapeDtypeStruct((2, rows - 2 * REACH, lines // 2, size_z), F32)
    return pl.pallas_call(
        middle_kernel,
        out_shape=(half, half),
        in_specs=[VMEM] * 4,
        out_specs=(VMEM,) * 2,
        compiler_params=params(24),
        cost_estimate=cost(1, 1),
        name="finish_middle",
    )(partial, ends, kept_courant, side)


def ends_kernel(ends, kept_courant, left, right, side, keep, give):
    shot, gy = lax.axis_index("shot"), lax.axis_index("gy")
    rows, lines, _ = kept_courant.shape
    for field in range(2):
        for row in range(REACH):
            below = above = None
            for d in range(row + 1, REACH + 1):
                term = WEIGHTS[d] * left[field, REACH + row - d]
                below = term if below is None else below + term
                term = WEIGHTS[d] * right[field, d - 1 - row]
                above = term if above is None else above + term
            far = rows - 1 - row
            below = below + side_lines(side, field, row, gy, lines)
            above = above + side_lines(side, field, far, gy, lines)
            pack_row(ends[field, 0, row] + kept_courant[row] * below, field, row, shot, keep, give)
            pack_row(
                ends[field, 1, row] + kept_courant[far] * above,
                field, 2 * REACH - 1 - row, shot, keep, give,
            )


def finish_ends(ends, kept_courant, left, right, side):
    _, lines, size_z = kept_courant.shape
    half = jax.ShapeDtypeStruct((2, 2 * REACH, lines // 2, size_z), F32)
    return pl.pallas_call(
        ends_kernel,
        out_shape=(half, half),
        in_specs=[VMEM] * 5,
        out_specs=(VMEM,) * 2,
        compiler_params=params(24),
        cost_estimate=cost(10**10, 3 * 2**20),
        name="finish_ends",
    )(ends, kept_courant, left, right, side)


def block_starts(rows):
    even = lax.axis_index("gx") % 2 == 0
    return HALF, jnp.where(even, HALF + rows, 0), jnp.where(even, 0, HALF + rows)


def products(rows_of, sample, shift, here):
    total = None
    for group in range(rows_of.shape[0]):
        term = (
            rows_of[group, 0, 2 * HALF + sample - shift, here, :]
            * rows_of[group, 1, sample + shift, here, :]
        )
        total = term if total is None else total + term
    return total


def layout_copies(middles, ends, middle_starts, end_starts, rows_of, sems):
    copies = []

    def copy(src, part, start, count):
        dst = rows_of.at[part, :, pl.ds(start, count)]
        copies.append(pltpu.make_async_copy(src, dst, sems.at[len(copies)]))

    count = middles[0][0].shape[1]
    for part in range(2):
        for src, start in zip(middles[part], middle_starts):
            copy(src, part, start + REACH, count)
        for src, start in zip(ends[part], end_starts):
            copy(src.at[:, pl.ds(0, REACH)], part, start, REACH)
            copy(src.at[:, pl.ds(REACH, REACH)], part, start + REACH + count, REACH)
    return copies


def first_image_kernel(*refs):
    blocks, (out, rows_of, sems) = refs[:10], refs[10:]
    rows = blocks[0].shape[1] + 2 * REACH

    @pl.when(pl.program_id(0) == 0)
    def _():
        starts = block_starts(rows)
        ends = [[blocks[6 + part], blocks[8 + part].at[0], blocks[8 + part].at[1]] for part in range(2)]
        run_copies(layout_copies([blocks[:3], blocks[3:6]], ends, starts, starts, rows_of, sems))

    sample = 4 * pl.program_id(0)
    for chunk in range(rows_of.shape[3] // 8):
        here = pl.ds(8 * chunk, 8)
        for shift in range(OFFSETS):
            out[0, shift, here, :] = products(rows_of, sample, shift, here)


def first_image(blocks):
    _, middle_rows, lines, size_z = blocks[0].shape
    rows = middle_rows + 2 * REACH
    samples = rows // 4
    return pl.pallas_call(
        first_image_kernel,
        grid=(samples,),
        out_shape=jax.ShapeDtypeStruct((samples, OFFSETS, lines, size_z), F32),
        in_specs=[ANY] * len(blocks),
        out_specs=pl.BlockSpec((1, OFFSETS, lines, size_z), lambda i: (i, 0, 0, 0)),
        scratch_shapes=[
            pltpu.VMEM((2, 2, rows + 2 * HALF, lines, size_z), F32),
            pltpu.SemaphoreType.DMA((18,)),
        ],
        compiler_params=params(16),
        cost_estimate=cost(10**10, 8 * 2**20),
        name="first_image",
    )(*blocks)


def image_kernel(token, first, *refs):
    blocks, (out, rows_of, turned, staged, sems, out_sems) = refs[:9], refs[9:]
    rows = blocks[0].shape[1] + 2 * REACH
    step, steps_in_all = pl.program_id(0), pl.num_programs(0)

    @pl.when(step == 0)
    def _():
        ends = [[ref.at[part] for ref in blocks[6:]] for part in range(2)]
        end_starts = (HALF, 0, HALF + rows)
        run_copies(
            layout_copies([blocks[:3], blocks[3:6]], ends, block_starts(rows), end_starts, rows_of, sems)
        )

    lines, size_z = rows_of.shape[3], rows_of.shape[4]
    chunks = lines // 8

    def leave(at_step, chunk, half):
        slot = at_step % 2
        here = pl.ds(half * lines + 8 * chunk, 8)
        return pltpu.make_async_copy(staged.at[slot, here], out.at[at_step, here], out_sems.at[slot, chunk, half])

    sample = 4 * step
    for chunk in range(chunks):
        here = pl.ds(8 * chunk, 8)
        for shift in range(OFFSETS):
            total = first[0, shift, here, :] + products(rows_of, sample, shift, here)
            turned[chunk, pl.ds(shift, 8, stride=OFFSET_ROWS), :] = total

        @pl.when(step >= 2)
        def _():
            for half in range(2):
                leave(step - 2, chunk, half).wait()

        for line in range(8):
            values = turned[chunk, line * OFFSET_ROWS : (line + 1) * OFFSET_ROWS, :].T
            at = 8 * chunk + line
            staged[step % 2, at] = values[: size_z // 2, :OFFSETS]
            staged[step % 2, lines + at] = values[size_z // 2 :, :OFFSETS]
        for half in range(2):
            leave(step, chunk, half).start()

    @pl.when(step == steps_in_all - 1)
    def _():
        for back in (1, 0):
            for chunk in range(chunks):
                for half in range(2):
                    leave(step - back, chunk, half).wait()


def image(token, first, blocks):
    samples, _, lines, size_z = first.shape
    rows = 4 * samples
    return pl.pallas_call(
        image_kernel,
        grid=(samples,),
        out_shape=jax.ShapeDtypeStruct((samples, 2 * lines, size_z // 2, OFFSETS), F32),
        in_specs=[SMEM, pl.BlockSpec((1, OFFSETS, lines, size_z), lambda i: (i, 0, 0, 0))] + [ANY] * len(blocks),
        out_specs=HBM,
        scratch_shapes=[
            pltpu.VMEM((2, 2, rows + 2 * HALF, lines, size_z), F32),
            pltpu.VMEM((lines // 8, 8 * OFFSET_ROWS, size_z), F32),
            pltpu.VMEM((2, 2 * lines, size_z // 2, OFFSETS), F32),
            pltpu.SemaphoreType.DMA((18,)),
            pltpu.SemaphoreType.DMA((2, lines // 8, 2)),
        ],
        compiler_params=params(20),
        cost_estimate=cost(10**10, 16 * 2**20),
        name="image",
    )(token, first, *blocks)


def in_order_kernel(*refs):
    refs[-1][0] = 0


def in_order(*arrays):
    return pl.pallas_call(
        in_order_kernel,
        out_shape=jax.ShapeDtypeStruct((1,), jnp.int32),
        in_specs=[ANY] * len(arrays),
        out_specs=SMEM,
        compiler_params=params(1),
        cost_estimate=cost(1, 1),
        name="in_order",
    )(*arrays)


def on_device(source_now, source_before, receiver_now, receiver_before, courant):
    size = lax.axis_size("gx")
    up_pairs = [(i, i + 1) for i in range(size - 1)]
    down_pairs = [(j, i) for i, j in up_pairs]
    partner = [(i, i ^ 1) for i in range(size)]
    onward = [(i, i + 2) for i in range(0, size - 2, 2)] + [(i, i - 2) for i in range(3, size, 2)]
    both = [(0, 1), (1, 0)]

    def exchange(array, axis, pairs):
        return lax.ppermute(array, axis, pairs)

    barrier = lax.optimization_barrier
    up, down, edge, keep, keep_ends, give, give_ends, side = pack(source_now, receiver_now)
    near_edge = exchange(edge, "gx", partner)
    left = exchange(up, "gx", up_pairs)
    right = exchange(down, "gx", down_pairs)
    side = exchange(side, "gy", both)
    other = exchange(give, "shot", both)
    other_ends = exchange(give_ends, "shot", both)
    side, keep, other = barrier((side, keep, other))
    near_keep = exchange(keep, "gx", partner)
    near_other = exchange(other, "gx", partner)
    blocks = [keep, near_keep, None, other, near_other, None, keep_ends, other_ends]
    partial, kept_courant, edge_courant, edge, side = steps(
        source_now, receiver_now, source_before, receiver_before, courant, side
    )
    near_edge, side = barrier((near_edge, side))
    far_edge = exchange(near_edge, "gx", onward)
    ends, up, down, side, keep_edges, give_edges = mend(
        left, right, near_edge, far_edge, partial, kept_courant, edge_courant, edge, side
    )
    blocks += [keep_edges, exchange(give_edges, "shot", both)]
    left = exchange(up, "gx", up_pairs)
    right = exchange(down, "gx", down_pairs)
    side = exchange(side, "gy", both)
    side, near_keep, blocks[7], blocks[9] = barrier((side, near_keep, blocks[7], blocks[9]))
    far_keep = exchange(near_keep, "gx", onward)

    keep, give = finish_middle(partial, ends, kept_courant, side)
    other = exchange(give, "shot", both)
    near_keep = exchange(keep, "gx", partner)

    left, right, blocks[2], blocks[4] = barrier((left, right, far_keep, near_other))
    blocks[5] = exchange(blocks[4], "gx", onward)
    keep_ends, give_ends = finish_ends(ends, kept_courant, left, right, side)
    other, keep_ends, give_ends = barrier((other, keep_ends, give_ends))
    near_other = exchange(other, "gx", partner)
    other_ends = exchange(give_ends, "shot", both)
    other_ends, near_keep = barrier((other_ends, near_keep))
    own = jnp.stack([keep_ends, other_ends])
    far_keep = exchange(near_keep, "gx", onward)
    left = exchange(own, "gx", up_pairs)
    right = exchange(own, "gx", down_pairs)
    far_other = exchange(near_other, "gx", onward)
    blocks[5], far_keep = lax.optimization_barrier((blocks[5], far_keep))
    first = first_image(blocks)
    token = in_order(left, right, first)
    blocks = [keep, near_keep, far_keep, other, near_other, far_other, own, left, right]
    return jnp.transpose(image(token, first, blocks), (3, 0, 1, 2))


def solution(mesh):
    in_specs = (
        P("shot", "gx", "gy", None),
        P("shot", "gx", "gy", None),
        P("shot", "gx", "gy", None),
        P("shot", "gx", "gy", None),
        P("gx", "gy", None),
    )
    out_specs = P(None, "gx", "gy", "shot")
    return jax.shard_map(
        on_device, mesh=mesh, in_specs=in_specs, out_specs=out_specs, check_vma=False
    )
```

```python
import functools

import jax
import jax.numpy as jnp
import numpy as np
from jax import lax
from jax.experimental import pallas as pl
from jax.experimental.pallas import tpu as pltpu
from jax.sharding import PartitionSpec as P

HALF = 32
REACH = 4
KEEP_EVERY = 4
OFFSETS = 2 * HALF + 1
OFFSET_ROWS = 72
LINES = 32
STEPS_MIB = 50
WEIGHTS = (-205.0 / 72.0, 8.0 / 5.0, -1.0 / 5.0, 8.0 / 315.0, -1.0 / 560.0)
PAD = 8
F32 = jnp.float32
HBM = pl.BlockSpec(memory_space=pltpu.HBM)
ANY = pl.BlockSpec(memory_space=pl.ANY)
VMEM = pl.BlockSpec(memory_space=pltpu.VMEM)
SMEM = pl.BlockSpec(memory_space=pltpu.SMEM)


def params(mib):
    return pltpu.CompilerParams(vmem_limit_bytes=mib * 2**20)


def cost(flops, nbytes):
    return pl.CostEstimate(flops=flops, bytes_accessed=nbytes, transcendentals=0)


def run_copies(copies):
    for copy in copies:
        copy.start()
    for copy in copies:
        copy.wait()


def z_halves(lines):
    count, size_z = lines.shape
    top, bottom = lines[: count // 2], lines[count // 2 :]
    low = lax.broadcasted_iota(jnp.int32, top.shape, 1) < size_z // 2
    first = jnp.where(low, top, pltpu.roll(bottom, size_z // 2, 1))
    second = jnp.where(low, pltpu.roll(top, size_z // 2, 1), bottom)
    return first, second


def pack_kernel(
    source, receiver, up, down, edge, keep, keep_ends, give, give_ends, side, fields, sems
):
    shot, gy = lax.axis_index("shot"), lax.axis_index("gy")
    _, rows, size_y, _ = fields.shape
    lines = size_y // KEEP_EVERY
    pieces = sems.shape[0]
    count = rows // pieces
    order = [0, pieces - 1] + list(range(1, pieces - 1))
    copies = {}
    for index in order:
        part = pl.ds(count * index, count)
        for field, ref in enumerate((source, receiver)):
            copies[index, field] = pltpu.make_async_copy(
                ref.at[0, part], fields.at[field, part], sems.at[index, field]
            )
            copies[index, field].start()

    def one_row(row, keep_ref, give_ref, to):
        parts = []
        for field in range(2):
            first, second = z_halves(fields[field, row, pl.ds(0, lines, stride=KEEP_EVERY), :])
            keep_ref[field, to] = jnp.where(shot == 0, first, second)
            give_ref[field, to] = jnp.where(shot == 0, second, first)
            low = fields[field, row, 0:REACH, :]
            high = fields[field, row, size_y - REACH : size_y, :]
            parts.append(jnp.where(gy == 0, high, low))
        side[row] = jnp.concatenate(parts, axis=0)

    def middle_row(row, carry):
        one_row(row, keep, give, row - REACH)
        return carry

    def end_rows(out, start, to):
        for row in range(REACH):
            for field in range(2):
                edge[field, to + row] = fields[field, start + row, pl.ds(0, lines, stride=KEEP_EVERY), :]
                for phase in range(1, KEEP_EVERY):
                    out[field, row, (phase - 1) * lines : phase * lines, :] = fields[
                        field, start + row, pl.ds(phase, lines, stride=KEEP_EVERY), :
                    ]
            one_row(start + row, keep_ends, give_ends, to + row)

    for index in order:
        for field in range(2):
            copies[index, field].wait()
        low, high = count * index, count * (index + 1)
        if index == 0:
            end_rows(down, 0, 0)
            low += REACH
        if index == pieces - 1:
            end_rows(up, rows - REACH, REACH)
            high -= REACH
        if low < high:
            lax.fori_loop(low, high, middle_row, 0, unroll=4)


def pack(source, receiver):
    _, rows, size_y, size_z = source.shape
    lines = size_y // KEEP_EVERY
    apart = jax.ShapeDtypeStruct((2, REACH, size_y - lines, size_z), F32)
    middle = jax.ShapeDtypeStruct((2, rows - 2 * REACH, lines // 2, size_z), F32)
    ends = jax.ShapeDtypeStruct((2, 2 * REACH, lines // 2, size_z), F32)
    return pl.pallas_call(
        pack_kernel,
        out_shape=(
            apart,
            apart,
            jax.ShapeDtypeStruct((2, 2 * REACH, lines, size_z), F32),
            middle,
            ends,
            middle,
            ends,
            jax.ShapeDtypeStruct((rows, 2 * REACH, size_z), F32),
        ),
        in_specs=[HBM, HBM],
        out_specs=(VMEM,) * 8,
        scratch_shapes=[
            pltpu.VMEM((2, rows, size_y, size_z), F32),
            pltpu.SemaphoreType.DMA((8, 2)),
        ],
        compiler_params=params(56),
        cost_estimate=cost(10**10, 7 * 2**20),
        name="pack",
    )(source, receiver)


def z_weights(size_z):
    z = lax.broadcasted_iota(jnp.int32, (8, size_z), 1)
    return [
        (jnp.where(z >= d, WEIGHTS[d], 0.0), jnp.where(z < size_z - d, WEIGHTS[d], 0.0))
        for d in range(1, REACH + 1)
    ]


def z_terms(center, masks):
    size_z = center.shape[1]
    center = center.reshape(-1, 8, size_z)
    total = None
    for d, (below, above) in enumerate(masks, start=1):
        term = below * pltpu.roll(center, d, 2) + above * pltpu.roll(center, size_z - d, 2)
        total = term if total is None else total + term
    return total.reshape(-1, size_z)


def z_matrix(size_z):
    z = np.arange(size_z)
    apart = np.abs(z[:, None] - z[None, :])
    weights = np.array((0.0,) + WEIGHTS[1:] + (0.0,), np.float32)[np.minimum(apart, REACH + 1)]
    high = weights.astype(jnp.bfloat16)
    low = (weights - high.astype(np.float32)).astype(jnp.bfloat16)
    return jnp.asarray(np.block([[high, low], [high, np.zeros_like(low)]]))


def z_product(lines, matrix):
    size_z = lines.shape[1]
    high = lines.astype(jnp.bfloat16)
    low = (lines - high.astype(F32)).astype(jnp.bfloat16)
    both = jnp.dot(jnp.concatenate([high, low], axis=1), matrix, preferred_element_type=F32)
    return both[:, :size_z] + both[:, size_z:]


def first_step(now, row, z_sums, before, before_row, scale, scale_row, after, field):
    size_y = before.shape[2]
    lines = size_y // KEEP_EVERY
    for phase in range(KEEP_EVERY):
        kept = lambda start: pl.ds(start, lines, stride=KEEP_EVERY)
        at = PAD + phase
        center = now[field, row, kept(at), :]
        total = (3.0 * WEIGHTS[0]) * center + z_sums[field, kept(phase), :]
        for d in range(1, REACH + 1):
            around = (
                now[field, row + d, kept(at), :]
                + now[field, row - d, kept(at), :]
                + now[field, row, kept(at + d), :]
                + now[field, row, kept(at - d), :]
            )
            total = total + WEIGHTS[d] * around
        after[field, row, kept(at), :] = (
            2.0 * center
            - before[field, before_row, kept(phase), :]
            + scale[scale_row, kept(phase), :] * total
        )


def second_step(now, row, scale, scale_row, after, field, z_sum):
    size_y = scale.shape[1]
    lines = size_y // KEEP_EVERY
    kept = lambda start: pl.ds(start, lines, stride=KEEP_EVERY)
    center = after[field, row, kept(PAD), :]
    total = (3.0 * WEIGHTS[0]) * center + z_sum
    for d in range(1, REACH + 1):
        around = (
            after[field, row + d, kept(PAD), :]
            + after[field, row - d, kept(PAD), :]
            + after[field, row, kept(PAD + d), :]
            + after[field, row, kept(PAD - d), :]
        )
        total = total + WEIGHTS[d] * around
    return 2.0 * center - now[field, row, kept(PAD), :] + scale[scale_row, kept(0), :] * total


def side_term(after, after_row, field, size_y, gy):
    lowest = WEIGHTS[REACH] * after[field, after_row, PAD : PAD + 1, :]
    highest = sum(
        WEIGHTS[d] * after[field, after_row, PAD + size_y - d : PAD + size_y - d + 1, :]
        for d in range(1, REACH + 1)
    )
    return jnp.where(gy == 0, highest, lowest)


def fill_sides(now, row, got, field, size_y, gy):
    blank = jnp.zeros_like(got)
    now[field, row, PAD - REACH : PAD, :] = jnp.where(gy == 0, blank, got)
    now[field, row, size_y + PAD : size_y + PAD + REACH, :] = jnp.where(gy == 0, got, blank)


def blank_sides(after, row, field, size_y):
    blank = jnp.zeros((REACH, after.shape[3]), F32)
    after[field, row, PAD - REACH : PAD, :] = blank
    after[field, row, size_y + PAD : size_y + PAD + REACH, :] = blank


def steps_kernel(
    source, receiver, source_before, receiver_before, courant, side, matrix,
    partial, kept_courant, edge_courant, edge, side_out, now, before, scale, after, z_sums, sems,
):
    gy = lax.axis_index("gy")
    rows, size_y, size_z = courant.shape
    lines = size_y // KEEP_EVERY
    piece = 2 * REACH
    middle = pl.ds(PAD, size_y)

    def copies(index):
        part = pl.ds(piece * index, piece)
        found = []
        for field in range(2):
            src = (source, receiver)[field].at[0, part]
            dst = now.at[field, pl.ds(REACH + piece * index, piece), middle]
            found.append(pltpu.make_async_copy(src, dst, sems.at[index, field]))
        for field in range(2):
            src = (source_before, receiver_before)[field].at[0, part]
            found.append(pltpu.make_async_copy(src, before.at[field, part], sems.at[index, 2 + field]))
        found.append(pltpu.make_async_copy(courant.at[part], scale.at[part], sems.at[index, 4]))
        return found

    for index in range(rows // piece):
        for one in copies(index):
            one.start()

    for field in range(2):
        for row in list(range(REACH)) + list(range(rows + REACH, rows + 2 * REACH)):
            now[field, row] = jnp.zeros((size_y + 2 * PAD, size_z), F32)
            after[field, row] = jnp.zeros((size_y + 2 * PAD, size_z), F32)

    def fill(row, carry):
        for field in range(2):
            got = side[row, field * REACH : (field + 1) * REACH, :]
            fill_sides(now, row + REACH, got, field, size_y, gy)
            blank_sides(after, row + REACH, field, size_y)
        return carry

    lax.fori_loop(0, rows, fill, 0)
    for one in copies(0)[:2]:
        one.wait()

    def z_next(row):
        found = z_product(
            jnp.concatenate([now[field, row + REACH, middle, :] for field in range(2)], axis=0), matrix[...]
        )
        for field in range(2):
            z_sums[row % 2, field] = found[field * size_y : (field + 1) * size_y]

    z_next(0)

    def first(row, carry):
        @pl.when(row % piece == 0)
        def _():
            index = row // piece
            for one in copies(index)[2:]:
                one.wait()

            @pl.when(index + 1 < rows // piece)
            def _():
                for one in copies(index + 1)[:2]:
                    one.wait()

        at = row + REACH
        for field in range(2):
            first_step(now, at, z_sums.at[row % 2], before, row, scale, row, after, field)
        z_next(row + 1)
        for field in range(2):
            side_out[field, pl.ds(row, 1), :] = side_term(after, at, field, size_y, gy)
        return carry

    lax.fori_loop(0, rows, first, 0)

    def second(row, carry):
        at = row + REACH
        kept_courant[row] = scale[row, pl.ds(0, lines, stride=KEEP_EVERY), :]
        centers = [after[field, at, pl.ds(PAD, lines, stride=KEEP_EVERY), :] for field in range(2)]
        z_sum = z_product(jnp.concatenate(centers, axis=0), matrix[...])
        for field in range(2):
            partial[field, row] = second_step(
                now, at, scale, row, after, field, z_sum[field * lines : (field + 1) * lines]
            )
        return carry

    lax.fori_loop(0, rows, second, 0, unroll=2)
    for end in range(2):
        for row in range(REACH):
            at = rows - 1 - row if end else row
            edge_courant[end, row] = scale[at]
            for field in range(2):
                edge[field, end, row] = after[field, REACH + at, pl.ds(PAD, lines, stride=KEEP_EVERY), :]


def steps(source, receiver, source_before, receiver_before, courant, side):
    rows, size_y, size_z = courant.shape
    lines = size_y // KEEP_EVERY
    return pl.pallas_call(
        steps_kernel,
        out_shape=(
            jax.ShapeDtypeStruct((2, rows, lines, size_z), F32),
            jax.ShapeDtypeStruct((rows, lines, size_z), F32),
            jax.ShapeDtypeStruct((2, REACH, size_y, size_z), F32),
            jax.ShapeDtypeStruct((2, 2, REACH, lines, size_z), F32),
            jax.ShapeDtypeStruct((2, rows, size_z), F32),
        ),
        in_specs=[HBM] * 5 + [VMEM] * 2,
        out_specs=(VMEM,) * 5,
        scratch_shapes=[
            pltpu.VMEM((2, rows + 2 * REACH, size_y + 2 * PAD, size_z), F32),
            pltpu.VMEM((2, rows, size_y, size_z), F32),
            pltpu.VMEM((rows, size_y, size_z), F32),
            pltpu.VMEM((2, rows + 2 * REACH, size_y + 2 * PAD, size_z), F32),
            pltpu.VMEM((2, 2, size_y, size_z), F32),
            pltpu.SemaphoreType.DMA((rows // (2 * REACH), 5)),
        ],
        compiler_params=params(STEPS_MIB),
        cost_estimate=cost(2 * 10**10, 2**20),
        name="steps",
    )(source, receiver, source_before, receiver_before, courant, side, z_matrix(size_z))


def mend_kernel(
    left, right, near, far, partial, kept_courant, edge_courant, edge, side_in,
    ends, up, down, side_out, keep, give, added,
):
    gy, shot = lax.axis_index("gy"), lax.axis_index("shot")
    even = lax.axis_index("gx") % 2 == 0
    rows, lines, size_z = kept_courant.shape
    size_y = KEEP_EVERY * lines
    masks = z_weights(size_z)
    kept = lambda start: pl.ds(start, lines, stride=KEEP_EVERY)
    side_out[...] = side_in[...]
    for end in range(2):
        for field in range(2):
            group = 2 * end + field
            for row in range(REACH):
                blank_sides(added, row, group, size_y)
                for phase in range(KEEP_EVERY):
                    total = None
                    for d in range(row + 1, REACH + 1):
                        beyond = d - row - 1
                        at = beyond if end else REACH - 1 - beyond
                        if phase:
                            halo = (right if end else left)[field, at, (phase - 1) * lines : phase * lines, :]
                        elif end:
                            halo = jnp.where(even, near[field, at], far[field, at])
                        else:
                            halo = jnp.where(even, far[field, REACH + at], near[field, REACH + at])
                        term = WEIGHTS[d] * halo
                        total = term if total is None else total + term
                    scaled = edge_courant[end, row, pl.ds(phase, lines, stride=KEEP_EVERY), :]
                    added[group, row, kept(PAD + phase), :] = scaled * total
            for row in range(2 * REACH):
                at = rows - 1 - row if end else row
                total = None
                for other in range(REACH):
                    if 0 < abs(row - other) <= REACH:
                        term = WEIGHTS[abs(row - other)] * added[group, other, kept(PAD), :]
                        total = term if total is None else total + term
                value = partial[field, at]
                if row < REACH:
                    center = added[group, row, kept(PAD), :]
                    total = total + (3.0 * WEIGHTS[0]) * center + z_terms(center, masks)
                    for d in range(1, REACH + 1):
                        around = added[group, row, kept(PAD + d), :] + added[group, row, kept(PAD - d), :]
                        total = total + WEIGHTS[d] * around
                    value = value + 2.0 * center
                    first = edge[field, end, row] + center
                    if end:
                        up[field, REACH - 1 - row] = first
                    else:
                        down[field, row] = first
                    side_out[field, at : at + 1, :] = side_in[field, at : at + 1, :] + side_term(
                        added, row, group, size_y, gy
                    )
                ends[field, end, row] = value + kept_courant[at] * total
    for kind, ref in enumerate((near, far)):
        for field in range(2):
            for row in range(2 * REACH):
                pack_row(ref[field, row], field, row, shot, keep.at[kind], give.at[kind])


def mend(left, right, near, far, partial, kept_courant, edge_courant, edge, side_in):
    rows, lines, size_z = kept_courant.shape
    halo = jax.ShapeDtypeStruct((2, REACH, lines, size_z), F32)
    half = jax.ShapeDtypeStruct((2, 2, 2 * REACH, lines // 2, size_z), F32)
    return pl.pallas_call(
        mend_kernel,
        out_shape=(
            jax.ShapeDtypeStruct((2, 2, 2 * REACH, lines, size_z), F32),
            halo,
            halo,
            jax.ShapeDtypeStruct((2, rows, size_z), F32),
            half,
            half,
        ),
        in_specs=[VMEM] * 9,
        out_specs=(VMEM,) * 6,
        scratch_shapes=[pltpu.VMEM((4, REACH, KEEP_EVERY * lines + 2 * PAD, size_z), F32)],
        compiler_params=params(24),
        cost_estimate=cost(10**6, 2**20),
        name="mend",
    )(left, right, near, far, partial, kept_courant, edge_courant, edge, side_in)


def pack_row(value, field, row, shot, keep, give):
    first, second = z_halves(value)
    keep[field, row] = jnp.where(shot == 0, first, second)
    give[field, row] = jnp.where(shot == 0, second, first)


def side_lines(side, field, row, gy, lines):
    line = lax.broadcasted_iota(jnp.int32, (lines, side.shape[2]), 0)
    meets = line == jnp.where(gy == 0, lines - 1, 0)
    return jnp.where(meets, side[field, pl.ds(row, 1), :], 0.0)


def middle_kernel(partial, ends, kept_courant, side, keep, give):
    shot, gy = lax.axis_index("shot"), lax.axis_index("gy")
    rows, lines, _ = kept_courant.shape

    def one_row(row, values):
        for field in range(2):
            total = side_lines(side, field, row, gy, lines)
            pack_row(values[field] + kept_courant[row] * total, field, row - REACH, shot, keep, give)

    def middle(row, carry):
        one_row(row, [partial[field, row] for field in range(2)])
        return carry

    lax.fori_loop(2 * REACH, rows - 2 * REACH, middle, 0)
    for row in range(REACH, 2 * REACH):
        one_row(row, [ends[field, 0, row] for field in range(2)])
        one_row(rows - 1 - row, [ends[field, 1, row] for field in range(2)])


def finish_middle(partial, ends, kept_courant, side):
    rows, lines, size_z = kept_courant.shape
    half = jax.ShapeDtypeStruct((2, rows - 2 * REACH, lines // 2, size_z), F32)
    return pl.pallas_call(
        middle_kernel,
        out_shape=(half, half),
        in_specs=[VMEM] * 4,
        out_specs=(VMEM,) * 2,
        compiler_params=params(24),
        cost_estimate=cost(1, 1),
        name="finish_middle",
    )(partial, ends, kept_courant, side)


def ends_kernel(ends, kept_courant, left, right, side, keep, give):
    shot, gy = lax.axis_index("shot"), lax.axis_index("gy")
    rows, lines, _ = kept_courant.shape
    for field in range(2):
        for row in range(REACH):
            below = above = None
            for d in range(row + 1, REACH + 1):
                term = WEIGHTS[d] * left[field, REACH + row - d]
                below = term if below is None else below + term
                term = WEIGHTS[d] * right[field, d - 1 - row]
                above = term if above is None else above + term
            far = rows - 1 - row
            below = below + side_lines(side, field, row, gy, lines)
            above = above + side_lines(side, field, far, gy, lines)
            pack_row(ends[field, 0, row] + kept_courant[row] * below, field, row, shot, keep, give)
            pack_row(
                ends[field, 1, row] + kept_courant[far] * above,
                field, 2 * REACH - 1 - row, shot, keep, give,
            )


def finish_ends(ends, kept_courant, left, right, side):
    _, lines, size_z = kept_courant.shape
    half = jax.ShapeDtypeStruct((2, 2 * REACH, lines // 2, size_z), F32)
    return pl.pallas_call(
        ends_kernel,
        out_shape=(half, half),
        in_specs=[VMEM] * 5,
        out_specs=(VMEM,) * 2,
        compiler_params=params(24),
        cost_estimate=cost(10**10, 3 * 2**20),
        name="finish_ends",
    )(ends, kept_courant, left, right, side)


def block_starts(rows):
    even = lax.axis_index("gx") % 2 == 0
    return HALF, jnp.where(even, HALF + rows, 0), jnp.where(even, 0, HALF + rows)


def products(rows_of, sample, shift, here):
    total = None
    for group in range(rows_of.shape[0]):
        term = (
            rows_of[group, 0, 2 * HALF + sample - shift, here, :]
            * rows_of[group, 1, sample + shift, here, :]
        )
        total = term if total is None else total + term
    return total


def layout_copies(middles, ends, middle_starts, end_starts, rows_of, sems):
    copies = []

    def copy(src, part, start, count):
        dst = rows_of.at[part, :, pl.ds(start, count)]
        copies.append(pltpu.make_async_copy(src, dst, sems.at[len(copies)]))

    count = middles[0][0].shape[1]
    for part in range(2):
        for src, start in zip(middles[part], middle_starts):
            copy(src, part, start + REACH, count)
        for src, start in zip(ends[part], end_starts):
            copy(src.at[:, pl.ds(0, REACH)], part, start, REACH)
            copy(src.at[:, pl.ds(REACH, REACH)], part, start + REACH + count, REACH)
    return copies


def first_image_kernel(*refs):
    blocks, (out, rows_of, sems) = refs[:10], refs[10:]
    rows = blocks[0].shape[1] + 2 * REACH

    @pl.when(pl.program_id(0) == 0)
    def _():
        starts = block_starts(rows)
        ends = [[blocks[6 + part], blocks[8 + part].at[0], blocks[8 + part].at[1]] for part in range(2)]
        run_copies(layout_copies([blocks[:3], blocks[3:6]], ends, starts, starts, rows_of, sems))

    sample = 4 * pl.program_id(0)
    for chunk in range(rows_of.shape[3] // 8):
        here = pl.ds(8 * chunk, 8)
        for shift in range(OFFSETS):
            out[0, shift, here, :] = products(rows_of, sample, shift, here)


def first_image(blocks):
    _, middle_rows, lines, size_z = blocks[0].shape
    rows = middle_rows + 2 * REACH
    samples = rows // 4
    return pl.pallas_call(
        first_image_kernel,
        grid=(samples,),
        out_shape=jax.ShapeDtypeStruct((samples, OFFSETS, lines, size_z), F32),
        in_specs=[ANY] * len(blocks),
        out_specs=pl.BlockSpec((1, OFFSETS, lines, size_z), lambda i: (i, 0, 0, 0)),
        scratch_shapes=[
            pltpu.VMEM((2, 2, rows + 2 * HALF, lines, size_z), F32),
            pltpu.SemaphoreType.DMA((18,)),
        ],
        compiler_params=params(16),
        cost_estimate=cost(10**10, 8 * 2**20),
        name="first_image",
    )(*blocks)


def image_kernel(token, first, *refs):
    blocks, (out, rows_of, turned, staged, sems, out_sems) = refs[:9], refs[9:]
    rows = blocks[0].shape[1] + 2 * REACH
    step, steps_in_all = pl.program_id(0), pl.num_programs(0)

    @pl.when(step == 0)
    def _():
        ends = [[ref.at[part] for ref in blocks[6:]] for part in range(2)]
        end_starts = (HALF, 0, HALF + rows)
        run_copies(
            layout_copies([blocks[:3], blocks[3:6]], ends, block_starts(rows), end_starts, rows_of, sems)
        )

    lines, size_z = rows_of.shape[3], rows_of.shape[4]
    chunks = lines // 8

    def leave(at_step, chunk, half):
        slot = at_step % 2
        here = pl.ds(half * lines + 4 * chunk, 4)
        return pltpu.make_async_copy(staged.at[slot, here], out.at[at_step, here], out_sems.at[slot, chunk, half])

    sample = 4 * step
    for chunk in range(chunks):
        here = pl.ds(8 * chunk, 8)
        for shift in range(OFFSETS):
            total = first[0, shift, here, :] + products(rows_of, sample, shift, here)
            turned[chunk, pl.ds(shift, 8, stride=OFFSET_ROWS), :] = total

        @pl.when(step >= 2)
        def _():
            for part in range(2 * chunk, 2 * chunk + 2):
                for half in range(2):
                    leave(step - 2, part, half).wait()

        for line in range(8):
            values = turned[chunk, line * OFFSET_ROWS : (line + 1) * OFFSET_ROWS, :].T
            at = 8 * chunk + line
            staged[step % 2, at] = values[: size_z // 2, :OFFSETS]
            staged[step % 2, lines + at] = values[size_z // 2 :, :OFFSETS]
            if line % 4 == 3:
                for half in range(2):
                    leave(step, at // 4, half).start()

    @pl.when(step == steps_in_all - 1)
    def _():
        for back in (1, 0):
            for part in range(2 * chunks):
                for half in range(2):
                    leave(step - back, part, half).wait()


def image(token, first, blocks):
    samples, _, lines, size_z = first.shape
    rows = 4 * samples
    return pl.pallas_call(
        image_kernel,
        grid=(samples,),
        out_shape=jax.ShapeDtypeStruct((samples, 2 * lines, size_z // 2, OFFSETS), F32),
        in_specs=[SMEM, pl.BlockSpec((1, OFFSETS, lines, size_z), lambda i: (i, 0, 0, 0))] + [ANY] * len(blocks),
        out_specs=HBM,
        scratch_shapes=[
            pltpu.VMEM((2, 2, rows + 2 * HALF, lines, size_z), F32),
            pltpu.VMEM((lines // 8, 8 * OFFSET_ROWS, size_z), F32),
            pltpu.VMEM((2, 2 * lines, size_z // 2, OFFSETS), F32),
            pltpu.SemaphoreType.DMA((18,)),
            pltpu.SemaphoreType.DMA((2, lines // 4, 2)),
        ],
        compiler_params=params(20),
        cost_estimate=cost(10**10, 16 * 2**20),
        name="image",
    )(token, first, *blocks)


def in_order_kernel(*refs):
    refs[-1][0] = 0


def in_order(*arrays):
    return pl.pallas_call(
        in_order_kernel,
        out_shape=jax.ShapeDtypeStruct((1,), jnp.int32),
        in_specs=[ANY] * len(arrays),
        out_specs=SMEM,
        compiler_params=params(1),
        cost_estimate=cost(1, 1),
        name="in_order",
    )(*arrays)


def on_device(source_now, source_before, receiver_now, receiver_before, courant):
    size = lax.axis_size("gx")
    up_pairs = [(i, i + 1) for i in range(size - 1)]
    down_pairs = [(j, i) for i, j in up_pairs]
    partner = [(i, i ^ 1) for i in range(size)]
    onward = [(i, i + 2) for i in range(0, size - 2, 2)] + [(i, i - 2) for i in range(3, size, 2)]
    both = [(0, 1), (1, 0)]

    def exchange(array, axis, pairs):
        return lax.ppermute(array, axis, pairs)

    barrier = lax.optimization_barrier
    up, down, edge, keep, keep_ends, give, give_ends, side = pack(source_now, receiver_now)
    near_edge = exchange(edge, "gx", partner)
    left = exchange(up, "gx", up_pairs)
    right = exchange(down, "gx", down_pairs)
    side = exchange(side, "gy", both)
    other = exchange(give, "shot", both)
    other_ends = exchange(give_ends, "shot", both)
    side, keep, other = barrier((side, keep, other))
    near_keep = exchange(keep, "gx", partner)
    near_other = exchange(other, "gx", partner)
    blocks = [keep, near_keep, None, other, near_other, None, keep_ends, other_ends]
    partial, kept_courant, edge_courant, edge, side = steps(
        source_now, receiver_now, source_before, receiver_before, courant, side
    )
    near_edge, side = barrier((near_edge, side))
    far_edge = exchange(near_edge, "gx", onward)
    ends, up, down, side, keep_edges, give_edges = mend(
        left, right, near_edge, far_edge, partial, kept_courant, edge_courant, edge, side
    )
    blocks += [keep_edges, exchange(give_edges, "shot", both)]
    left = exchange(up, "gx", up_pairs)
    right = exchange(down, "gx", down_pairs)
    side = exchange(side, "gy", both)
    side, near_keep, blocks[7], blocks[9] = barrier((side, near_keep, blocks[7], blocks[9]))
    far_keep = exchange(near_keep, "gx", onward)

    keep, give = finish_middle(partial, ends, kept_courant, side)
    other = exchange(give, "shot", both)
    near_keep = exchange(keep, "gx", partner)

    left, right, blocks[2], blocks[4] = barrier((left, right, far_keep, near_other))
    blocks[5] = exchange(blocks[4], "gx", onward)
    keep_ends, give_ends = finish_ends(ends, kept_courant, left, right, side)
    other, keep_ends, give_ends = barrier((other, keep_ends, give_ends))
    near_other = exchange(other, "gx", partner)
    other_ends = exchange(give_ends, "shot", both)
    other_ends, near_keep = barrier((other_ends, near_keep))
    own = jnp.stack([keep_ends, other_ends])
    far_keep = exchange(near_keep, "gx", onward)
    left = exchange(own, "gx", up_pairs)
    right = exchange(own, "gx", down_pairs)
    far_other = exchange(near_other, "gx", onward)
    blocks[5], far_keep = lax.optimization_barrier((blocks[5], far_keep))
    first = first_image(blocks)
    token = in_order(left, right, first)
    blocks = [keep, near_keep, far_keep, other, near_other, far_other, own, left, right]
    return jnp.transpose(image(token, first, blocks), (3, 0, 1, 2))


def solution(mesh):
    in_specs = (
        P("shot", "gx", "gy", None),
        P("shot", "gx", "gy", None),
        P("shot", "gx", "gy", None),
        P("shot", "gx", "gy", None),
        P("gx", "gy", None),
    )
    out_specs = P(None, "gx", "gy", "shot")
    return jax.shard_map(
        on_device, mesh=mesh, in_specs=in_specs, out_specs=out_specs, check_vma=False
    )
```
